512 devices in a mesh: tok: 64 (over y, x, core), hid: 8 (over z).
Axes of the slice: x: 4, y: 8, z: 8, core: 2. Of those that a mesh axis runs over, the one named last changes fastest.
Arguments:
- acts: bfloat16 [32768, 14336], P('tok', 'hid'), may hold values from -6 to 6
- dictionary: float32 [14336, 256], P('hid'), may hold values from -0.046875 to 0.046875
- codes: float32 [32768, 256], P('tok'), may hold values from 0.02 to 1, as said below
Outputs:
- codes_out: float32 [32768, 256], P('tok')
- dict_out: float32 [14336, 256], P('hid')
The draws below stay inside these ranges and needn't reach their ends.
Inputs may be any that keep to these rules, and one draw needn't show every extreme that they name: `codes`: every starting code is positive.
All inputs are finite; a program needn't handle non-finite values.
Results may differ from the reference program's by a relative error of at most 0.0043.
Values sent between devices are 32-bit elements; how exact they have to be, the bound alone decides.
A program may use at most 64 MiB of HBM per device.

```python
import math
import jax
import jax.numpy as jnp
from jax import lax

HID = 14336
COMP = 256
TOKENS = 32768


def draw_codes(key, part):
    key = jax.random.fold_in(key, 7)
    value_key = jax.random.fold_in(key, 1)
    row_key = jax.random.fold_in(key, 2)
    low_key = jax.random.fold_in(key, 3)
    spread_codes = jnp.exp(jax.random.uniform(value_key, (TOKENS, COMP), jnp.float32, math.log(0.02), 0.0))
    faint_codes = jnp.exp(jax.random.uniform(low_key, (TOKENS, COMP), jnp.float32, math.log(0.02), math.log(0.025)))
    picked = jax.random.randint(row_key, (TOKENS, 1), 0, 8) == 0
    return jnp.clip(jnp.where(picked, faint_codes, spread_codes), 0.02, 1.0)


def level_of(rng, dims, cuts, least, top_value):
    gain, own = 1.0, jax.random.fold_in(rng, 6)
    for dim, shards_of in cuts:
        draws = jnp.exp(jax.random.uniform(jax.random.fold_in(own, dim), (shards_of,), jnp.float32, least / len(cuts), top_value / len(cuts)))
        gain = gain * jnp.repeat(draws, dims[dim] // shards_of).reshape([-1 if axis == dim else 1 for axis in range(len(dims))])
    return gain


def noise(rng, extent, scale, limit, split=(), kind=jnp.bfloat16):
    gain = level_of(rng, extent, split, -0.22, 0.18) if split else 1.0
    values = jax.random.normal(rng, extent, jnp.float32) * scale * gain
    return jnp.minimum(jnp.maximum(values, -limit), limit).astype(kind)


def setup_inputs(seed: int = 0) -> dict:
    keys = jax.random.split(jax.random.key(seed), 4)
    return {
        "acts": noise(keys[0], (TOKENS, HID), 1.0, 6.0, ((0, 64), (1, 8))),
        "dictionary": noise(keys[1], (HID, COMP), HID ** -0.5, 0.046875, ((0, 8),), jnp.float32),
        "codes": draw_codes(jax.random.fold_in(keys[3], 71), 0),
    }


floor_value = 0.05

def refine(codes, proj, gram):
    gram_pos = jnp.maximum(gram, 0.0)
    gram_neg = jnp.maximum(-gram, 0.0)
    numer = jnp.maximum(proj, 0.0) + jnp.dot(codes, gram_neg, precision=lax.Precision.HIGHEST)
    denom = jnp.maximum(jnp.maximum(-proj, 0.0) + jnp.dot(codes, gram_pos, precision=lax.Precision.HIGHEST), floor_value)
    return codes * jnp.sqrt(numer / denom)

def solve_rows(cross, gram):
    lower = jnp.linalg.cholesky(gram)
    return jax.scipy.linalg.cho_solve((lower, True), cross.T).T

def reference(acts, dictionary, codes):
    dict_low = dictionary.astype(jnp.bfloat16)
    proj = jnp.dot(acts.astype(jnp.float32), dict_low.astype(jnp.float32), preferred_element_type=jnp.float32)
    gram_dict = jnp.dot(dictionary.T, dictionary, precision=lax.Precision.HIGHEST)
    codes_mid = refine(codes, proj, gram_dict)
    codes_low = codes_mid.astype(jnp.bfloat16)
    cross = jnp.dot(acts.T.astype(jnp.float32), codes_low.astype(jnp.float32), preferred_element_type=jnp.float32)
    gram_codes = jnp.dot(codes_low.T.astype(jnp.float32), codes_low.astype(jnp.float32), preferred_element_type=jnp.float32)
    dict_out = solve_rows(cross, gram_codes)
    gram_new = jnp.dot(dict_out.T, dict_out, precision=lax.Precision.HIGHEST)
    proj_two = jnp.dot(acts.astype(jnp.float32), dict_out.astype(jnp.bfloat16).astype(jnp.float32), preferred_element_type=jnp.float32)
    codes_out = refine(codes_mid, proj_two, gram_new)
    return (codes_out, dict_out)
```

```python
import functools

import jax
import jax.numpy as jnp
from jax import lax
from jax.experimental import pallas as pl
from jax.experimental.pallas import tpu as pltpu
from jax.sharding import PartitionSpec as P

MESH = pl.DeviceIdType.MESH
HIGHEST = lax.Precision.HIGHEST
floor_value = 0.05
XS, YS, ZS = 4, 8, 8
COMP = 256
BLOCK = 16
TN = (((0,), (0,)), ((), ()))
NT = (((1,), (1,)), ((), ()))


def split3(v):
    hi = v.astype(jnp.bfloat16)
    rest = v - hi.astype(jnp.float32)
    mid = rest.astype(jnp.bfloat16)
    low = (rest - mid.astype(jnp.float32)).astype(jnp.bfloat16)
    return hi, mid, low


def outer6(c, y):
    ch, cm, cl = split3(c)
    yh, ym, yl = split3(y)
    lhs = jnp.concatenate([ch, ch, cm, cm, ch, cl], axis=0)
    rhs = jnp.concatenate([yh, ym, yh, ym, yl, yh], axis=0)
    return lax.dot_general(lhs, rhs, TN, preferred_element_type=jnp.float32)


def panel_invert(panel, k):
    size = panel.shape[1]
    tile = jnp.where(k < 128 // BLOCK, panel[:, :128], panel[:, 128:])
    tile = pltpu.roll(tile, lax.rem(128 - lax.rem(k * BLOCK, 128), 128), 1)
    cols = [jnp.broadcast_to(tile[:, j : j + 1], (BLOCK, 128)) for j in range(BLOCK)]
    row = lax.broadcasted_iota(jnp.int32, (BLOCK, 128), 0)
    lane = lax.broadcasted_iota(jnp.int32, (BLOCK, size), 1) - k * BLOCK
    wide_row = lax.broadcasted_iota(jnp.int32, (BLOCK, size), 0)
    for i in range(BLOCK):
        inv = 1.0 / cols[i][i : i + 1, :]
        scaled = cols[i] * inv
        scaled2 = jnp.concatenate([scaled, scaled], axis=1)
        inv2 = jnp.concatenate([inv, inv], axis=1)
        pivot = panel[i : i + 1, :]
        new = jnp.where(wide_row == i, pivot * inv2, panel - scaled2 * pivot)
        panel = jnp.where(lane == i, jnp.where(wide_row == i, inv2, -scaled2), new)
        for j in range(i + 1, BLOCK):
            c = cols[j][i : i + 1, :]
            cols[j] = jnp.where(row == i, c * inv, cols[j] - scaled * c)
    return panel


def invert_blocks(a, first, last):
    size = a.shape[0]

    def body(k, _):
        rows = pl.ds(pl.multiple_of(k * BLOCK, BLOCK), BLOCK)
        panel = a[rows, :]
        lane = lax.broadcasted_iota(jnp.int32, (1, size), 1)
        column = panel * jnp.where(lane < k * BLOCK, -1.0, 1.0)
        new = panel_invert(panel, k)
        inside = (lane >= k * BLOCK) & (lane < k * BLOCK + BLOCK)
        a[...] = jnp.where(inside, 0.0, a[...]) - outer6(column, new)
        a[rows, :] = new
        return 0

    lax.fori_loop(first, last, body, 0)


def update(part, proj, gram, codes):
    both = jnp.concatenate([jnp.maximum(-gram, 0.0), jnp.maximum(gram, 0.0)], axis=0)
    prod = jnp.dot(both, codes, precision=HIGHEST, preferred_element_type=jnp.float32)
    n = gram.shape[0]
    numer = jnp.maximum(proj, 0.0) + prod[:n]
    denom = jnp.maximum(jnp.maximum(-proj, 0.0) + prod[n:], floor_value)
    return part * jnp.sqrt(numer / denom)


def kernel(
    acts, dic, codes, codes_out, dict_out,
    dt, ct, proj, gram, proj_in, gram_in, mid,
    gk, gk_c, gk_x, gk_y, ginv,
    cr, cr_c, cr_x, cr_y, cr_xs, full,
    proj2, gram2, proj2_in, gram2_in, out_t,
    zs, zr, ys, yr, xs, xr, cs, crs,
):
    tok, z = lax.axis_index("tok"), lax.axis_index("hid")
    core, x, y = lax.rem(tok, 2), lax.rem(tok // 2, XS), tok // (2 * XS)

    def at(dx=0, dy=0, dz=0, dc=0):
        px, py = lax.rem(x + dx, XS), lax.rem(y + dy, YS)
        return ((py * XS + px) * 2 + lax.rem(core + dc, 2), lax.rem(z + dz, ZS))

    zorder = (4, 3, 5, 2, 6, 1, 7)
    xorder = (2, 1, 3)

    barrier = pltpu.get_barrier_semaphore()
    partners = [at(dz=o) for o in zorder] + [at(dy=o) for o in zorder] + [at(dx=o) for o in xorder] + [at(dc=1)]
    for p in partners:
        pl.semaphore_signal(barrier, inc=1, device_id=p, device_id_type=MESH)

    def push(src, dst, ss, rs, dev):
        c = pltpu.make_async_remote_copy(
            src_ref=src, dst_ref=dst, send_sem=ss, recv_sem=rs, device_id=dev, device_id_type=MESH
        )
        c.start()
        return c

    def rows(i, n):
        return pl.ds(pl.multiple_of(i * n, n), n)

    n = COMP // ZS

    def scatter_z(part, slots, sem):
        out = []
        for o in zorder:
            dev = at(dz=o)
            out.append(push(part.at[rows(dev[1], n)], slots.at[o - 1], zs.at[sem, o - 1], zr.at[sem, o - 1], dev))
        return out

    def gather_z(buf, sem):
        own = buf.at[rows(z, n)]
        return [push(own, own, zs.at[sem, o - 1], zr.at[sem, o - 1], at(dz=o)) for o in zorder]

    def finish(copies):
        for c in copies:
            c.wait()

    dt[...] = dic[...].T
    proj[...] = lax.dot_general(dt[...].astype(jnp.bfloat16), acts[...], NT, preferred_element_type=jnp.float32)
    pl.semaphore_wait(barrier, len(partners))
    sent = scatter_z(proj, proj_in, 0)
    gram[...] = lax.dot_general(dt[...], dt[...], NT, precision=HIGHEST, preferred_element_type=jnp.float32)
    sent_gram = scatter_z(gram, gram_in, 1)
    ct[...] = codes[...].T
    own = rows(z, n)
    finish(sent)
    proj_sum = proj[own, :] + sum(proj_in[i] for i in range(ZS - 1))
    finish(sent_gram)
    gram_sum = gram[own, :] + sum(gram_in[i] for i in range(ZS - 1))
    mid[own, :] = update(ct[own, :], proj_sum, gram_sum, ct[...])
    finish(gather_z(mid, 2))

    low = mid[...].astype(jnp.bfloat16)
    gk[...] = lax.dot_general(low, low, NT, preferred_element_type=jnp.float32)
    half = COMP // 2
    g_core = push(gk.at[rows(1 - core, half)], gk_c, cs.at[0], crs.at[0], at(dc=1))
    tiles = acts.shape[1] // 128
    for j in range(0, tiles, 2):
        block = jnp.dot(low, acts[:, j * 128 : j * 128 + 256], preferred_element_type=jnp.float32)
        for i in (j, j + 1):
            cr[i // (tiles // 2), pl.ds((i % (tiles // 2)) * COMP, COMP), :] = block[:, (i - j) * 128 : (i - j + 1) * 128]
    c_core = push(cr.at[1 - core], cr_c, cs.at[1], crs.at[1], at(dc=1))
    g_core.wait()
    gk_c[...] += gk[rows(core, half), :]
    quarter = half // XS
    g_x = []
    for o in xorder:
        px = lax.rem(x + o, XS)
        g_x.append(push(gk_c.at[rows(px, quarter)], gk_x.at[o - 1], xs.at[0, o - 1], xr.at[0, o - 1], at(dx=o)))
    c_core.wait()
    cr_c[...] += cr[core]
    span = cr_c.shape[0] // XS
    c_x = []
    for o in xorder:
        px = lax.rem(x + o, XS)
        c_x.append(push(cr_c.at[rows(px, span)], cr_x.at[o - 1], xs.at[1, o - 1], xr.at[1, o - 1], at(dx=o)))
    finish(g_x)
    gk_y[y] = gk_c[rows(x, quarter), :] + gk_x[0] + gk_x[1] + gk_x[2]
    g_y = [push(gk_y.at[y], gk_y.at[y], ys.at[0, o - 1], yr.at[0, o - 1], at(dy=o)) for o in zorder]
    finish(g_y)
    place = core * XS + x
    ginv[rows(place, quarter), :] = sum(gk_y[i] for i in range(YS))
    spot = ginv.at[rows(place, quarter)]
    g_x2 = [push(spot, spot, xs.at[2, o - 1], xr.at[2, o - 1], at(dx=o)) for o in xorder]
    finish(c_x)
    cr_xs[...] = cr_c[rows(x, span), :] + cr_x[0] + cr_x[1] + cr_x[2]
    piece = span // YS
    c_y = []
    for o in zorder:
        py = lax.rem(y + o, YS)
        c_y.append(push(cr_xs.at[rows(py, piece)], cr_y.at[o - 1], ys.at[1, o - 1], yr.at[1, o - 1], at(dy=o)))
    finish(g_x2)
    spot = ginv.at[rows(core, half)]
    push(spot, spot, cs.at[2], crs.at[2], at(dc=1)).wait()

    steps = COMP // BLOCK
    invert_blocks(ginv, 0, steps // 2)
    finish(c_y)
    spot = full.at[core, rows(x * YS + y, piece)]
    spot[...] = cr_xs[rows(y, piece), :] + sum(cr_y[i] for i in range(YS - 1))
    c_y2 = [push(spot, spot, ys.at[2, o - 1], yr.at[2, o - 1], at(dy=o)) for o in zorder]
    invert_blocks(ginv, steps // 2, steps)
    finish(c_y2)
    spot = full.at[core, rows(x, span)]
    finish([push(spot, spot, xs.at[3, o - 1], xr.at[3, o - 1], at(dx=o)) for o in xorder])
    spot = full.at[core]
    push(spot, spot, cs.at[3], crs.at[3], at(dc=1)).wait()

    for j in range(0, tiles, 2):
        pair = [full[i // (tiles // 2), pl.ds((i % (tiles // 2)) * COMP, COMP), :] for i in (j, j + 1)]
        block = jnp.concatenate(pair, axis=1)
        dt[:, j * 128 : j * 128 + 256] = jnp.dot(
            ginv[...], block, precision=HIGHEST, preferred_element_type=jnp.float32
        )
    proj2[...] = lax.dot_general(dt[...].astype(jnp.bfloat16), acts[...], NT, preferred_element_type=jnp.float32)
    sent = scatter_z(proj2, proj2_in, 3)
    gram2[...] = lax.dot_general(dt[...], dt[...], NT, precision=HIGHEST, preferred_element_type=jnp.float32)
    sent_gram = scatter_z(gram2, gram2_in, 4)
    dict_out[...] = dt[...].T
    finish(sent)
    proj_sum = proj2[own, :] + sum(proj2_in[i] for i in range(ZS - 1))
    finish(sent_gram)
    gram_sum = gram2[own, :] + sum(gram2_in[i] for i in range(ZS - 1))
    out_t[own, :] = update(mid[own, :], proj_sum, gram_sum, mid[...])
    finish(gather_z(out_t, 5))
    codes_out[...] = out_t[...].T


def per_device(acts, dictionary, codes):
    tokens, hid = acts.shape
    f32 = jnp.float32
    v = lambda *s: pltpu.VMEM(s, f32)
    n = COMP // ZS
    half = hid * COMP // 2 // 128
    vmem = pl.BlockSpec(memory_space=pltpu.VMEM)
    dma = pltpu.SemaphoreType.DMA
    return pl.pallas_call(
        kernel,
        name="semi_nmf",
        out_shape=(jax.ShapeDtypeStruct((tokens, COMP), f32), jax.ShapeDtypeStruct((hid, COMP), f32)),
        in_specs=[vmem] * 3,
        out_specs=(vmem, vmem),
        scratch_shapes=[
            v(COMP, hid), v(COMP, tokens), v(COMP, tokens), v(COMP, COMP),
            v(ZS - 1, n, tokens), v(ZS - 1, n, COMP), v(COMP, tokens),
            v(COMP, COMP), v(COMP // 2, COMP), v(XS - 1, COMP // 2 // XS, COMP), v(YS, COMP // 2 // XS, COMP),
            v(COMP, COMP),
            v(2, half, 128), v(half, 128), v(XS - 1, half // XS, 128), v(YS - 1, half // XS // YS, 128),
            v(half // XS, 128), v(2, half, 128),
            v(COMP, tokens), v(COMP, COMP), v(ZS - 1, n, tokens), v(ZS - 1, n, COMP), v(COMP, tokens),
            dma((6, ZS - 1)), dma((6, ZS - 1)), dma((3, YS - 1)), dma((3, YS - 1)),
            dma((4, XS - 1)), dma((4, XS - 1)), dma((4,)), dma((4,)),
        ],
        compiler_params=pltpu.CompilerParams(
            collective_id=0, has_side_effects=True, vmem_limit_bytes=56 * 1024 * 1024
        ),
    )(acts, dictionary, codes)


def solution(mesh):
    return jax.shard_map(
        per_device,
        mesh=mesh,
        in_specs=(P("tok", "hid"), P("hid", None), P("tok", None)),
        out_specs=(P("tok", None), P("hid", None)),
        check_vma=False,
    )
```

```python
import functools

import jax
import jax.numpy as jnp
from jax import lax
from jax.experimental import pallas as pl
from jax.experimental.pallas import tpu as pltpu
from jax.sharding import PartitionSpec as P

MESH = pl.DeviceIdType.MESH
HIGHEST = lax.Precision.HIGHEST
floor_value = 0.05
XS, YS, ZS = 4, 8, 8
COMP = 256
BLOCK = 16
TN = (((0,), (0,)), ((), ()))
NT = (((1,), (1,)), ((), ()))


def split3(v):
    hi = v.astype(jnp.bfloat16)
    rest = v - hi.astype(jnp.float32)
    mid = rest.astype(jnp.bfloat16)
    low = (rest - mid.astype(jnp.float32)).astype(jnp.bfloat16)
    return hi, mid, low


def outer6(c, y):
    ch, cm, cl = split3(c)
    yh, ym, yl = split3(y)
    lhs = jnp.concatenate([ch, ch, cm, cm, ch, cl], axis=0)
    rhs = jnp.concatenate([yh, ym, yh, ym, yl, yh], axis=0)
    return lax.dot_general(lhs, rhs, TN, preferred_element_type=jnp.float32)


def panel_invert(panel, k):
    size = panel.shape[1]
    tile = jnp.where(k < 128 // BLOCK, panel[:, :128], panel[:, 128:])
    tile = pltpu.roll(tile, lax.rem(128 - lax.rem(k * BLOCK, 128), 128), 1)
    cols = [jnp.broadcast_to(tile[:, j : j + 1], (BLOCK, 128)) for j in range(BLOCK)]
    row = lax.broadcasted_iota(jnp.int32, (BLOCK, 128), 0)
    lane = lax.broadcasted_iota(jnp.int32, (BLOCK, size), 1) - k * BLOCK
    wide_row = lax.broadcasted_iota(jnp.int32, (BLOCK, size), 0)
    for i in range(BLOCK):
        inv = 1.0 / cols[i][i : i + 1, :]
        scaled = cols[i] * inv
        scaled2 = jnp.concatenate([scaled, scaled], axis=1)
        inv2 = jnp.concatenate([inv, inv], axis=1)
        pivot = panel[i : i + 1, :]
        new = jnp.where(wide_row == i, pivot * inv2, panel - scaled2 * pivot)
        panel = jnp.where(lane == i, jnp.where(wide_row == i, inv2, -scaled2), new)
        for j in range(i + 1, BLOCK):
            c = cols[j][i : i + 1, :]
            cols[j] = jnp.where(row == i, c * inv, cols[j] - scaled * c)
    return panel


def invert_blocks(a, first, last):
    size = a.shape[0]

    def body(k, _):
        rows = pl.ds(pl.multiple_of(k * BLOCK, BLOCK), BLOCK)
        panel = a[rows, :]
        lane = lax.broadcasted_iota(jnp.int32, (1, size), 1)
        column = panel * jnp.where(lane < k * BLOCK, -1.0, 1.0)
        new = panel_invert(panel, k)
        inside = (lane >= k * BLOCK) & (lane < k * BLOCK + BLOCK)
        a[...] = jnp.where(inside, 0.0, a[...]) - outer6(column, new)
        a[rows, :] = new
        return 0

    lax.fori_loop(first, last, body, 0)


def update(part, proj, gram, codes):
    both = jnp.concatenate([jnp.maximum(-gram, 0.0), jnp.maximum(gram, 0.0)], axis=0)
    prod = jnp.dot(both, codes, precision=HIGHEST, preferred_element_type=jnp.float32)
    n = gram.shape[0]
    numer = jnp.maximum(proj, 0.0) + prod[:n]
    denom = jnp.maximum(jnp.maximum(-proj, 0.0) + prod[n:], floor_value)
    return part * jnp.sqrt(numer / denom)


def kernel(
    acts, dic, codes, out_t, dict_out,
    dt, ct, proj, gram, proj_in, gram_in, gram_tiles, mid,
    gk, gk_c, gk_x, gk_y, ginv,
    cr, cr_c, cr_x, cr_y, cr_xs, full,
    proj2, gram2, proj2_in, gram2_in, gram2_tiles,
    zs, zr, ys, yr, xs, xr, cs, crs,
):
    tok, z = lax.axis_index("tok"), lax.axis_index("hid")
    core, x, y = lax.rem(tok, 2), lax.rem(tok // 2, XS), tok // (2 * XS)

    def at(dx=0, dy=0, dz=0, dc=0):
        px, py = lax.rem(x + dx, XS), lax.rem(y + dy, YS)
        return ((py * XS + px) * 2 + lax.rem(core + dc, 2), lax.rem(z + dz, ZS))

    zorder = (4, 3, 5, 2, 6, 1, 7)
    xorder = (2, 1, 3)

    barrier = pltpu.get_barrier_semaphore()
    partners = [at(dz=o) for o in zorder] + [at(dy=o) for o in zorder] + [at(dx=o) for o in xorder] + [at(dc=1)]
    for p in partners:
        pl.semaphore_signal(barrier, inc=1, device_id=p, device_id_type=MESH)

    def push(src, dst, ss, rs, dev):
        c = pltpu.make_async_remote_copy(
            src_ref=src, dst_ref=dst, send_sem=ss, recv_sem=rs, device_id=dev, device_id_type=MESH
        )
        c.start()
        return c

    def rows(i, n):
        return pl.ds(pl.multiple_of(i * n, n), n)

    n = COMP // ZS

    def scatter_z(part, slots, sem):
        out = []
        for o in zorder:
            dev = at(dz=o)
            out.append(push(part.at[rows(dev[1], n)], slots.at[o - 1], zs.at[sem, o - 1], zr.at[sem, o - 1], dev))
        return out

    def gather_z(buf, sem):
        own = buf.at[rows(z, n)]
        return [push(own, own, zs.at[sem, o - 1], zr.at[sem, o - 1], at(dz=o)) for o in zorder]

    def send_gram(matrix, part, slots, sem):
        picked = [matrix[pl.ds(pl.multiple_of(j * n + x * 8, 8), 8), :] for j in range(ZS)]
        part[...] = lax.dot_general(
            jnp.concatenate(picked, axis=0), matrix[rows(core, 128), :], NT,
            precision=HIGHEST, preferred_element_type=jnp.float32,
        ).reshape(part.shape)
        out = []
        for o in zorder:
            dev = at(dz=o)
            out.append(push(part.at[dev[1]], slots.at[o - 1], zs.at[sem, o - 1], zr.at[sem, o - 1], dev))
        return out

    def share_gram(sent, part, slots, tiles, step):
        finish(sent)
        spot = tiles.at[core, x]
        spot[...] = part[z] + sum(slots[i] for i in range(ZS - 1))
        finish([push(spot, spot, xs.at[step, o - 1], xr.at[step, o - 1], at(dx=o)) for o in xorder])
        spot = tiles.at[core]
        push(spot, spot, cs.at[step], crs.at[step], at(dc=1)).wait()
        return jnp.concatenate([tiles[i].reshape(n, 128) for i in range(2)], axis=1)

    def finish(copies):
        for c in copies:
            c.wait()

    dt[...] = dic[...].T
    proj[...] = lax.dot_general(dt[...].astype(jnp.bfloat16), acts[...], NT, preferred_element_type=jnp.float32)
    pl.semaphore_wait(barrier, len(partners))
    sent_gram = send_gram(dt, gram, gram_in, 1)
    sent = scatter_z(proj, proj_in, 0)
    ct[...] = codes[...].T
    own = rows(z, n)
    gram_sum = share_gram(sent_gram, gram, gram_in, gram_tiles, 4)
    finish(sent)
    proj_sum = proj[own, :] + sum(proj_in[i] for i in range(ZS - 1))
    mid[own, :] = update(ct[own, :], proj_sum, gram_sum, ct[...])
    finish(gather_z(mid, 2))

    low = mid[...].astype(jnp.bfloat16)
    gk[...] = lax.dot_general(low, low, NT, preferred_element_type=jnp.float32)
    half = COMP // 2
    g_core = push(gk.at[rows(1 - core, half)], gk_c, cs.at[0], crs.at[0], at(dc=1))
    tiles = acts.shape[1] // 128
    for j in range(0, tiles, 2):
        block = jnp.dot(low, acts[:, j * 128 : j * 128 + 256], preferred_element_type=jnp.float32)
        for i in (j, j + 1):
            cr[i // (tiles // 2), pl.ds((i % (tiles // 2)) * COMP, COMP), :] = block[:, (i - j) * 128 : (i - j + 1) * 128]
    c_core = push(cr.at[1 - core], cr_c, cs.at[1], crs.at[1], at(dc=1))
    g_core.wait()
    gk_c[...] += gk[rows(core, half), :]
    quarter = half // XS
    g_x = []
    for o in xorder:
        px = lax.rem(x + o, XS)
        g_x.append(push(gk_c.at[rows(px, quarter)], gk_x.at[o - 1], xs.at[0, o - 1], xr.at[0, o - 1], at(dx=o)))
    c_core.wait()
    cr_c[...] += cr[core]
    span = cr_c.shape[0] // XS
    c_x = []
    for o in xorder:
        px = lax.rem(x + o, XS)
        c_x.append(push(cr_c.at[rows(px, span)], cr_x.at[o - 1], xs.at[1, o - 1], xr.at[1, o - 1], at(dx=o)))
    finish(g_x)
    gk_y[y] = gk_c[rows(x, quarter), :] + gk_x[0] + gk_x[1] + gk_x[2]
    g_y = [push(gk_y.at[y], gk_y.at[y], ys.at[0, o - 1], yr.at[0, o - 1], at(dy=o)) for o in zorder]
    finish(g_y)
    place = core * XS + x
    ginv[rows(place, quarter), :] = sum(gk_y[i] for i in range(YS))
    spot = ginv.at[rows(place, quarter)]
    g_x2 = [push(spot, spot, xs.at[2, o - 1], xr.at[2, o - 1], at(dx=o)) for o in xorder]
    finish(c_x)
    cr_xs[...] = cr_c[rows(x, span), :] + cr_x[0] + cr_x[1] + cr_x[2]
    piece = span // YS
    c_y = []
    for o in zorder:
        py = lax.rem(y + o, YS)
        c_y.append(push(cr_xs.at[rows(py, piece)], cr_y.at[o - 1], ys.at[1, o - 1], yr.at[1, o - 1], at(dy=o)))
    finish(g_x2)
    spot = ginv.at[rows(core, half)]
    push(spot, spot, cs.at[2], crs.at[2], at(dc=1)).wait()

    steps = COMP // BLOCK
    invert_blocks(ginv, 0, steps // 2)
    finish(c_y)
    spot = full.at[core, rows(x * YS + y, piece)]
    spot[...] = cr_xs[rows(y, piece), :] + sum(cr_y[i] for i in range(YS - 1))
    c_y2 = [push(spot, spot, ys.at[2, o - 1], yr.at[2, o - 1], at(dy=o)) for o in zorder]
    invert_blocks(ginv, steps // 2, steps)
    finish(c_y2)
    spot = full.at[core, rows(x, span)]
    finish([push(spot, spot, xs.at[3, o - 1], xr.at[3, o - 1], at(dx=o)) for o in xorder])
    spot = full.at[core]
    push(spot, spot, cs.at[3], crs.at[3], at(dc=1)).wait()

    for j in range(0, tiles, 2):
        pair = [full[i // (tiles // 2), pl.ds((i % (tiles // 2)) * COMP, COMP), :] for i in (j, j + 1)]
        block = jnp.concatenate(pair, axis=1)
        dt[:, j * 128 : j * 128 + 256] = jnp.dot(
            ginv[...], block, precision=HIGHEST, preferred_element_type=jnp.float32
        )
    sent_gram = send_gram(dt, gram2, gram2_in, 4)
    proj2[...] = lax.dot_general(dt[...].astype(jnp.bfloat16), acts[...], NT, preferred_element_type=jnp.float32)
    sent = scatter_z(proj2, proj2_in, 3)
    dict_out[...] = dt[...].T
    gram_sum = share_gram(sent_gram, gram2, gram2_in, gram2_tiles, 5)
    finish(sent)
    proj_sum = proj2[own, :] + sum(proj2_in[i] for i in range(ZS - 1))
    out_t[own, :] = update(mid[own, :], proj_sum, gram_sum, mid[...])
    finish(gather_z(out_t, 5))


def leave(out_t, dict_in, codes_out, dict_out, sem):
    parts = 4
    step = dict_in.shape[0] // parts
    copies = []
    for i in range(parts):
        spot = pl.ds(i * step, step)
        copies.append(pltpu.make_async_copy(dict_in.at[spot], dict_out.at[spot], sem.at[i]))
    for c in copies:
        c.start()
    codes_out[...] = out_t[...].T
    for c in copies:
        c.wait()


def per_device(acts, dictionary, codes):
    tokens, hid = acts.shape
    f32 = jnp.float32
    v = lambda *s: pltpu.VMEM(s, f32)
    n = COMP // ZS
    half = hid * COMP // 2 // 128
    vmem = pl.BlockSpec(memory_space=pltpu.VMEM)
    dma = pltpu.SemaphoreType.DMA
    out_t, dict_new = pl.pallas_call(
        kernel,
        name="semi_nmf",
        out_shape=(jax.ShapeDtypeStruct((COMP, tokens), f32), jax.ShapeDtypeStruct((hid, COMP), f32)),
        in_specs=[vmem] * 3,
        out_specs=(vmem, vmem),
        scratch_shapes=[
            v(COMP, hid), v(COMP, tokens), v(COMP, tokens), v(ZS, 8, 128),
            v(ZS - 1, n, tokens), v(ZS - 1, 8, 128), v(2, XS, 8, 128), v(COMP, tokens),
            v(COMP, COMP), v(COMP // 2, COMP), v(XS - 1, COMP // 2 // XS, COMP), v(YS, COMP // 2 // XS, COMP),
            v(COMP, COMP),
            v(2, half, 128), v(half, 128), v(XS - 1, half // XS, 128), v(YS - 1, half // XS // YS, 128),
            v(half // XS, 128), v(2, half, 128),
            v(COMP, tokens), v(ZS, 8, 128), v(ZS - 1, n, tokens), v(ZS - 1, 8, 128), v(2, XS, 8, 128),
            dma((6, ZS - 1)), dma((6, ZS - 1)), dma((3, YS - 1)), dma((3, YS - 1)),
            dma((6, XS - 1)), dma((6, XS - 1)), dma((6,)), dma((6,)),
        ],
        compiler_params=pltpu.CompilerParams(
            collective_id=0, has_side_effects=True, vmem_limit_bytes=56 * 1024 * 1024
        ),
    )(acts, dictionary, codes)
    anywhere = pl.BlockSpec(memory_space=pl.ANY)
    return pl.pallas_call(
        leave,
        name="leave",
        out_shape=(jax.ShapeDtypeStruct((tokens, COMP), f32), jax.ShapeDtypeStruct((hid, COMP), f32)),
        in_specs=[vmem, anywhere],
        out_specs=(vmem, anywhere),
        scratch_shapes=[dma((4,))],
        compiler_params=pltpu.CompilerParams(vmem_limit_bytes=56 * 1024 * 1024),
    )(out_t, dict_new)


def solution(mesh):
    return jax.shard_map(
        per_device,
        mesh=mesh,
        in_specs=(P("tok", "hid"), P("hid", None), P("tok", None)),
        out_specs=(P("tok", None), P("hid", None)),
        check_vma=False,
    )
```

```python
import functools

import jax
import jax.numpy as jnp
from jax import lax
from jax.experimental import pallas as pl
from jax.experimental.pallas import tpu as pltpu
from jax.sharding import PartitionSpec as P

MESH = pl.DeviceIdType.MESH
HIGHEST = lax.Precision.HIGHEST
floor_value = 0.05
XS, YS, ZS = 4, 8, 8
COMP = 256
BLOCK = 16
TN = (((0,), (0,)), ((), ()))
NT = (((1,), (1,)), ((), ()))


def split3(v):
    hi = v.astype(jnp.bfloat16)
    rest = v - hi.astype(jnp.float32)
    mid = rest.astype(jnp.bfloat16)
    low = (rest - mid.astype(jnp.float32)).astype(jnp.bfloat16)
    return hi, mid, low


def outer6(c, y):
    ch, cm, cl = split3(c)
    yh, ym, yl = split3(y)
    lhs = jnp.concatenate([ch, ch, cm, cm, ch, cl], axis=0)
    rhs = jnp.concatenate([yh, ym, yh, ym, yl, yh], axis=0)
    return lax.dot_general(lhs, rhs, TN, preferred_element_type=jnp.float32)


def panel_invert(panel, k):
    size = panel.shape[1]
    tile = jnp.where(k < 128 // BLOCK, panel[:, :128], panel[:, 128:])
    tile = pltpu.roll(tile, lax.rem(128 - lax.rem(k * BLOCK, 128), 128), 1)
    cols = [jnp.broadcast_to(tile[:, j : j + 1], (BLOCK, 128)) for j in range(BLOCK)]
    row = lax.broadcasted_iota(jnp.int32, (BLOCK, 128), 0)
    lane = lax.broadcasted_iota(jnp.int32, (BLOCK, size), 1) - k * BLOCK
    wide_row = lax.broadcasted_iota(jnp.int32, (BLOCK, size), 0)
    for i in range(BLOCK):
        inv = 1.0 / cols[i][i : i + 1, :]
        scaled = cols[i] * inv
        scaled2 = jnp.concatenate([scaled, scaled], axis=1)
        inv2 = jnp.concatenate([inv, inv], axis=1)
        pivot = panel[i : i + 1, :]
        new = jnp.where(wide_row == i, pivot * inv2, panel - scaled2 * pivot)
        panel = jnp.where(lane == i, jnp.where(wide_row == i, inv2, -scaled2), new)
        for j in range(i + 1, BLOCK):
            c = cols[j][i : i + 1, :]
            cols[j] = jnp.where(row == i, c * inv, cols[j] - scaled * c)
    return panel


def invert_blocks(a, first, last):
    size = a.shape[0]

    def body(k, _):
        rows = pl.ds(pl.multiple_of(k * BLOCK, BLOCK), BLOCK)
        panel = a[rows, :]
        lane = lax.broadcasted_iota(jnp.int32, (1, size), 1)
        column = panel * jnp.where(lane < k * BLOCK, -1.0, 1.0)
        new = panel_invert(panel, k)
        inside = (lane >= k * BLOCK) & (lane < k * BLOCK + BLOCK)
        a[...] = jnp.where(inside, 0.0, a[...]) - outer6(column, new)
        a[rows, :] = new
        return 0

    lax.fori_loop(first, last, body, 0)


def update(part, proj, gram, codes):
    both = jnp.concatenate([jnp.maximum(-gram, 0.0), jnp.maximum(gram, 0.0)], axis=0)
    prod = jnp.dot(both, codes, precision=HIGHEST, preferred_element_type=jnp.float32)
    n = gram.shape[0]
    numer = jnp.maximum(proj, 0.0) + prod[:n]
    denom = jnp.maximum(jnp.maximum(-proj, 0.0) + prod[n:], floor_value)
    return part * jnp.sqrt(numer / denom)


def kernel(
    acts, dic, codes, out_t, dict_out,
    dt, ct, proj, gram, proj_in, gram_in, gram_tiles, mid,
    gk, gk_c, gk_x, gk_y, gk_z, ginv,
    cr, cr_c, cr_x0, cr_s0, cr_y0, cr_y1, cr_s1, cr_x1, full,
    proj2, gram2, proj2_in, gram2_in, gram2_tiles,
    zs, zr, ys, yr, xs, xr, cs, crs,
):
    tok, z = lax.axis_index("tok"), lax.axis_index("hid")
    core, x, y = lax.rem(tok, 2), lax.rem(tok // 2, XS), tok // (2 * XS)

    def at(dx=0, dy=0, dz=0, dc=0):
        px, py = lax.rem(x + dx, XS), lax.rem(y + dy, YS)
        return ((py * XS + px) * 2 + lax.rem(core + dc, 2), lax.rem(z + dz, ZS))

    zorder = (4, 3, 5, 2, 6, 1, 7)
    xorder = (2, 1, 3)

    barrier = pltpu.get_barrier_semaphore()
    partners = [at(dz=o) for o in zorder] + [at(dy=o) for o in zorder] + [at(dx=o) for o in xorder] + [at(dc=1)]
    for p in partners:
        pl.semaphore_signal(barrier, inc=1, device_id=p, device_id_type=MESH)

    def push(src, dst, ss, rs, dev):
        c = pltpu.make_async_remote_copy(
            src_ref=src, dst_ref=dst, send_sem=ss, recv_sem=rs, device_id=dev, device_id_type=MESH
        )
        c.start()
        return c

    def rows(i, n):
        return pl.ds(pl.multiple_of(i * n, n), n)

    n = COMP // ZS

    def scatter_z(part, slots, sem):
        out = []
        for o in zorder:
            dev = at(dz=o)
            out.append(push(part.at[rows(dev[1], n)], slots.at[o - 1], zs.at[sem, o - 1], zr.at[sem, o - 1], dev))
        return out

    def gather_z(buf, sem):
        own = buf.at[rows(z, n)]
        return [push(own, own, zs.at[sem, o - 1], zr.at[sem, o - 1], at(dz=o)) for o in zorder]

    def send_gram(matrix, part, slots, sem):
        picked = [matrix[pl.ds(pl.multiple_of(j * n + x * 8, 8), 8), :] for j in range(ZS)]
        part[...] = lax.dot_general(
            jnp.concatenate(picked, axis=0), matrix[rows(core, 128), :], NT,
            precision=HIGHEST, preferred_element_type=jnp.float32,
        ).reshape(part.shape)
        out = []
        for o in zorder:
            dev = at(dz=o)
            out.append(push(part.at[dev[1]], slots.at[o - 1], zs.at[sem, o - 1], zr.at[sem, o - 1], dev))
        return out

    def share_gram(sent, part, slots, tiles, step):
        finish(sent)
        spot = tiles.at[core, x]
        spot[...] = part[z] + sum(slots[i] for i in range(ZS - 1))
        finish([push(spot, spot, xs.at[step, o - 1], xr.at[step, o - 1], at(dx=o)) for o in xorder])
        spot = tiles.at[core]
        push(spot, spot, cs.at[step], crs.at[step], at(dc=1)).wait()
        return jnp.concatenate([tiles[i].reshape(n, 128) for i in range(2)], axis=1)

    def finish(copies):
        for c in copies:
            c.wait()

    dt[...] = dic[...].T
    proj[...] = lax.dot_general(dt[...].astype(jnp.bfloat16), acts[...], NT, preferred_element_type=jnp.float32)
    pl.semaphore_wait(barrier, len(partners))
    sent_gram = send_gram(dt, gram, gram_in, 1)
    sent = scatter_z(proj, proj_in, 0)
    ct[...] = codes[...].T
    own = rows(z, n)
    gram_sum = share_gram(sent_gram, gram, gram_in, gram_tiles, 4)
    finish(sent)
    proj_sum = proj[own, :] + sum(proj_in[i] for i in range(ZS - 1))
    mid[own, :] = update(ct[own, :], proj_sum, gram_sum, ct[...])
    finish(gather_z(mid, 2))

    low = mid[...].astype(jnp.bfloat16)
    low_own = mid[own, :].astype(jnp.bfloat16)
    gk[...] = lax.dot_general(low_own, low, NT, preferred_element_type=jnp.float32).reshape(gk.shape)
    g_c = push(gk.at[1 - core], gk_c, cs.at[0], crs.at[0], at(dc=1))

    halftiles = acts.shape[1] // 256
    part0 = halftiles - halftiles // 3
    cut = part0 * COMP
    rest = halftiles * COMP - cut

    def cross(which, first, last):
        for j in range(first, last):
            lanes = pl.ds(pl.multiple_of((which * halftiles + j) * 128, 128), 128)
            cr[which, pl.ds(j * COMP, COMP), :] = jnp.dot(low, acts[:, lanes], preferred_element_type=jnp.float32)

    head, tail = pl.ds(0, cut), pl.ds(cut, rest)
    cross(1 - core, 0, part0)
    c_c0 = push(cr.at[1 - core, head], cr_c.at[head], cs.at[1], crs.at[1], at(dc=1))
    cross(1 - core, part0, halftiles)
    c_c1 = push(cr.at[1 - core, tail], cr_c.at[tail], cs.at[2], crs.at[2], at(dc=1))
    g_c.wait()
    gk_x[x] = gk[core] + gk_c[...]
    g_x = [push(gk_x.at[x], gk_x.at[x], xs.at[0, o - 1], xr.at[0, o - 1], at(dx=o)) for o in xorder]
    cross(core, 0, halftiles)
    c_c0.wait()
    cr_c[head, :] += cr[core, head, :]
    xspan, xpiece = cut // XS, cut // XS // YS
    yspan, ypiece = rest // YS, rest // YS // XS

    def tail_rows(i, size):
        return pl.ds(pl.multiple_of(cut + i * size, size), size)

    c0 = []
    for o in xorder:
        px = lax.rem(x + o, XS)
        c0.append(push(cr_c.at[rows(px, xspan)], cr_x0.at[o - 1], xs.at[1, o - 1], xr.at[1, o - 1], at(dx=o)))
    finish(g_x)
    gk_y[y] = sum(gk_x[i] for i in range(XS))
    g_y = [push(gk_y.at[y], gk_y.at[y], ys.at[0, o - 1], yr.at[0, o - 1], at(dy=o)) for o in zorder]
    c_c1.wait()
    cr_c[tail, :] += cr[core, tail, :]
    c1 = []
    for o in zorder:
        py = lax.rem(y + o, YS)
        c1.append(push(cr_c.at[tail_rows(py, yspan)], cr_y1.at[o - 1], ys.at[1, o - 1], yr.at[1, o - 1], at(dy=o)))
    finish(g_y)
    spot = gk_z.at[z, core]
    spot[...] = sum(gk_y[i] for i in range(YS))
    g_z = [push(spot, spot, zs.at[6, o - 1], zr.at[6, o - 1], at(dz=o)) for o in zorder]
    finish(c0)
    cr_s0[...] = cr_c[rows(x, xspan), :] + cr_x0[0] + cr_x0[1] + cr_x0[2]
    c0 = []
    for o in zorder:
        py = lax.rem(y + o, YS)
        c0.append(push(cr_s0.at[rows(py, xpiece)], cr_y0.at[o - 1], ys.at[2, o - 1], yr.at[2, o - 1], at(dy=o)))
    finish(c1)
    cr_s1[...] = cr_c[tail_rows(y, yspan), :] + sum(cr_y1[i] for i in range(YS - 1))
    c1 = []
    for o in xorder:
        px = lax.rem(x + o, XS)
        c1.append(push(cr_s1.at[rows(px, ypiece)], cr_x1.at[o - 1], xs.at[2, o - 1], xr.at[2, o - 1], at(dx=o)))
    finish(c1)
    spot = full.at[core, tail_rows(y * XS + x, ypiece)]
    spot[...] = cr_s1[rows(x, ypiece), :] + cr_x1[0] + cr_x1[1] + cr_x1[2]
    c1 = [push(spot, spot, xs.at[3, o - 1], xr.at[3, o - 1], at(dx=o)) for o in xorder]
    finish(g_z)
    spot = gk_z.at[:, core]
    g_c = push(spot, spot, cs.at[3], crs.at[3], at(dc=1))
    finish(c0)
    spot = full.at[core, rows(x * YS + y, xpiece)]
    spot[...] = cr_s0[rows(y, xpiece), :] + sum(cr_y0[i] for i in range(YS - 1))
    c0 = [push(spot, spot, ys.at[3, o - 1], yr.at[3, o - 1], at(dy=o)) for o in zorder]
    finish(c1)
    spot = full.at[core, tail_rows(y, yspan)]
    c1 = [push(spot, spot, ys.at[4, o - 1], yr.at[4, o - 1], at(dy=o)) for o in zorder]
    g_c.wait()
    ginv[...] = gk_z[...].reshape(COMP, COMP)

    steps = COMP // BLOCK
    invert_blocks(ginv, 0, steps // 2)
    finish(c0)
    spot = full.at[core, rows(x, xspan)]
    c0 = [push(spot, spot, xs.at[6, o - 1], xr.at[6, o - 1], at(dx=o)) for o in xorder]
    finish(c1)
    spot = full.at[core, tail]
    c1 = push(spot, spot, cs.at[6], crs.at[6], at(dc=1))
    invert_blocks(ginv, steps // 2, steps)
    finish(c0)
    spot = full.at[core, head]
    c0 = push(spot, spot, cs.at[7], crs.at[7], at(dc=1))

    def solve(first, last):
        for j in range(first, last):
            span = pl.ds(j * COMP, COMP)
            block = jnp.concatenate([full[0, span, :], full[1, span, :]], axis=1)
            solved = jnp.dot(ginv[...], block, precision=HIGHEST, preferred_element_type=jnp.float32)
            for i in range(2):
                dt[:, (i * halftiles + j) * 128 : (i * halftiles + j + 1) * 128] = solved[:, i * 128 : i * 128 + 128]

    c1.wait()
    solve(part0, halftiles)
    c0.wait()
    solve(0, part0)
    sent_gram = send_gram(dt, gram2, gram2_in, 4)
    proj2[...] = lax.dot_general(dt[...].astype(jnp.bfloat16), acts[...], NT, preferred_element_type=jnp.float32)
    sent = scatter_z(proj2, proj2_in, 3)
    dict_out[...] = dt[...].T
    gram_sum = share_gram(sent_gram, gram2, gram2_in, gram2_tiles, 5)
    finish(sent)
    proj_sum = proj2[own, :] + sum(proj2_in[i] for i in range(ZS - 1))
    out_t[own, :] = update(mid[own, :], proj_sum, gram_sum, mid[...])
    finish(gather_z(out_t, 5))


def leave(out_t, dict_in, codes_out, dict_out, held_t, held_codes, held_dict, ins, outs):
    parts = 4
    step = dict_in.shape[0] // parts
    spots = [pl.ds(i * step, step) for i in range(parts)]
    first = pltpu.make_async_copy(out_t, held_t, ins.at[parts])
    first.start()
    arriving = [pltpu.make_async_copy(dict_in.at[p], held_dict.at[p], ins.at[i]) for i, p in enumerate(spots)]
    for c in arriving:
        c.start()
    leaving = []
    for i, p in enumerate(spots):
        arriving[i].wait()
        leaving.append(pltpu.make_async_copy(held_dict.at[p], dict_out.at[p], outs.at[i]))
        leaving[-1].start()
    first.wait()
    held_codes[...] = held_t[...].T
    leaving.append(pltpu.make_async_copy(held_codes, codes_out, outs.at[parts]))
    leaving[-1].start()
    for c in leaving:
        c.wait()


def per_device(acts, dictionary, codes):
    tokens, hid = acts.shape
    f32 = jnp.float32
    v = lambda *s: pltpu.VMEM(s, f32)
    n = COMP // ZS
    half = hid * COMP // 2 // 128
    cut = (hid // 256 - hid // 256 // 3) * COMP
    rest = half - cut
    vmem = pl.BlockSpec(memory_space=pltpu.VMEM)
    dma = pltpu.SemaphoreType.DMA
    out_t, dict_new = pl.pallas_call(
        kernel,
        name="semi_nmf",
        out_shape=(jax.ShapeDtypeStruct((COMP, tokens), f32), jax.ShapeDtypeStruct((hid, COMP), f32)),
        in_specs=[vmem] * 3,
        out_specs=(vmem, vmem),
        scratch_shapes=[
            v(COMP, hid), v(COMP, tokens), v(COMP, tokens), v(ZS, 8, 128),
            v(ZS - 1, n, tokens), v(ZS - 1, 8, 128), v(2, XS, 8, 128), v(COMP, tokens),
            v(2, n // 2, COMP), v(n // 2, COMP), v(XS, n // 2, COMP), v(YS, n // 2, COMP), v(ZS, 2, n // 2, COMP),
            v(COMP, COMP),
            v(2, half, 128), v(half, 128), v(XS - 1, cut // XS, 128), v(cut // XS, 128), v(YS - 1, cut // XS // YS, 128),
            v(YS - 1, rest // YS, 128), v(rest // YS, 128), v(XS - 1, rest // YS // XS, 128), v(2, half, 128),
            v(COMP, tokens), v(ZS, 8, 128), v(ZS - 1, n, tokens), v(ZS - 1, 8, 128), v(2, XS, 8, 128),
            dma((7, ZS - 1)), dma((7, ZS - 1)), dma((5, YS - 1)), dma((5, YS - 1)),
            dma((7, XS - 1)), dma((7, XS - 1)), dma((8,)), dma((8,)),
        ],
        compiler_params=pltpu.CompilerParams(
            collective_id=0, has_side_effects=True, vmem_limit_bytes=56 * 1024 * 1024
        ),
    )(acts, dictionary, codes)
    anywhere = pl.BlockSpec(memory_space=pl.ANY)
    return pl.pallas_call(
        leave,
        name="leave",
        out_shape=(jax.ShapeDtypeStruct((tokens, COMP), f32), jax.ShapeDtypeStruct((hid, COMP), f32)),
        in_specs=[anywhere] * 2,
        out_specs=(anywhere, anywhere),
        scratch_shapes=[v(COMP, tokens), v(tokens, COMP), v(hid, COMP), dma((5,)), dma((5,))],
        compiler_params=pltpu.CompilerParams(vmem_limit_bytes=56 * 1024 * 1024),
    )(out_t, dict_new)


def solution(mesh):
    return jax.shard_map(
        per_device,
        mesh=mesh,
        in_specs=(P("tok", "hid"), P("hid", None), P("tok", None)),
        out_specs=(P("tok", None), P("hid", None)),
        check_vma=False,
    )
```

```python
import functools

import jax
import jax.numpy as jnp
from jax import lax
from jax.experimental import pallas as pl
from jax.experimental.pallas import tpu as pltpu
from jax.sharding import PartitionSpec as P

MESH = pl.DeviceIdType.MESH
HIGHEST = lax.Precision.HIGHEST
floor_value = 0.05
XS, YS, ZS = 4, 8, 8
COMP = 256
BLOCK = 16
TN = (((0,), (0,)), ((), ()))
NT = (((1,), (1,)), ((), ()))


def split3(v):
    hi = v.astype(jnp.bfloat16)
    rest = v - hi.astype(jnp.float32)
    mid = rest.astype(jnp.bfloat16)
    low = (rest - mid.astype(jnp.float32)).astype(jnp.bfloat16)
    return hi, mid, low


def outer6(c, y):
    ch, cm, cl = split3(c)
    yh, ym, yl = split3(y)
    lhs = jnp.concatenate([ch, ch, cm, cm, ch, cl], axis=0)
    rhs = jnp.concatenate([yh, ym, yh, ym, yl, yh], axis=0)
    return lax.dot_general(lhs, rhs, TN, preferred_element_type=jnp.float32)


def panel_invert(panel, k):
    size = panel.shape[1]
    tile = jnp.where(k < 128 // BLOCK, panel[:, :128], panel[:, 128:])
    tile = pltpu.roll(tile, lax.rem(128 - lax.rem(k * BLOCK, 128), 128), 1)
    cols = [jnp.broadcast_to(tile[:, j : j + 1], (BLOCK, 128)) for j in range(BLOCK)]
    row = lax.broadcasted_iota(jnp.int32, (BLOCK, 128), 0)
    lane = lax.broadcasted_iota(jnp.int32, (BLOCK, size), 1) - k * BLOCK
    wide_row = lax.broadcasted_iota(jnp.int32, (BLOCK, size), 0)
    for i in range(BLOCK):
        inv = 1.0 / cols[i][i : i + 1, :]
        scaled = cols[i] * inv
        scaled2 = jnp.concatenate([scaled, scaled], axis=1)
        inv2 = jnp.concatenate([inv, inv], axis=1)
        pivot = panel[i : i + 1, :]
        new = jnp.where(wide_row == i, pivot * inv2, panel - scaled2 * pivot)
        panel = jnp.where(lane == i, jnp.where(wide_row == i, inv2, -scaled2), new)
        for j in range(i + 1, BLOCK):
            c = cols[j][i : i + 1, :]
            cols[j] = jnp.where(row == i, c * inv, cols[j] - scaled * c)
    return panel


def invert_blocks(a, first, last):
    size = a.shape[0]

    def body(k, _):
        rows = pl.ds(pl.multiple_of(k * BLOCK, BLOCK), BLOCK)
        panel = a[rows, :]
        lane = lax.broadcasted_iota(jnp.int32, (1, size), 1)
        column = panel * jnp.where(lane < k * BLOCK, -1.0, 1.0)
        new = panel_invert(panel, k)
        inside = (lane >= k * BLOCK) & (lane < k * BLOCK + BLOCK)
        a[...] = jnp.where(inside, 0.0, a[...]) - outer6(column, new)
        a[rows, :] = new
        return 0

    lax.fori_loop(first, last, body, 0)


def gram_products(gram, codes):
    both = jnp.concatenate([jnp.maximum(-gram, 0.0), jnp.maximum(gram, 0.0)], axis=0)
    return jnp.dot(both, codes, precision=HIGHEST, preferred_element_type=jnp.float32)


def update(part, proj, prod, p):
    n = prod.shape[0] // 2
    numer = jnp.maximum(proj, 0.0) + prod[p * 8 : p * 8 + 8]
    denom = jnp.maximum(jnp.maximum(-proj, 0.0) + prod[n + p * 8 : n + p * 8 + 8], floor_value)
    return part * jnp.sqrt(numer / denom)


def kernel(
    acts, dic, codes, out_t, dict_out,
    dt, ct, proj, gram, gram_in, gram_tiles, mid,
    gk, gk_c, gk_x, gk_y, gk_z, ginv,
    cr, cr_c, cr_x0, cr_s0, cr_y0, cr_y1, cr_s1, cr_x1, full,
    proj2, gram2, gram2_in, gram2_tiles,
    a1, a2, a3, a4, a5, b1, b2, b3, b4, b5,
    zs, zr, ds, dr, ys, yr, xs, xr, cs, crs,
):
    tok, z = lax.axis_index("tok"), lax.axis_index("hid")
    core, x, y = lax.rem(tok, 2), lax.rem(tok // 2, XS), tok // (2 * XS)

    def at(dx=0, dy=0, dz=0, dc=0):
        px, py = lax.rem(x + dx, XS), lax.rem(y + dy, YS)
        return ((py * XS + px) * 2 + lax.rem(core + dc, 2), lax.rem(z + dz, ZS))

    zorder = (4, 3, 5, 2, 6, 1, 7)
    xorder = (2, 1, 3)

    bufs, bufs2 = (a1, a2, a3, a4, a5), (b1, b2, b3, b4, b5)

    barrier = pltpu.get_barrier_semaphore()
    partners = [at(dz=o) for o in zorder] + [at(dy=o) for o in zorder] + [at(dx=o) for o in xorder] + [at(dc=1)]
    for p in partners:
        pl.semaphore_signal(barrier, inc=1, device_id=p, device_id_type=MESH)

    def push(src, dst, ss, rs, dev):
        c = pltpu.make_async_remote_copy(
            src_ref=src, dst_ref=dst, send_sem=ss, recv_sem=rs, device_id=dev, device_id_type=MESH
        )
        c.start()
        return c

    def rows(i, n):
        return pl.ds(pl.multiple_of(i * n, n), n)

    n = COMP // ZS

    pieces = n // 8
    ways = (1, -1)

    def chunk(owner, p, size=1):
        return pl.ds(pl.multiple_of(owner * n + p * 8, 8), size * 8)

    def scatter_z(part, bufs, phase):
        via1, via2, relay, fin1, fin2 = bufs
        held = {}
        for i, d in enumerate(ways):
            for p in range(pieces // 2):
                src = part.at[chunk(lax.rem(z + 4, ZS), p + i * (pieces // 2))]
                ss, rs = zs.at[phase, i, p], zr.at[phase, i, p]
                held["via2", i, p + i * (pieces // 2)] = push(src, via2.at[i, pl.ds(p * 8, 8)], ss, rs, at(dz=2 * d + ZS))
        for p in range(pieces):
            for i, d in enumerate(ways):
                src = part.at[chunk(lax.rem(z + 3 * d + ZS, ZS), p)]
                ss, rs = zs.at[phase, i, 2 + p], zr.at[phase, i, 2 + p]
                held["via1", i, p] = push(src, via1.at[i, pl.ds(p * 8, 8)], ss, rs, at(dz=d + ZS))
        for i, d in enumerate(ways):
            src = part.at[chunk(lax.rem(z + d + ZS, ZS), 0, pieces)]
            held["fin1", i] = push(src, fin1.at[i], zs.at[phase, i, 6], zr.at[phase, i, 6], at(dz=d + ZS))
        return held

    def relay_z(part, bufs, phase, held):
        via1, via2, relay, fin1, fin2 = bufs
        for p in range(pieces):
            for i, d in enumerate(ways):
                span = pl.ds(p * 8, 8)
                held["via1", i, p].wait_recv()
                total = part[chunk(lax.rem(z + 2 * d + ZS, ZS), p), :] + via1[i, span, :]
                if p // (pieces // 2) == i:
                    held["via2", i, p].wait_recv()
                    total += via2[i, pl.ds((p - i * (pieces // 2)) * 8, 8), :]
                relay[i, span, :] = total
                ss, rs = zs.at[phase, i, 7 + p], zr.at[phase, i, 7 + p]
                held["fin2", i, p] = push(relay.at[i, span], fin2.at[i, span], ss, rs, at(dz=2 * d + ZS))

    def summed_z(part, bufs, held, p):
        via1, via2, relay, fin1, fin2 = bufs
        span = pl.ds(p * 8, 8)
        total = part[chunk(z, p), :]
        for i in range(2):
            if p == 0:
                held["fin1", i].wait_recv()
            total += fin1[i, span, :]
        for i in range(2):
            held["fin2", i, p].wait_recv()
            total += fin2[i, span, :]
        return total

    def gather_z(buf, phase, held, p):
        spot = buf.at[chunk(z, p)]
        for j, hops in ((0, 2), (4, 1)):
            for i, d in enumerate(ways):
                dev = at(dz=hops * d + ZS)
                held[hops, i, p] = push(spot, spot, zs.at[phase, i, j + p], zr.at[phase, i, j + p], dev)

    def forward_z(buf, phase, held):
        for p in range(pieces):
            for i, d in enumerate(ways):
                held[2, i, p].wait_recv()
                spot = buf.at[chunk(lax.rem(z - 2 * d + ZS, ZS), p)]
                if p // (pieces // 2) == i:
                    q = 8 + p - i * (pieces // 2)
                    held[4, i, p] = push(spot, spot, zs.at[phase, i, q], zr.at[phase, i, q], at(dz=2 * d + ZS))
                held[3, i, p] = push(spot, spot, zs.at[phase, i, 10 + p], zr.at[phase, i, 10 + p], at(dz=d + ZS))
        for key, c in held.items():
            c.wait_send()
            if key[0] != 2:
                c.wait_recv()

    def send_gram(matrix, part, slots, sem):
        picked = [matrix[pl.ds(pl.multiple_of(j * n + x * 8, 8), 8), :] for j in range(ZS)]
        part[...] = lax.dot_general(
            jnp.concatenate(picked, axis=0), matrix[rows(core, 128), :], NT,
            precision=HIGHEST, preferred_element_type=jnp.float32,
        ).reshape(part.shape)
        out = []
        for o in zorder:
            dev = at(dz=o)
            out.append(push(part.at[dev[1]], slots.at[o - 1], ds.at[sem, o - 1], dr.at[sem, o - 1], dev))
        return out

    def share_gram(sent, part, slots, tiles, step):
        finish(sent)
        spot = tiles.at[core, x]
        spot[...] = part[z] + sum(slots[i] for i in range(ZS - 1))
        return [push(spot, spot, xs.at[step, o - 1], xr.at[step, o - 1], at(dx=o)) for o in xorder]

    def whole_gram(sent, tiles, step):
        finish(sent)
        spot = tiles.at[core]
        push(spot, spot, cs.at[step], crs.at[step], at(dc=1)).wait()
        return jnp.concatenate([tiles[i].reshape(n, 128) for i in range(2)], axis=1)

    def finish(copies):
        for c in copies:
            c.wait()

    dt[...] = dic[...].T
    proj[...] = lax.dot_general(dt[...].astype(jnp.bfloat16), acts[...], NT, preferred_element_type=jnp.float32)
    pl.semaphore_wait(barrier, len(partners))
    sent_gram = send_gram(dt, gram, gram_in, 0)
    held = scatter_z(proj, bufs, 0)
    ct[...] = codes[...].T
    own = rows(z, n)
    sent_gram = share_gram(sent_gram, gram, gram_in, gram_tiles, 4)
    relay_z(proj, bufs, 0, held)
    prod = gram_products(whole_gram(sent_gram, gram_tiles, 4), ct[...])
    passed = {}
    for p in range(pieces):
        mid[chunk(z, p), :] = update(ct[chunk(z, p), :], summed_z(proj, bufs, held, p), prod, p)
        gather_z(mid, 1, passed, p)
    for c in held.values():
        c.wait_send()
    forward_z(mid, 1, passed)

    low = mid[...].astype(jnp.bfloat16)
    low_own = mid[own, :].astype(jnp.bfloat16)
    gk[...] = lax.dot_general(low_own, low, NT, preferred_element_type=jnp.float32).reshape(gk.shape)
    g_c = push(gk.at[1 - core], gk_c, cs.at[0], crs.at[0], at(dc=1))

    halftiles = acts.shape[1] // 256
    part0 = halftiles - halftiles // 3
    cut = part0 * COMP
    rest = halftiles * COMP - cut

    def cross(which, first, last):
        for j in range(first, last):
            lanes = pl.ds(pl.multiple_of((which * halftiles + j) * 128, 128), 128)
            cr[which, pl.ds(j * COMP, COMP), :] = jnp.dot(low, acts[:, lanes], preferred_element_type=jnp.float32)

    head, tail = pl.ds(0, cut), pl.ds(cut, rest)
    cross(1 - core, 0, part0)
    c_c0 = push(cr.at[1 - core, head], cr_c.at[head], cs.at[1], crs.at[1], at(dc=1))
    cross(1 - core, part0, halftiles)
    c_c1 = push(cr.at[1 - core, tail], cr_c.at[tail], cs.at[2], crs.at[2], at(dc=1))
    g_c.wait()
    gk_x[x] = gk[core] + gk_c[...]
    g_x = [push(gk_x.at[x], gk_x.at[x], xs.at[0, o - 1], xr.at[0, o - 1], at(dx=o)) for o in xorder]
    cross(core, 0, halftiles)
    c_c0.wait()
    cr_c[head, :] += cr[core, head, :]
    xspan, xpiece = cut // XS, cut // XS // YS
    yspan, ypiece = rest // YS, rest // YS // XS

    def tail_rows(i, size):
        return pl.ds(pl.multiple_of(cut + i * size, size), size)

    c0 = []
    for o in xorder:
        px = lax.rem(x + o, XS)
        c0.append(push(cr_c.at[rows(px, xspan)], cr_x0.at[o - 1], xs.at[1, o - 1], xr.at[1, o - 1], at(dx=o)))
    finish(g_x)
    gk_y[y] = sum(gk_x[i] for i in range(XS))
    g_y = [push(gk_y.at[y], gk_y.at[y], ys.at[0, o - 1], yr.at[0, o - 1], at(dy=o)) for o in zorder]
    c_c1.wait()
    cr_c[tail, :] += cr[core, tail, :]
    c1 = []
    for o in zorder:
        py = lax.rem(y + o, YS)
        c1.append(push(cr_c.at[tail_rows(py, yspan)], cr_y1.at[o - 1], ys.at[1, o - 1], yr.at[1, o - 1], at(dy=o)))
    finish(g_y)
    spot = gk_z.at[z, core]
    spot[...] = sum(gk_y[i] for i in range(YS))
    g_z = [push(spot, spot, ds.at[2, o - 1], dr.at[2, o - 1], at(dz=o)) for o in zorder]
    finish(c0)
    cr_s0[...] = cr_c[rows(x, xspan), :] + cr_x0[0] + cr_x0[1] + cr_x0[2]
    c0 = []
    for o in zorder:
        py = lax.rem(y + o, YS)
        c0.append(push(cr_s0.at[rows(py, xpiece)], cr_y0.at[o - 1], ys.at[2, o - 1], yr.at[2, o - 1], at(dy=o)))
    finish(c1)
    cr_s1[...] = cr_c[tail_rows(y, yspan), :] + sum(cr_y1[i] for i in range(YS - 1))
    c1 = []
    for o in xorder:
        px = lax.rem(x + o, XS)
        c1.append(push(cr_s1.at[rows(px, ypiece)], cr_x1.at[o - 1], xs.at[2, o - 1], xr.at[2, o - 1], at(dx=o)))
    finish(c1)
    spot = full.at[core, tail_rows(y * XS + x, ypiece)]
    spot[...] = cr_s1[rows(x, ypiece), :] + cr_x1[0] + cr_x1[1] + cr_x1[2]
    c1 = [push(spot, spot, xs.at[3, o - 1], xr.at[3, o - 1], at(dx=o)) for o in xorder]
    finish(g_z)
    spot = gk_z.at[:, core]
    g_c = push(spot, spot, cs.at[3], crs.at[3], at(dc=1))
    finish(c0)
    spot = full.at[core, rows(x * YS + y, xpiece)]
    spot[...] = cr_s0[rows(y, xpiece), :] + sum(cr_y0[i] for i in range(YS - 1))
    c0 = [push(spot, spot, ys.at[3, o - 1], yr.at[3, o - 1], at(dy=o)) for o in zorder]
    finish(c1)
    spot = full.at[core, tail_rows(y, yspan)]
    c1 = [push(spot, spot, ys.at[4, o - 1], yr.at[4, o - 1], at(dy=o)) for o in zorder]
    g_c.wait()
    ginv[...] = gk_z[...].reshape(COMP, COMP)

    steps = COMP // BLOCK
    invert_blocks(ginv, 0, steps // 2)
    finish(c0)
    spot = full.at[core, rows(x, xspan)]
    c0 = [push(spot, spot, xs.at[6, o - 1], xr.at[6, o - 1], at(dx=o)) for o in xorder]
    finish(c1)
    spot = full.at[core, tail]
    c1 = push(spot, spot, cs.at[6], crs.at[6], at(dc=1))
    invert_blocks(ginv, steps // 2, steps)
    finish(c0)
    spot = full.at[core, head]
    c0 = push(spot, spot, cs.at[7], crs.at[7], at(dc=1))

    def solve(first, last):
        for j in range(first, last):
            span = pl.ds(j * COMP, COMP)
            block = jnp.concatenate([full[0, span, :], full[1, span, :]], axis=1)
            solved = jnp.dot(ginv[...], block, precision=HIGHEST, preferred_element_type=jnp.float32)
            for i in range(2):
                dt[:, (i * halftiles + j) * 128 : (i * halftiles + j + 1) * 128] = solved[:, i * 128 : i * 128 + 128]

    c1.wait()
    solve(part0, halftiles)
    c0.wait()
    solve(0, part0)
    sent_gram = send_gram(dt, gram2, gram2_in, 1)
    proj2[...] = lax.dot_general(dt[...].astype(jnp.bfloat16), acts[...], NT, preferred_element_type=jnp.float32)
    held = scatter_z(proj2, bufs2, 2)
    dict_out[...] = dt[...].T
    sent_gram = share_gram(sent_gram, gram2, gram2_in, gram2_tiles, 5)
    relay_z(proj2, bufs2, 2, held)
    prod = gram_products(whole_gram(sent_gram, gram2_tiles, 5), mid[...])
    passed = {}
    for p in range(pieces):
        out_t[chunk(z, p), :] = update(mid[chunk(z, p), :], summed_z(proj2, bufs2, held, p), prod, p)
        gather_z(out_t, 3, passed, p)
    for c in held.values():
        c.wait_send()
    forward_z(out_t, 3, passed)


def leave(out_t, dict_in, codes_out, dict_out, held_t, held_codes, held_dict, ins, outs):
    parts = 4
    step = dict_in.shape[0] // parts
    spots = [pl.ds(i * step, step) for i in range(parts)]
    first = pltpu.make_async_copy(out_t, held_t, ins.at[parts])
    first.start()
    arriving = [pltpu.make_async_copy(dict_in.at[p], held_dict.at[p], ins.at[i]) for i, p in enumerate(spots)]
    for c in arriving:
        c.start()
    leaving = []
    for i, p in enumerate(spots):
        arriving[i].wait()
        leaving.append(pltpu.make_async_copy(held_dict.at[p], dict_out.at[p], outs.at[i]))
        leaving[-1].start()
    first.wait()
    held_codes[...] = held_t[...].T
    leaving.append(pltpu.make_async_copy(held_codes, codes_out, outs.at[parts]))
    leaving[-1].start()
    for c in leaving:
        c.wait()


def per_device(acts, dictionary, codes):
    tokens, hid = acts.shape
    f32 = jnp.float32
    v = lambda *s: pltpu.VMEM(s, f32)
    n = COMP // ZS
    half = hid * COMP // 2 // 128
    cut = (hid // 256 - hid // 256 // 3) * COMP
    rest = half - cut
    sums = (v(2, n, tokens), v(2, n // 2, tokens), v(2, n, tokens), v(2, n, tokens), v(2, n, tokens))
    vmem = pl.BlockSpec(memory_space=pltpu.VMEM)
    dma = pltpu.SemaphoreType.DMA
    out_t, dict_new = pl.pallas_call(
        kernel,
        name="semi_nmf",
        out_shape=(jax.ShapeDtypeStruct((COMP, tokens), f32), jax.ShapeDtypeStruct((hid, COMP), f32)),
        in_specs=[vmem] * 3,
        out_specs=(vmem, vmem),
        scratch_shapes=[
            v(COMP, hid), v(COMP, tokens), v(COMP, tokens), v(ZS, 8, 128),
            v(ZS - 1, 8, 128), v(2, XS, 8, 128), v(COMP, tokens),
            v(2, n // 2, COMP), v(n // 2, COMP), v(XS, n // 2, COMP), v(YS, n // 2, COMP), v(ZS, 2, n // 2, COMP),
            v(COMP, COMP),
            v(2, half, 128), v(half, 128), v(XS - 1, cut // XS, 128), v(cut // XS, 128), v(YS - 1, cut // XS // YS, 128),
            v(YS - 1, rest // YS, 128), v(rest // YS, 128), v(XS - 1, rest // YS // XS, 128), v(2, half, 128),
            v(COMP, tokens), v(ZS, 8, 128), v(ZS - 1, 8, 128), v(2, XS, 8, 128),
            *sums, *sums,
            dma((4, 2, 14)), dma((4, 2, 14)), dma((3, ZS - 1)), dma((3, ZS - 1)), dma((5, YS - 1)), dma((5, YS - 1)),
            dma((7, XS - 1)), dma((7, XS - 1)), dma((8,)), dma((8,)),
        ],
        compiler_params=pltpu.CompilerParams(
            collective_id=0, has_side_effects=True, vmem_limit_bytes=56 * 1024 * 1024
        ),
    )(acts, dictionary, codes)
    anywhere = pl.BlockSpec(memory_space=pl.ANY)
    return pl.pallas_call(
        leave,
        name="leave",
        out_shape=(jax.ShapeDtypeStruct((tokens, COMP), f32), jax.ShapeDtypeStruct((hid, COMP), f32)),
        in_specs=[anywhere] * 2,
        out_specs=(anywhere, anywhere),
        scratch_shapes=[v(COMP, tokens), v(tokens, COMP), v(hid, COMP), dma((5,)), dma((5,))],
        compiler_params=pltpu.CompilerParams(vmem_limit_bytes=56 * 1024 * 1024),
    )(out_t, dict_new)


def solution(mesh):
    return jax.shard_map(
        per_device,
        mesh=mesh,
        in_specs=(P("tok", "hid"), P("hid", None), P("tok", None)),
        out_specs=(P("tok", None), P("hid", None)),
        check_vma=False,
    )
```

```python
import functools

import jax
import jax.numpy as jnp
from jax import lax
from jax.experimental import pallas as pl
from jax.experimental.pallas import tpu as pltpu
from jax.sharding import PartitionSpec as P

MESH = pl.DeviceIdType.MESH
HIGHEST = lax.Precision.HIGHEST
floor_value = 0.05
XS, YS, ZS = 4, 8, 8
COMP = 256
BLOCK = 16
TN = (((0,), (0,)), ((), ()))
NT = (((1,), (1,)), ((), ()))


def split3(v):
    hi = v.astype(jnp.bfloat16)
    rest = v - hi.astype(jnp.float32)
    mid = rest.astype(jnp.bfloat16)
    low = (rest - mid.astype(jnp.float32)).astype(jnp.bfloat16)
    return hi, mid, low


def outer6(c, y):
    ch, cm, cl = split3(c)
    yh, ym, yl = split3(y)
    lhs = jnp.concatenate([ch, ch, cm, cm, ch, cl], axis=0)
    rhs = jnp.concatenate([yh, ym, yh, ym, yl, yh], axis=0)
    return lax.dot_general(lhs, rhs, TN, preferred_element_type=jnp.float32)


def panel_invert(panel, k):
    size = panel.shape[1]
    tile = jnp.where(k < 128 // BLOCK, panel[:, :128], panel[:, 128:])
    tile = pltpu.roll(tile, lax.rem(128 - lax.rem(k * BLOCK, 128), 128), 1)
    cols = [jnp.broadcast_to(tile[:, j : j + 1], (BLOCK, 128)) for j in range(BLOCK)]
    row = lax.broadcasted_iota(jnp.int32, (BLOCK, 128), 0)
    lane = lax.broadcasted_iota(jnp.int32, (BLOCK, size), 1) - k * BLOCK
    wide_row = lax.broadcasted_iota(jnp.int32, (BLOCK, size), 0)
    for i in range(BLOCK):
        scaled = jnp.where(row == i, -1.0, cols[i]) * (1.0 / cols[i][i : i + 1, :])
        wide = jnp.concatenate([scaled] * (size // 128), axis=1)
        pivot = panel[i : i + 1, :]
        panel = jnp.where(lane == i, -wide, jnp.where(wide_row == i, 0.0, panel) - wide * pivot)
        for j in range(i + 1, BLOCK):
            c = cols[j][i : i + 1, :]
            cols[j] = jnp.where(row == i, 0.0, cols[j]) - scaled * c
    return panel


def invert_blocks(a, first, last):
    size = a.shape[0]

    def body(k, _):
        rows = pl.ds(pl.multiple_of(k * BLOCK, BLOCK), BLOCK)
        panel = a[rows, :]
        lane = lax.broadcasted_iota(jnp.int32, (1, size), 1)
        column = panel * jnp.where(lane < k * BLOCK, -1.0, 1.0)
        new = panel_invert(panel, k)
        inside = (lane >= k * BLOCK) & (lane < k * BLOCK + BLOCK)
        a[...] = jnp.where(inside, 0.0, a[...]) - outer6(column, new)
        a[rows, :] = new
        return 0

    lax.fori_loop(first, last, body, 0)


def gram_products(gram, codes):
    both = jnp.concatenate([jnp.maximum(-gram, 0.0), jnp.maximum(gram, 0.0)], axis=0)
    return jnp.dot(both, codes, precision=HIGHEST, preferred_element_type=jnp.float32)


def update(part, proj, prod, p):
    n = prod.shape[0] // 2
    numer = jnp.maximum(proj, 0.0) + prod[p * 8 : p * 8 + 8]
    denom = jnp.maximum(jnp.maximum(-proj, 0.0) + prod[n + p * 8 : n + p * 8 + 8], floor_value)
    return part * jnp.sqrt(numer / denom)


def part_list(halftiles):
    b, c = halftiles - 2 * (halftiles * 2 // 7), halftiles * 2 // 7
    return ((0, b, "xy"), (b, c, "xy"), (b + c, c, "yx"))


def kernel(
    acts_in, dic_in, codes_in, out_t, dict_out,
    acts, dic, codes, loaded, dt, ct, proj, gram, gram_in, gram_tiles, mid,
    gk, gk_c, gk_x, gk_y, gk_z, ginv,
    cr, cr_c, full, *rest,
):
    tok, z = lax.axis_index("tok"), lax.axis_index("hid")
    core, x, y = lax.rem(tok, 2), lax.rem(tok // 2, XS), tok // (2 * XS)

    def at(dx=0, dy=0, dz=0, dc=0):
        px, py = lax.rem(x + dx, XS), lax.rem(y + dy, YS)
        return ((py * XS + px) * 2 + lax.rem(core + dc, 2), lax.rem(z + dz, ZS))

    zorder = (4, 3, 5, 2, 6, 1, 7)
    xorder = (2, 1, 3)

    in1, sum1, in2, rest = rest[:3], rest[3:6], rest[6:9], rest[9:]
    (proj2, gram2, gram2_in, gram2_tiles), rest = rest[:4], rest[4:]
    bufs, bufs2, rest = rest[:5], rest[5:10], rest[10:]
    zs, zr, ds, dr, ys, yr, xs, xr, cs, crs = rest

    barrier = pltpu.get_barrier_semaphore()
    partners = [at(dz=o) for o in zorder] + [at(dy=o) for o in zorder] + [at(dx=o) for o in xorder] + [at(dc=1)]
    for p in partners:
        pl.semaphore_signal(barrier, inc=1, device_id=p, device_id_type=MESH)

    def push(src, dst, ss, rs, dev):
        c = pltpu.make_async_remote_copy(
            src_ref=src, dst_ref=dst, send_sem=ss, recv_sem=rs, device_id=dev, device_id_type=MESH
        )
        c.start()
        return c

    def rows(i, n):
        return pl.ds(pl.multiple_of(i * n, n), n)

    n = COMP // ZS

    pieces = n // 8
    ways = (1, -1)

    def chunk(owner, p, size=1):
        return pl.ds(pl.multiple_of(owner * n + p * 8, 8), size * 8)

    def scatter_z(part, bufs, phase):
        via1, via2, relay, fin1, fin2 = bufs
        held = {}
        for i, d in enumerate(ways):
            for p in range(pieces // 2):
                src = part.at[chunk(lax.rem(z + 4, ZS), p + i * (pieces // 2))]
                ss, rs = zs.at[phase, i, p], zr.at[phase, i, p]
                held["via2", i, p + i * (pieces // 2)] = push(src, via2.at[i, pl.ds(p * 8, 8)], ss, rs, at(dz=2 * d + ZS))
        for p in range(pieces):
            for i, d in enumerate(ways):
                src = part.at[chunk(lax.rem(z + 3 * d + ZS, ZS), p)]
                ss, rs = zs.at[phase, i, 2 + p], zr.at[phase, i, 2 + p]
                held["via1", i, p] = push(src, via1.at[i, pl.ds(p * 8, 8)], ss, rs, at(dz=d + ZS))
        for i, d in enumerate(ways):
            src = part.at[chunk(lax.rem(z + d + ZS, ZS), 0, pieces)]
            held["fin1", i] = push(src, fin1.at[i], zs.at[phase, i, 6], zr.at[phase, i, 6], at(dz=d + ZS))
        return held

    def relay_z(part, bufs, phase, held):
        via1, via2, relay, fin1, fin2 = bufs
        for p in range(pieces):
            for i, d in enumerate(ways):
                span = pl.ds(p * 8, 8)
                held["via1", i, p].wait_recv()
                total = part[chunk(lax.rem(z + 2 * d + ZS, ZS), p), :] + via1[i, span, :]
                if p // (pieces // 2) == i:
                    held["via2", i, p].wait_recv()
                    total += via2[i, pl.ds((p - i * (pieces // 2)) * 8, 8), :]
                relay[i, span, :] = total
                ss, rs = zs.at[phase, i, 7 + p], zr.at[phase, i, 7 + p]
                held["fin2", i, p] = push(relay.at[i, span], fin2.at[i, span], ss, rs, at(dz=2 * d + ZS))

    def summed_z(part, bufs, held, p):
        via1, via2, relay, fin1, fin2 = bufs
        span = pl.ds(p * 8, 8)
        total = part[chunk(z, p), :]
        for i in range(2):
            if p == 0:
                held["fin1", i].wait_recv()
            total += fin1[i, span, :]
        for i in range(2):
            held["fin2", i, p].wait_recv()
            total += fin2[i, span, :]
        return total

    def gather_z(buf, phase, held, p):
        spot = buf.at[chunk(z, p)]
        for j, hops in ((0, 2), (4, 1)):
            for i, d in enumerate(ways):
                dev = at(dz=hops * d + ZS)
                held[hops, i, p] = push(spot, spot, zs.at[phase, i, j + p], zr.at[phase, i, j + p], dev)

    def forward_z(buf, phase, held):
        for p in range(pieces):
            for i, d in enumerate(ways):
                held[2, i, p].wait_recv()
                spot = buf.at[chunk(lax.rem(z - 2 * d + ZS, ZS), p)]
                if p // (pieces // 2) == i:
                    q = 8 + p - i * (pieces // 2)
                    held[4, i, p] = push(spot, spot, zs.at[phase, i, q], zr.at[phase, i, q], at(dz=2 * d + ZS))
                held[3, i, p] = push(spot, spot, zs.at[phase, i, 10 + p], zr.at[phase, i, 10 + p], at(dz=d + ZS))
        for key, c in held.items():
            c.wait_send()
            if key[0] != 2:
                c.wait_recv()

    def send_gram(matrix, part, slots, sem):
        picked = [matrix[pl.ds(pl.multiple_of(j * n + x * 8, 8), 8), :] for j in range(ZS)]
        part[...] = lax.dot_general(
            jnp.concatenate(picked, axis=0), matrix[rows(core, 128), :], NT,
            precision=HIGHEST, preferred_element_type=jnp.float32,
        ).reshape(part.shape)
        out = []
        for o in zorder:
            dev = at(dz=o)
            out.append(push(part.at[dev[1]], slots.at[o - 1], ds.at[sem, o - 1], dr.at[sem, o - 1], dev))
        return out

    def share_gram(sent, part, slots, tiles, step, _):
        finish(sent)
        spot = tiles.at[core, x]
        spot[...] = part[z] + sum(slots[i] for i in range(ZS - 1))
        return [push(spot, spot, xs.at[step, o - 1], xr.at[step, o - 1], at(dx=o)) for o in xorder]

    def whole_gram(sent, tiles, _, step):
        finish(sent)
        spot = tiles.at[core]
        push(spot, spot, cs.at[step], crs.at[step], at(dc=1)).wait()
        return jnp.concatenate([tiles[i].reshape(n, 128) for i in range(2)], axis=1)

    def finish(copies):
        for c in copies:
            c.wait()

    loads = [
        pltpu.make_async_copy(src, dst, loaded.at[i])
        for i, (src, dst) in enumerate(((dic_in, dic), (acts_in, acts), (codes_in, codes)))
    ]
    for c in loads:
        c.start()
    loads[0].wait()
    dt[...] = dic[...].T
    loads[1].wait()
    proj[...] = lax.dot_general(dt[...].astype(jnp.bfloat16), acts[...], NT, preferred_element_type=jnp.float32)
    pl.semaphore_wait(barrier, len(partners))
    sent_gram = send_gram(dt, gram, gram_in, 0)
    held = scatter_z(proj, bufs, 0)
    loads[2].wait()
    ct[...] = codes[...].T
    own = rows(z, n)
    sent_gram = share_gram(sent_gram, gram, gram_in, gram_tiles, 7, 8)
    relay_z(proj, bufs, 0, held)
    prod = gram_products(whole_gram(sent_gram, gram_tiles, 7, 8), ct[...])
    passed = {}
    for p in range(pieces):
        mid[chunk(z, p), :] = update(ct[chunk(z, p), :], summed_z(proj, bufs, held, p), prod, p)
        gather_z(mid, 1, passed, p)
    for c in held.values():
        c.wait_send()
    forward_z(mid, 1, passed)

    low = mid[...].astype(jnp.bfloat16)
    low_own = mid[own, :].astype(jnp.bfloat16)
    gk[...] = lax.dot_general(low_own, low, NT, preferred_element_type=jnp.float32).reshape(gk.shape)
    g_c = push(gk.at[1 - core], gk_c, cs.at[6], crs.at[6], at(dc=1))

    halftiles = acts.shape[1] // 256
    parts = part_list(halftiles)

    def cross(which, p):
        first, count, _ = parts[p]
        lanes = pl.ds(pl.multiple_of((which * halftiles + first) * 128, 128), count * 128)
        block = jnp.dot(low, acts[:, lanes], preferred_element_type=jnp.float32)
        for j in range(count):
            cr[which, pl.ds((first + j) * COMP, COMP), :] = block[:, j * 128 : j * 128 + 128]

    axes = {"x": (x, XS, xorder, xs, xr), "y": (y, YS, zorder, ys, yr)}

    def shares(p):
        first, count, order = parts[p]
        one, two = axes[order[0]], axes[order[1]]
        size = count * COMP
        return first * COMP, size, one, two, size // one[1], size // one[1] // two[1]

    def span_of(base, i, size):
        return pl.ds(pl.multiple_of(base + i * size, size), size)

    def along(name, row, src_of, dst_of):
        me, count, order, ss, rs = axes[name]
        out = []
        for o in order:
            dev = at(dx=o) if name == "x" else at(dy=o)
            out.append(push(src_of(lax.rem(me + o, count)), dst_of(o), ss.at[row, o - 1], rs.at[row, o - 1], dev))
        return out

    def send_core(p):
        base, size, _, _, _, _ = shares(p)
        span = pl.ds(base, size)
        return [push(cr.at[1 - core, span], cr_c.at[span], cs.at[p], crs.at[p], at(dc=1))]

    def send_first(p, copies):
        finish(copies)
        base, size, one, two, n1, n2 = shares(p)
        span = pl.ds(base, size)
        cr_c[span, :] += cr[core, span, :]
        return along(parts[p][2][0], 2 * p, lambda i: cr_c.at[span_of(base, i, n1)], lambda o: in1[p].at[o - 1])

    def send_second(p, copies):
        finish(copies)
        base, size, one, two, n1, n2 = shares(p)
        sum1[p][...] = cr_c[span_of(base, one[0], n1), :] + sum(in1[p][i] for i in range(one[1] - 1))
        return along(parts[p][2][1], 2 * p, lambda i: sum1[p].at[span_of(0, i, n2)], lambda o: in2[p].at[o - 1])

    def gather_second(p, copies):
        finish(copies)
        base, size, one, two, n1, n2 = shares(p)
        spot = full.at[core, span_of(base, one[0] * two[1] + two[0], n2)]
        spot[...] = sum1[p][span_of(0, two[0], n2), :] + sum(in2[p][i] for i in range(two[1] - 1))
        return along(parts[p][2][1], 2 * p + 1, lambda i: spot, lambda o: spot)

    def gather_first(p, copies):
        finish(copies)
        base, size, one, two, n1, n2 = shares(p)
        spot = full.at[core, span_of(base, one[0], n1)]
        return along(parts[p][2][0], 2 * p + 1, lambda i: spot, lambda o: spot)

    def gather_core(p, copies):
        finish(copies)
        base, size, _, _, _, _ = shares(p)
        spot = full.at[core, pl.ds(base, size)]
        return [push(spot, spot, cs.at[3 + p], crs.at[3 + p], at(dc=1))]

    c = [None] * 3
    for p in range(3):
        cross(1 - core, p)
        c[p] = send_core(p)
    g_c.wait()
    gk_x[x] = gk[core] + gk_c[...]
    g_x = along("x", 6, lambda i: gk_x.at[x], lambda o: gk_x.at[x])
    for p in range(3):
        cross(core, p)
    c[0] = send_first(0, c[0])
    c[1] = send_first(1, c[1])
    finish(g_x)
    gk_y[y] = sum(gk_x[i] for i in range(XS))
    g_y = along("y", 6, lambda i: gk_y.at[y], lambda o: gk_y.at[y])
    c[2] = send_first(2, c[2])
    c[0] = send_second(0, c[0])
    c[1] = send_second(1, c[1])
    finish(g_y)
    spot = gk_z.at[z, core]
    spot[...] = sum(gk_y[i] for i in range(YS))
    g_z = [push(spot, spot, ds.at[2, o - 1], dr.at[2, o - 1], at(dz=o)) for o in zorder]
    c[2] = send_second(2, c[2])
    c[0] = gather_second(0, c[0])
    c[1] = gather_second(1, c[1])
    c[2] = gather_second(2, c[2])
    finish(g_z)
    spot = gk_z.at[:, core]
    g_c = push(spot, spot, cs.at[7], crs.at[7], at(dc=1))
    c[2] = gather_first(2, c[2])
    g_c.wait()
    ginv[...] = gk_z[...].reshape(COMP, COMP)

    invert_blocks(ginv, 0, 2)
    c[0] = gather_first(0, c[0])
    c[1] = gather_first(1, c[1])
    invert_blocks(ginv, 2, 8)
    c[0] = gather_core(0, c[0])
    c[2] = gather_core(2, c[2])
    invert_blocks(ginv, 8, 12)
    c[1] = gather_core(1, c[1])
    invert_blocks(ginv, 12, 16)

    def solve(first, last):
        for j in range(first, last):
            span = pl.ds(j * COMP, COMP)
            block = jnp.concatenate([full[0, span, :], full[1, span, :]], axis=1)
            solved = jnp.dot(ginv[...], block, precision=HIGHEST, preferred_element_type=jnp.float32)
            for i in range(2):
                dt[:, (i * halftiles + j) * 128 : (i * halftiles + j + 1) * 128] = solved[:, i * 128 : i * 128 + 128]

    for p in (0, 2, 1):
        finish(c[p])
        solve(parts[p][0], parts[p][0] + parts[p][1])
    sent_gram = send_gram(dt, gram2, gram2_in, 1)
    proj2[...] = lax.dot_general(dt[...].astype(jnp.bfloat16), acts[...], NT, preferred_element_type=jnp.float32)
    held = scatter_z(proj2, bufs2, 2)
    dict_out[...] = dt[...].T
    sent_gram = share_gram(sent_gram, gram2, gram2_in, gram2_tiles, 8, 9)
    relay_z(proj2, bufs2, 2, held)
    prod = gram_products(whole_gram(sent_gram, gram2_tiles, 8, 9), mid[...])
    passed = {}
    for p in range(pieces):
        out_t[chunk(z, p), :] = update(mid[chunk(z, p), :], summed_z(proj2, bufs2, held, p), prod, p)
        gather_z(out_t, 3, passed, p)
    for c in held.values():
        c.wait_send()
    forward_z(out_t, 3, passed)


def leave(out_t, dict_in, codes_out, dict_out, held, sem):
    parts = 4
    step = dict_in.shape[0] // parts
    spots = [pl.ds(i * step, step) for i in range(parts)]
    copies = [pltpu.make_async_copy(dict_in.at[p], dict_out.at[p], sem.at[i]) for i, p in enumerate(spots)]
    for c in copies:
        c.start()
    held[...] = out_t[...].T
    copies.append(pltpu.make_async_copy(held, codes_out, sem.at[parts]))
    copies[-1].start()
    for c in copies:
        c.wait()


def per_device(acts, dictionary, codes):
    tokens, hid = acts.shape
    f32 = jnp.float32
    v = lambda *s: pltpu.VMEM(s, f32)
    n = COMP // ZS
    half = hid * COMP // 2 // 128
    count = {"x": XS, "y": YS}
    shapes = [(k * COMP, count[order[0]], count[order[1]]) for _, k, order in part_list(hid // 256)]
    sums = (v(2, n, tokens), v(2, n // 2, tokens), v(2, n, tokens), v(2, n, tokens), v(2, n, tokens))
    vmem = pl.BlockSpec(memory_space=pltpu.VMEM)
    anywhere = pl.BlockSpec(memory_space=pl.ANY)
    dma = pltpu.SemaphoreType.DMA
    out_t, dict_new = pl.pallas_call(
        kernel,
        name="semi_nmf",
        out_shape=(pltpu.VMEM((COMP, tokens), f32), pltpu.VMEM((hid, COMP), f32)),
        in_specs=[anywhere] * 3,
        out_specs=(vmem, vmem),
        scratch_shapes=[
            pltpu.VMEM((tokens, hid), jnp.bfloat16), v(hid, COMP), v(tokens, COMP), dma((3,)),
            v(COMP, hid), v(COMP, tokens), v(COMP, tokens), v(ZS, 8, 128),
            v(ZS - 1, 8, 128), v(2, XS, 8, 128), v(COMP, tokens),
            v(2, n // 2, COMP), v(n // 2, COMP), v(XS, n // 2, COMP), v(YS, n // 2, COMP), v(ZS, 2, n // 2, COMP),
            v(COMP, COMP),
            v(2, half, 128), v(half, 128), v(2, half, 128),
            *[v(one - 1, size // one, 128) for size, one, two in shapes],
            *[v(size // one, 128) for size, one, two in shapes],
            *[v(two - 1, size // one // two, 128) for size, one, two in shapes],
            v(COMP, tokens), v(ZS, 8, 128), v(ZS - 1, 8, 128), v(2, XS, 8, 128),
            *sums, *sums,
            dma((4, 2, 14)), dma((4, 2, 14)), dma((3, ZS - 1)), dma((3, ZS - 1)), dma((7, YS - 1)), dma((7, YS - 1)),
            dma((9, XS - 1)), dma((9, XS - 1)), dma((10,)), dma((10,)),
        ],
        compiler_params=pltpu.CompilerParams(
            collective_id=0, has_side_effects=True, vmem_limit_bytes=56 * 1024 * 1024
        ),
    )(acts, dictionary, codes)
    return pl.pallas_call(
        leave,
        name="leave",
        out_shape=(jax.ShapeDtypeStruct((tokens, COMP), f32), jax.ShapeDtypeStruct((hid, COMP), f32)),
        in_specs=[vmem] * 2,
        out_specs=(anywhere, anywhere),
        scratch_shapes=[v(tokens, COMP), dma((5,))],
        compiler_params=pltpu.CompilerParams(vmem_limit_bytes=16 * 1024 * 1024),
    )(out_t, dict_new)


def solution(mesh):
    return jax.shard_map(
        per_device,
        mesh=mesh,
        in_specs=(P("tok", "hid"), P("hid", None), P("tok", None)),
        out_specs=(P("tok", None), P("hid", None)),
        check_vma=False,
    )
```

```python
import functools

import jax
import jax.numpy as jnp
from jax import lax
from jax.experimental import pallas as pl
from jax.experimental.pallas import tpu as pltpu
from jax.sharding import PartitionSpec as P

MESH = pl.DeviceIdType.MESH
HIGHEST = lax.Precision.HIGHEST
floor_value = 0.05
XS, YS, ZS = 4, 8, 8
COMP = 256
BLOCK = 16
TN = (((0,), (0,)), ((), ()))
NT = (((1,), (1,)), ((), ()))


def split3(v):
    hi = v.astype(jnp.bfloat16)
    rest = v - hi.astype(jnp.float32)
    mid = rest.astype(jnp.bfloat16)
    low = (rest - mid.astype(jnp.float32)).astype(jnp.bfloat16)
    return hi, mid, low


def split2(v):
    hi = v.astype(jnp.bfloat16)
    return jnp.concatenate([hi, (v - hi.astype(jnp.float32)).astype(jnp.bfloat16)], axis=0)


def outer6(c, y):
    ch, cm, cl = split3(c)
    yh, ym, yl = split3(y)
    lhs = jnp.concatenate([ch, ch, cm, cm, ch, cl], axis=0)
    rhs = jnp.concatenate([yh, ym, yh, ym, yl, yh], axis=0)
    return lax.dot_general(lhs, rhs, TN, preferred_element_type=jnp.float32)


def panel_invert(panel, k):
    size = panel.shape[1]
    tile = jnp.where(k < 128 // BLOCK, panel[:, :128], panel[:, 128:])
    tile = pltpu.roll(tile, lax.rem(128 - lax.rem(k * BLOCK, 128), 128), 1)
    cols = [jnp.broadcast_to(tile[:, j : j + 1], (BLOCK, 128)) for j in range(BLOCK)]
    row = lax.broadcasted_iota(jnp.int32, (BLOCK, 128), 0)
    lane = lax.broadcasted_iota(jnp.int32, (BLOCK, size), 1) - k * BLOCK
    wide_row = lax.broadcasted_iota(jnp.int32, (BLOCK, size), 0)
    for i in range(BLOCK):
        scaled = jnp.where(row == i, -1.0, cols[i]) * (1.0 / cols[i][i : i + 1, :])
        wide = jnp.concatenate([scaled] * (size // 128), axis=1)
        pivot = panel[i : i + 1, :]
        panel = jnp.where(lane == i, -wide, jnp.where(wide_row == i, 0.0, panel) - wide * pivot)
        for j in range(i + 1, BLOCK):
            c = cols[j][i : i + 1, :]
            cols[j] = jnp.where(row == i, 0.0, cols[j]) - scaled * c
    return panel


def invert_blocks(a, first, last):
    size = a.shape[0]

    def body(k, _):
        rows = pl.ds(pl.multiple_of(k * BLOCK, BLOCK), BLOCK)
        panel = a[rows, :]
        lane = lax.broadcasted_iota(jnp.int32, (1, size), 1)
        column = panel * jnp.where(lane < k * BLOCK, -1.0, 1.0)
        new = panel_invert(panel, k)
        inside = (lane >= k * BLOCK) & (lane < k * BLOCK + BLOCK)
        a[...] = jnp.where(inside, 0.0, a[...]) - outer6(column, new)
        a[rows, :] = new
        return 0

    lax.fori_loop(first, last, body, 0)


def gram_products(gram, codes):
    both = jnp.concatenate([jnp.maximum(-gram, 0.0), jnp.maximum(gram, 0.0)], axis=0)
    return jnp.dot(both, codes, precision=HIGHEST, preferred_element_type=jnp.float32)


def update(part, proj, prod, p):
    n = prod.shape[0] // 2
    numer = jnp.maximum(proj, 0.0) + prod[p * 8 : p * 8 + 8]
    denom = jnp.maximum(jnp.maximum(-proj, 0.0) + prod[n + p * 8 : n + p * 8 + 8], floor_value)
    return part * jnp.sqrt(numer / denom)


def part_list(halftiles):
    b, c = halftiles - 2 * (halftiles * 2 // 7), halftiles * 2 // 7
    return ((0, b, "xy"), (b, c, "xy"), (b + c, c, "yx"))


def kernel(
    acts_in, dic_in, codes_in, out_t, dict_out,
    acts, dic, codes, loaded, dt, ct, proj, gram, gram_in, gram_tiles, mid,
    gk, gk_c, gk_x, gk_y, gk_z, ginv,
    cr, cr_c, full, *rest,
):
    tok, z = lax.axis_index("tok"), lax.axis_index("hid")
    core, x, y = lax.rem(tok, 2), lax.rem(tok // 2, XS), tok // (2 * XS)

    def at(dx=0, dy=0, dz=0, dc=0):
        px, py = lax.rem(x + dx, XS), lax.rem(y + dy, YS)
        return ((py * XS + px) * 2 + lax.rem(core + dc, 2), lax.rem(z + dz, ZS))

    zorder = (4, 3, 5, 2, 6, 1, 7)
    xorder = (2, 1, 3)

    in1, sum1, in2, rest = rest[:3], rest[3:6], rest[6:9], rest[9:]
    (proj2, gram2, gram2_in, gram2_tiles), rest = rest[:4], rest[4:]
    bufs, bufs2, rest = rest[:5], rest[5:10], rest[10:]
    zs, zr, ds, dr, ys, yr, xs, xr, cs, crs = rest

    barrier = pltpu.get_barrier_semaphore()
    partners = [at(dz=o) for o in zorder] + [at(dy=o) for o in zorder] + [at(dx=o) for o in xorder] + [at(dc=1)]
    for p in partners:
        pl.semaphore_signal(barrier, inc=1, device_id=p, device_id_type=MESH)

    def push(src, dst, ss, rs, dev):
        c = pltpu.make_async_remote_copy(
            src_ref=src, dst_ref=dst, send_sem=ss, recv_sem=rs, device_id=dev, device_id_type=MESH
        )
        c.start()
        return c

    def rows(i, n):
        return pl.ds(pl.multiple_of(i * n, n), n)

    n = COMP // ZS

    pieces = n // 8
    ways = (1, -1)

    def chunk(owner, p, size=1):
        return pl.ds(pl.multiple_of(owner * n + p * 8, 8), size * 8)

    def scatter_z(part, bufs, phase):
        via1, via2, relay, fin1, fin2 = bufs
        held = {}
        for i, d in enumerate(ways):
            for p in range(pieces // 2):
                src = part.at[chunk(lax.rem(z + 4, ZS), p + i * (pieces // 2))]
                ss, rs = zs.at[phase, i, p], zr.at[phase, i, p]
                held["via2", i, p + i * (pieces // 2)] = push(src, via2.at[i, pl.ds(p * 8, 8)], ss, rs, at(dz=2 * d + ZS))
        for p in range(pieces):
            for i, d in enumerate(ways):
                src = part.at[chunk(lax.rem(z + 3 * d + ZS, ZS), p)]
                ss, rs = zs.at[phase, i, 2 + p], zr.at[phase, i, 2 + p]
                held["via1", i, p] = push(src, via1.at[i, pl.ds(p * 8, 8)], ss, rs, at(dz=d + ZS))
        for i, d in enumerate(ways):
            src = part.at[chunk(lax.rem(z + d + ZS, ZS), 0, pieces)]
            held["fin1", i] = push(src, fin1.at[i], zs.at[phase, i, 6], zr.at[phase, i, 6], at(dz=d + ZS))
        return held

    def relay_z(part, bufs, phase, held):
        via1, via2, relay, fin1, fin2 = bufs
        for p in range(pieces):
            for i, d in enumerate(ways):
                span = pl.ds(p * 8, 8)
                held["via1", i, p].wait_recv()
                total = part[chunk(lax.rem(z + 2 * d + ZS, ZS), p), :] + via1[i, span, :]
                if p // (pieces // 2) == i:
                    held["via2", i, p].wait_recv()
                    total += via2[i, pl.ds((p - i * (pieces // 2)) * 8, 8), :]
                relay[i, span, :] = total
                ss, rs = zs.at[phase, i, 7 + p], zr.at[phase, i, 7 + p]
                held["fin2", i, p] = push(relay.at[i, span], fin2.at[i, span], ss, rs, at(dz=2 * d + ZS))

    def summed_z(part, bufs, held, p):
        via1, via2, relay, fin1, fin2 = bufs
        span = pl.ds(p * 8, 8)
        total = part[chunk(z, p), :]
        for i in range(2):
            if p == 0:
                held["fin1", i].wait_recv()
            total += fin1[i, span, :]
        for i in range(2):
            held["fin2", i, p].wait_recv()
            total += fin2[i, span, :]
        return total

    def gather_z(buf, phase, held, p):
        spot = buf.at[chunk(z, p)]
        for j, hops in ((0, 2), (4, 1)):
            for i, d in enumerate(ways):
                dev = at(dz=hops * d + ZS)
                held[hops, i, p] = push(spot, spot, zs.at[phase, i, j + p], zr.at[phase, i, j + p], dev)

    def forward_z(buf, phase, held):
        for p in range(pieces):
            for i, d in enumerate(ways):
                held[2, i, p].wait_recv()
                spot = buf.at[chunk(lax.rem(z - 2 * d + ZS, ZS), p)]
                if p // (pieces // 2) == i:
                    q = 8 + p - i * (pieces // 2)
                    held[4, i, p] = push(spot, spot, zs.at[phase, i, q], zr.at[phase, i, q], at(dz=2 * d + ZS))
                held[3, i, p] = push(spot, spot, zs.at[phase, i, 10 + p], zr.at[phase, i, 10 + p], at(dz=d + ZS))
        for key, c in held.items():
            c.wait_send()
            if key[0] != 2:
                c.wait_recv()

    def send_gram(matrix, part, slots, sem):
        picked = [matrix[pl.ds(pl.multiple_of(j * n + x * 8, 8), 8), :] for j in range(ZS)]
        both = split2(jnp.concatenate(picked, axis=0))
        prod = lax.dot_general(both, split2(matrix[rows(core, 128), :]), NT, preferred_element_type=jnp.float32)
        m = 8 * ZS
        tile = prod[:m, :128] + (prod[:m, 128:] + prod[m:, :128] + prod[m:, 128:])
        part[...] = tile.reshape(part.shape)
        out = []
        for o in zorder:
            dev = at(dz=o)
            out.append(push(part.at[dev[1]], slots.at[o - 1], ds.at[sem, o - 1], dr.at[sem, o - 1], dev))
        return out

    def share_gram(sent, part, slots, tiles, step, _):
        finish(sent)
        spot = tiles.at[core, x]
        spot[...] = part[z] + sum(slots[i] for i in range(ZS - 1))
        return [push(spot, spot, xs.at[step, o - 1], xr.at[step, o - 1], at(dx=o)) for o in xorder]

    def whole_gram(sent, tiles, _, step):
        finish(sent)
        spot = tiles.at[core]
        push(spot, spot, cs.at[step], crs.at[step], at(dc=1)).wait()
        return jnp.concatenate([tiles[i].reshape(n, 128) for i in range(2)], axis=1)

    def finish(copies):
        for c in copies:
            c.wait()

    loads = [
        pltpu.make_async_copy(src, dst, loaded.at[i])
        for i, (src, dst) in enumerate(((dic_in, dic), (acts_in, acts), (codes_in, codes)))
    ]
    for c in loads:
        c.start()
    loads[0].wait()
    dt[...] = dic[...].T
    loads[1].wait()
    proj[...] = lax.dot_general(dt[...].astype(jnp.bfloat16), acts[...], NT, preferred_element_type=jnp.float32)
    pl.semaphore_wait(barrier, len(partners))
    sent_gram = send_gram(dt, gram, gram_in, 0)
    held = scatter_z(proj, bufs, 0)
    loads[2].wait()
    ct[...] = codes[...].T
    own = rows(z, n)
    sent_gram = share_gram(sent_gram, gram, gram_in, gram_tiles, 7, 8)
    relay_z(proj, bufs, 0, held)
    prod = gram_products(whole_gram(sent_gram, gram_tiles, 7, 8), ct[...])
    passed = {}
    for p in range(pieces):
        mid[chunk(z, p), :] = update(ct[chunk(z, p), :], summed_z(proj, bufs, held, p), prod, p)
        gather_z(mid, 1, passed, p)
    for c in held.values():
        c.wait_send()
    forward_z(mid, 1, passed)

    low = mid[...].astype(jnp.bfloat16)
    low_own = mid[own, :].astype(jnp.bfloat16)
    gk[...] = lax.dot_general(low_own, low, NT, preferred_element_type=jnp.float32).reshape(gk.shape)
    g_c = push(gk.at[1 - core], gk_c, cs.at[6], crs.at[6], at(dc=1))

    halftiles = acts.shape[1] // 256
    parts = part_list(halftiles)

    def cross(which, p):
        first, count, _ = parts[p]
        lanes = pl.ds(pl.multiple_of((which * halftiles + first) * 128, 128), count * 128)
        block = jnp.dot(low, acts[:, lanes], preferred_element_type=jnp.float32)
        for j in range(count):
            cr[which, pl.ds((first + j) * COMP, COMP), :] = block[:, j * 128 : j * 128 + 128]

    axes = {"x": (x, XS, xorder, xs, xr), "y": (y, YS, zorder, ys, yr)}

    def shares(p):
        first, count, order = parts[p]
        one, two = axes[order[0]], axes[order[1]]
        size = count * COMP
        return first * COMP, size, one, two, size // one[1], size // one[1] // two[1]

    def span_of(base, i, size):
        return pl.ds(pl.multiple_of(base + i * size, size), size)

    def along(name, row, src_of, dst_of):
        me, count, order, ss, rs = axes[name]
        out = []
        for o in order:
            dev = at(dx=o) if name == "x" else at(dy=o)
            out.append(push(src_of(lax.rem(me + o, count)), dst_of(o), ss.at[row, o - 1], rs.at[row, o - 1], dev))
        return out

    def send_core(p):
        base, size, _, _, _, _ = shares(p)
        span = pl.ds(base, size)
        return [push(cr.at[1 - core, span], cr_c.at[span], cs.at[p], crs.at[p], at(dc=1))]

    def send_first(p, copies):
        finish(copies)
        base, size, one, two, n1, n2 = shares(p)
        span = pl.ds(base, size)
        cr_c[span, :] += cr[core, span, :]
        return along(parts[p][2][0], 2 * p, lambda i: cr_c.at[span_of(base, i, n1)], lambda o: in1[p].at[o - 1])

    def send_second(p, copies):
        finish(copies)
        base, size, one, two, n1, n2 = shares(p)
        sum1[p][...] = cr_c[span_of(base, one[0], n1), :] + sum(in1[p][i] for i in range(one[1] - 1))
        return along(parts[p][2][1], 2 * p, lambda i: sum1[p].at[span_of(0, i, n2)], lambda o: in2[p].at[o - 1])

    def gather_second(p, copies):
        finish(copies)
        base, size, one, two, n1, n2 = shares(p)
        spot = full.at[core, span_of(base, one[0] * two[1] + two[0], n2)]
        spot[...] = sum1[p][span_of(0, two[0], n2), :] + sum(in2[p][i] for i in range(two[1] - 1))
        return along(parts[p][2][1], 2 * p + 1, lambda i: spot, lambda o: spot)

    def gather_first(p, copies):
        finish(copies)
        base, size, one, two, n1, n2 = shares(p)
        spot = full.at[core, span_of(base, one[0], n1)]
        return along(parts[p][2][0], 2 * p + 1, lambda i: spot, lambda o: spot)

    def gather_core(p, copies):
        finish(copies)
        base, size, _, _, _, _ = shares(p)
        spot = full.at[core, pl.ds(base, size)]
        return [push(spot, spot, cs.at[3 + p], crs.at[3 + p], at(dc=1))]

    c = [None] * 3
    for p in range(3):
        cross(1 - core, p)
        c[p] = send_core(p)
    g_c.wait()
    gk_x[x] = gk[core] + gk_c[...]
    g_x = along("x", 6, lambda i: gk_x.at[x], lambda o: gk_x.at[x])
    for p in range(3):
        cross(core, p)
    c[0] = send_first(0, c[0])
    c[1] = send_first(1, c[1])
    finish(g_x)
    gk_y[y] = sum(gk_x[i] for i in range(XS))
    g_y = along("y", 6, lambda i: gk_y.at[y], lambda o: gk_y.at[y])
    c[2] = send_first(2, c[2])
    c[0] = send_second(0, c[0])
    c[1] = send_second(1, c[1])
    finish(g_y)
    spot = gk_z.at[z, core]
    spot[...] = sum(gk_y[i] for i in range(YS))
    g_z = [push(spot, spot, ds.at[2, o - 1], dr.at[2, o - 1], at(dz=o)) for o in zorder]
    c[0] = gather_second(0, c[0])
    c[2] = send_second(2, c[2])
    c[1] = gather_second(1, c[1])
    finish(g_z)
    spot = gk_z.at[:, core]
    g_c = push(spot, spot, cs.at[7], crs.at[7], at(dc=1))
    c[2] = gather_second(2, c[2])
    g_c.wait()
    ginv[...] = gk_z[...].reshape(COMP, COMP)

    invert_blocks(ginv, 0, 3)
    c[0] = gather_first(0, c[0])
    c[2] = gather_first(2, c[2])
    invert_blocks(ginv, 3, 5)
    c[1] = gather_first(1, c[1])
    invert_blocks(ginv, 5, 11)
    c[0] = gather_core(0, c[0])
    invert_blocks(ginv, 11, 14)
    c[1] = gather_core(1, c[1])
    c[2] = gather_core(2, c[2])
    invert_blocks(ginv, 14, 16)

    def solve(first, last):
        for j in range(first, last):
            span = pl.ds(j * COMP, COMP)
            block = jnp.concatenate([full[0, span, :], full[1, span, :]], axis=1)
            solved = jnp.dot(ginv[...], block, precision=HIGHEST, preferred_element_type=jnp.float32)
            for i in range(2):
                dt[:, (i * halftiles + j) * 128 : (i * halftiles + j + 1) * 128] = solved[:, i * 128 : i * 128 + 128]

    for p in (0, 2, 1):
        finish(c[p])
        solve(parts[p][0], parts[p][0] + parts[p][1])
    sent_gram = send_gram(dt, gram2, gram2_in, 1)
    proj2[...] = lax.dot_general(dt[...].astype(jnp.bfloat16), acts[...], NT, preferred_element_type=jnp.float32)
    held = scatter_z(proj2, bufs2, 2)
    dict_out[...] = dt[...].T
    sent_gram = share_gram(sent_gram, gram2, gram2_in, gram2_tiles, 8, 9)
    relay_z(proj2, bufs2, 2, held)
    prod = gram_products(whole_gram(sent_gram, gram2_tiles, 8, 9), mid[...])
    passed = {}
    for p in range(pieces):
        out_t[chunk(z, p), :] = update(mid[chunk(z, p), :], summed_z(proj2, bufs2, held, p), prod, p)
        gather_z(out_t, 3, passed, p)
    for c in held.values():
        c.wait_send()
    forward_z(out_t, 3, passed)


def leave(out_t, dict_in, codes_out, dict_out, held, sem):
    parts = 4
    step = dict_in.shape[0] // parts
    spots = [pl.ds(i * step, step) for i in range(parts)]
    copies = [pltpu.make_async_copy(dict_in.at[p], dict_out.at[p], sem.at[i]) for i, p in enumerate(spots)]
    for c in copies:
        c.start()
    held[...] = out_t[...].T
    copies.append(pltpu.make_async_copy(held, codes_out, sem.at[parts]))
    copies[-1].start()
    for c in copies:
        c.wait()


def per_device(acts, dictionary, codes):
    tokens, hid = acts.shape
    f32 = jnp.float32
    v = lambda *s: pltpu.VMEM(s, f32)
    n = COMP // ZS
    half = hid * COMP // 2 // 128
    count = {"x": XS, "y": YS}
    shapes = [(k * COMP, count[order[0]], count[order[1]]) for _, k, order in part_list(hid // 256)]
    sums = (v(2, n, tokens), v(2, n // 2, tokens), v(2, n, tokens), v(2, n, tokens), v(2, n, tokens))
    vmem = pl.BlockSpec(memory_space=pltpu.VMEM)
    anywhere = pl.BlockSpec(memory_space=pl.ANY)
    dma = pltpu.SemaphoreType.DMA
    out_t, dict_new = pl.pallas_call(
        kernel,
        name="semi_nmf",
        out_shape=(pltpu.VMEM((COMP, tokens), f32), pltpu.VMEM((hid, COMP), f32)),
        in_specs=[anywhere] * 3,
        out_specs=(vmem, vmem),
        scratch_shapes=[
            pltpu.VMEM((tokens, hid), jnp.bfloat16), v(hid, COMP), v(tokens, COMP), dma((3,)),
            v(COMP, hid), v(COMP, tokens), v(COMP, tokens), v(ZS, 8, 128),
            v(ZS - 1, 8, 128), v(2, XS, 8, 128), v(COMP, tokens),
            v(2, n // 2, COMP), v(n // 2, COMP), v(XS, n // 2, COMP), v(YS, n // 2, COMP), v(ZS, 2, n // 2, COMP),
            v(COMP, COMP),
            v(2, half, 128), v(half, 128), v(2, half, 128),
            *[v(one - 1, size // one, 128) for size, one, two in shapes],
            *[v(size // one, 128) for size, one, two in shapes],
            *[v(two - 1, size // one // two, 128) for size, one, two in shapes],
            v(COMP, tokens), v(ZS, 8, 128), v(ZS - 1, 8, 128), v(2, XS, 8, 128),
            *sums, *sums,
            dma((4, 2, 14)), dma((4, 2, 14)), dma((3, ZS - 1)), dma((3, ZS - 1)), dma((7, YS - 1)), dma((7, YS - 1)),
            dma((9, XS - 1)), dma((9, XS - 1)), dma((10,)), dma((10,)),
        ],
        compiler_params=pltpu.CompilerParams(
            collective_id=0, has_side_effects=True, vmem_limit_bytes=56 * 1024 * 1024
        ),
    )(acts, dictionary, codes)
    return pl.pallas_call(
        leave,
        name="leave",
        out_shape=(jax.ShapeDtypeStruct((tokens, COMP), f32), jax.ShapeDtypeStruct((hid, COMP), f32)),
        in_specs=[vmem] * 2,
        out_specs=(anywhere, anywhere),
        scratch_shapes=[v(tokens, COMP), dma((5,))],
        compiler_params=pltpu.CompilerParams(vmem_limit_bytes=16 * 1024 * 1024),
    )(out_t, dict_new)


def solution(mesh):
    return jax.shard_map(
        per_device,
        mesh=mesh,
        in_specs=(P("tok", "hid"), P("hid", None), P("tok", None)),
        out_specs=(P("tok", None), P("hid", None)),
        check_vma=False,
    )
```

```python
import functools

import jax
import jax.numpy as jnp
from jax import lax
from jax.experimental import pallas as pl
from jax.experimental.pallas import tpu as pltpu
from jax.sharding import PartitionSpec as P

MESH = pl.DeviceIdType.MESH
HIGHEST = lax.Precision.HIGHEST
floor_value = 0.05
XS, YS, ZS = 4, 8, 8
COMP = 256
BLOCK = 16
TN = (((0,), (0,)), ((), ()))
NT = (((1,), (1,)), ((), ()))


def split3(v):
    hi = v.astype(jnp.bfloat16)
    rest = v - hi.astype(jnp.float32)
    mid = rest.astype(jnp.bfloat16)
    low = (rest - mid.astype(jnp.float32)).astype(jnp.bfloat16)
    return hi, mid, low


def split2(v):
    hi = v.astype(jnp.bfloat16)
    return jnp.concatenate([hi, (v - hi.astype(jnp.float32)).astype(jnp.bfloat16)], axis=0)


def outer6(c, y):
    ch, cm, cl = split3(c)
    yh, ym, yl = split3(y)
    lhs = jnp.concatenate([ch, ch, cm, cm, ch, cl], axis=0)
    rhs = jnp.concatenate([yh, ym, yh, ym, yl, yh], axis=0)
    return lax.dot_general(lhs, rhs, TN, preferred_element_type=jnp.float32)


def panel_invert(panel, k):
    size = panel.shape[1]
    tile = jnp.where(k < 128 // BLOCK, panel[:, :128], panel[:, 128:])
    tile = pltpu.roll(tile, lax.rem(128 - lax.rem(k * BLOCK, 128), 128), 1)
    cols = [jnp.broadcast_to(tile[:, j : j + 1], (BLOCK, 128)) for j in range(BLOCK)]
    row = lax.broadcasted_iota(jnp.int32, (BLOCK, 128), 0)
    lane = lax.broadcasted_iota(jnp.int32, (BLOCK, size), 1) - k * BLOCK
    wide_row = lax.broadcasted_iota(jnp.int32, (BLOCK, size), 0)
    for i in range(BLOCK):
        scaled = jnp.where(row == i, -1.0, cols[i]) * (1.0 / cols[i][i : i + 1, :])
        wide = jnp.concatenate([scaled] * (size // 128), axis=1)
        pivot = panel[i : i + 1, :]
        panel = jnp.where(lane == i, -wide, jnp.where(wide_row == i, 0.0, panel) - wide * pivot)
        for j in range(i + 1, BLOCK):
            c = cols[j][i : i + 1, :]
            cols[j] = jnp.where(row == i, 0.0, cols[j]) - scaled * c
    return panel


def invert_blocks(a, first, last):
    size = a.shape[0]

    def body(k, _):
        rows = pl.ds(pl.multiple_of(k * BLOCK, BLOCK), BLOCK)
        panel = a[rows, :]
        lane = lax.broadcasted_iota(jnp.int32, (1, size), 1)
        column = panel * jnp.where(lane < k * BLOCK, -1.0, 1.0)
        new = panel_invert(panel, k)
        inside = (lane >= k * BLOCK) & (lane < k * BLOCK + BLOCK)
        a[...] = jnp.where(inside, 0.0, a[...]) - outer6(column, new)
        a[rows, :] = new
        return 0

    lax.fori_loop(first, last, body, 0)


def gram_products(gram, codes):
    both = jnp.concatenate([jnp.maximum(-gram, 0.0), jnp.maximum(gram, 0.0)], axis=0)
    return jnp.dot(both, codes, precision=HIGHEST, preferred_element_type=jnp.float32)


def update(part, proj, prod, p):
    n = prod.shape[0] // 2
    numer = jnp.maximum(proj, 0.0) + prod[p * 8 : p * 8 + 8]
    denom = jnp.maximum(jnp.maximum(-proj, 0.0) + prod[n + p * 8 : n + p * 8 + 8], floor_value)
    return part * jnp.sqrt(numer / denom)


def part_list(halftiles):
    size = (halftiles - 1) * COMP // 2
    return ((0, size, "xy"), (size, size, "xy"), (2 * size, COMP, "yx"))


def kernel(
    acts_in, dic_in, codes_in, out_t, dict_out,
    acts, dic, codes, loaded, dt, ct, proj, gram, gram_in, gram_tiles, mid,
    gk, gk_c, gk_x, gk_y, gk_z, ginv,
    cr, cr_c, full, *rest,
):
    tok, z = lax.axis_index("tok"), lax.axis_index("hid")
    core, x, y = lax.rem(tok, 2), lax.rem(tok // 2, XS), tok // (2 * XS)

    def at(dx=0, dy=0, dz=0, dc=0):
        px, py = lax.rem(x + dx, XS), lax.rem(y + dy, YS)
        return ((py * XS + px) * 2 + lax.rem(core + dc, 2), lax.rem(z + dz, ZS))

    zorder = (4, 3, 5, 2, 6, 1, 7)
    xorder = (2, 1, 3)

    in1, sum1, in2, rest = rest[:3], rest[3:6], rest[6:9], rest[9:]
    (proj2, gram2, gram2_in, gram2_tiles), rest = rest[:4], rest[4:]
    bufs, bufs2, rest = rest[:5], rest[5:10], rest[10:]
    zs, zr, ds, dr, ys, yr, xs, xr, cs, crs = rest

    barrier = pltpu.get_barrier_semaphore()
    partners = [at(dz=o) for o in zorder] + [at(dy=o) for o in zorder] + [at(dx=o) for o in xorder] + [at(dc=1)]
    for p in partners:
        pl.semaphore_signal(barrier, inc=1, device_id=p, device_id_type=MESH)

    def push(src, dst, ss, rs, dev):
        c = pltpu.make_async_remote_copy(
            src_ref=src, dst_ref=dst, send_sem=ss, recv_sem=rs, device_id=dev, device_id_type=MESH
        )
        c.start()
        return c

    def rows(i, n):
        return pl.ds(pl.multiple_of(i * n, n), n)

    n = COMP // ZS

    pieces = n // 8
    ways = (1, -1)

    def chunk(owner, p, size=1):
        return pl.ds(pl.multiple_of(owner * n + p * 8, 8), size * 8)

    def scatter_z(part, bufs, phase):
        via1, via2, relay, fin1, fin2 = bufs
        held = {}
        for i, d in enumerate(ways):
            for p in range(pieces // 2):
                src = part.at[chunk(lax.rem(z + 4, ZS), p + i * (pieces // 2))]
                ss, rs = zs.at[phase, i, p], zr.at[phase, i, p]
                held["via2", i, p + i * (pieces // 2)] = push(src, via2.at[i, pl.ds(p * 8, 8)], ss, rs, at(dz=2 * d + ZS))
        for p in range(pieces):
            for i, d in enumerate(ways):
                src = part.at[chunk(lax.rem(z + 3 * d + ZS, ZS), p)]
                ss, rs = zs.at[phase, i, 2 + p], zr.at[phase, i, 2 + p]
                held["via1", i, p] = push(src, via1.at[i, pl.ds(p * 8, 8)], ss, rs, at(dz=d + ZS))
        for i, d in enumerate(ways):
            src = part.at[chunk(lax.rem(z + d + ZS, ZS), 0, pieces)]
            held["fin1", i] = push(src, fin1.at[i], zs.at[phase, i, 6], zr.at[phase, i, 6], at(dz=d + ZS))
        return held

    def relay_z(part, bufs, phase, held):
        via1, via2, relay, fin1, fin2 = bufs
        for p in range(pieces):
            for i, d in enumerate(ways):
                span = pl.ds(p * 8, 8)
                held["via1", i, p].wait_recv()
                total = part[chunk(lax.rem(z + 2 * d + ZS, ZS), p), :] + via1[i, span, :]
                if p // (pieces // 2) == i:
                    held["via2", i, p].wait_recv()
                    total += via2[i, pl.ds((p - i * (pieces // 2)) * 8, 8), :]
                relay[i, span, :] = total
                ss, rs = zs.at[phase, i, 7 + p], zr.at[phase, i, 7 + p]
                held["fin2", i, p] = push(relay.at[i, span], fin2.at[i, span], ss, rs, at(dz=2 * d + ZS))

    def summed_z(part, bufs, held, p):
        via1, via2, relay, fin1, fin2 = bufs
        span = pl.ds(p * 8, 8)
        total = part[chunk(z, p), :]
        for i in range(2):
            if p == 0:
                held["fin1", i].wait_recv()
            total += fin1[i, span, :]
        for i in range(2):
            held["fin2", i, p].wait_recv()
            total += fin2[i, span, :]
        return total

    def gather_z(buf, phase, held, p):
        spot = buf.at[chunk(z, p)]
        for j, hops in ((0, 2), (4, 1)):
            for i, d in enumerate(ways):
                dev = at(dz=hops * d + ZS)
                held[hops, i, p] = push(spot, spot, zs.at[phase, i, j + p], zr.at[phase, i, j + p], dev)

    def forward_z(buf, phase, held):
        for p in range(pieces):
            for i, d in enumerate(ways):
                held[2, i, p].wait_recv()
                spot = buf.at[chunk(lax.rem(z - 2 * d + ZS, ZS), p)]
                if p // (pieces // 2) == i:
                    q = 8 + p - i * (pieces // 2)
                    held[4, i, p] = push(spot, spot, zs.at[phase, i, q], zr.at[phase, i, q], at(dz=2 * d + ZS))
                held[3, i, p] = push(spot, spot, zs.at[phase, i, 10 + p], zr.at[phase, i, 10 + p], at(dz=d + ZS))

    def arrive_z(held, half):
        for (hops, i, p), c in held.items():
            if hops != 2 and p // (pieces // 2) == half:
                c.wait_recv()

    def send_gram(matrix, part, slots, sem):
        picked = [matrix[pl.ds(pl.multiple_of(j * n + x * 8, 8), 8), :] for j in range(ZS)]
        both = split2(jnp.concatenate(picked, axis=0))
        prod = lax.dot_general(both, split2(matrix[rows(core, 128), :]), NT, preferred_element_type=jnp.float32)
        m = 8 * ZS
        tile = prod[:m, :128] + (prod[:m, 128:] + prod[m:, :128] + prod[m:, 128:])
        part[...] = tile.reshape(part.shape)
        out = []
        for o in zorder:
            dev = at(dz=o)
            out.append(push(part.at[dev[1]], slots.at[o - 1], ds.at[sem, o - 1], dr.at[sem, o - 1], dev))
        return out

    def share_gram(sent, part, slots, tiles, step, _):
        finish(sent)
        spot = tiles.at[core, x]
        spot[...] = part[z] + sum(slots[i] for i in range(ZS - 1))
        return [push(spot, spot, xs.at[step, o - 1], xr.at[step, o - 1], at(dx=o)) for o in xorder]

    def whole_gram(sent, tiles, _, step):
        finish(sent)
        spot = tiles.at[core]
        push(spot, spot, cs.at[step], crs.at[step], at(dc=1)).wait()
        return jnp.concatenate([tiles[i].reshape(n, 128) for i in range(2)], axis=1)

    def finish(copies):
        for c in copies:
            c.wait()

    loads = [
        pltpu.make_async_copy(src, dst, loaded.at[i])
        for i, (src, dst) in enumerate(((dic_in, dic), (acts_in, acts), (codes_in, codes)))
    ]
    for c in loads:
        c.start()
    loads[0].wait()
    dt[...] = dic[...].T
    loads[1].wait()
    proj[...] = lax.dot_general(dt[...].astype(jnp.bfloat16), acts[...], NT, preferred_element_type=jnp.float32)
    pl.semaphore_wait(barrier, len(partners))
    sent_gram = send_gram(dt, gram, gram_in, 0)
    held = scatter_z(proj, bufs, 0)
    loads[2].wait()
    ct[...] = codes[...].T
    own = rows(z, n)
    sent_gram = share_gram(sent_gram, gram, gram_in, gram_tiles, 7, 8)
    relay_z(proj, bufs, 0, held)
    prod = gram_products(whole_gram(sent_gram, gram_tiles, 7, 8), ct[...])
    passed = {}
    for p in range(pieces):
        mid[chunk(z, p), :] = update(ct[chunk(z, p), :], summed_z(proj, bufs, held, p), prod, p)
        gather_z(mid, 1, passed, p)
    for c in held.values():
        c.wait_send()
    forward_z(mid, 1, passed)
    arrive_z(passed, 0)

    halftiles = acts.shape[1] // 256
    parts = part_list(halftiles)

    def low_half(half):
        return jnp.concatenate([mid[chunk(j, 2 * half, 2), :] for j in range(ZS)], axis=0).astype(jnp.bfloat16)

    def cross(which, p, codes_low):
        first = 0 if p < 2 else halftiles - 1
        count = halftiles - 1 if p < 2 else 1
        lanes = pl.ds(pl.multiple_of((which * halftiles + first) * 128, 128), count * 128)
        block = jnp.dot(codes_low, acts[:, lanes], preferred_element_type=jnp.float32)
        m = codes_low.shape[0]
        for j in range(count):
            cr[which, pl.ds(parts[p][0] + j * m, m), :] = block[:, j * 128 : j * 128 + 128]

    axes = {"x": (x, XS, xorder, xs, xr), "y": (y, YS, zorder, ys, yr)}

    def shares(p):
        base, size, order = parts[p]
        one, two = axes[order[0]], axes[order[1]]
        return base, size, one, two, size // one[1], size // one[1] // two[1]

    def span_of(base, i, size):
        return pl.ds(pl.multiple_of(base + i * size, size), size)

    def along(name, row, src_of, dst_of):
        me, count, order, ss, rs = axes[name]
        out = []
        for o in order:
            dev = at(dx=o) if name == "x" else at(dy=o)
            out.append(push(src_of(lax.rem(me + o, count)), dst_of(o), ss.at[row, o - 1], rs.at[row, o - 1], dev))
        return out

    def send_core(p):
        base, size, _, _, _, _ = shares(p)
        span = pl.ds(base, size)
        return [push(cr.at[1 - core, span], cr_c.at[span], cs.at[p], crs.at[p], at(dc=1))]

    def send_first(p, copies):
        finish(copies)
        base, size, one, two, n1, n2 = shares(p)
        span = pl.ds(base, size)
        cr_c[span, :] += cr[core, span, :]
        return along(parts[p][2][0], 2 * p, lambda i: cr_c.at[span_of(base, i, n1)], lambda o: in1[p].at[o - 1])

    def send_second(p, copies):
        finish(copies)
        base, size, one, two, n1, n2 = shares(p)
        sum1[p][...] = cr_c[span_of(base, one[0], n1), :] + sum(in1[p][i] for i in range(one[1] - 1))
        return along(parts[p][2][1], 2 * p, lambda i: sum1[p].at[span_of(0, i, n2)], lambda o: in2[p].at[o - 1])

    def gather_second(p, copies):
        finish(copies)
        base, size, one, two, n1, n2 = shares(p)
        spot = full.at[core, span_of(base, one[0] * two[1] + two[0], n2)]
        spot[...] = sum1[p][span_of(0, two[0], n2), :] + sum(in2[p][i] for i in range(two[1] - 1))
        return along(parts[p][2][1], 2 * p + 1, lambda i: spot, lambda o: spot)

    def gather_first(p, copies):
        finish(copies)
        base, size, one, two, n1, n2 = shares(p)
        spot = full.at[core, span_of(base, one[0], n1)]
        return along(parts[p][2][0], 2 * p + 1, lambda i: spot, lambda o: spot)

    def gather_core(p, copies):
        finish(copies)
        base, size, _, _, _, _ = shares(p)
        spot = full.at[core, pl.ds(base, size)]
        return [push(spot, spot, cs.at[3 + p], crs.at[3 + p], at(dc=1))]

    c = [None] * 3
    low0 = low_half(0)
    cross(1 - core, 0, low0)
    c[0] = send_core(0)
    cross(core, 0, low0)
    c[0] = send_first(0, c[0])
    arrive_z(passed, 1)

    low1 = low_half(1)
    low = jnp.concatenate([low0, low1], axis=0)
    low_own = mid[own, :].astype(jnp.bfloat16)
    gk[...] = lax.dot_general(low_own, low, NT, preferred_element_type=jnp.float32).reshape(gk.shape)
    g_c = push(gk.at[1 - core], gk_c, cs.at[6], crs.at[6], at(dc=1))
    cross(1 - core, 1, low1)
    c[1] = send_core(1)
    cross(1 - core, 2, low)
    c[2] = send_core(2)
    g_c.wait()
    gk_x[x] = gk[core] + gk_c[...]
    g_x = along("x", 6, lambda i: gk_x.at[x], lambda o: gk_x.at[x])
    cross(core, 1, low1)
    cross(core, 2, low)
    c[1] = send_first(1, c[1])
    finish(g_x)
    gk_y[y] = sum(gk_x[i] for i in range(XS))
    g_y = along("y", 6, lambda i: gk_y.at[y], lambda o: gk_y.at[y])
    c[2] = send_first(2, c[2])
    c[0] = send_second(0, c[0])
    c[1] = send_second(1, c[1])
    finish(g_y)
    spot = gk_z.at[core, z]
    spot[...] = sum(gk_y[i] for i in range(YS))
    g_z = [push(spot, spot, ds.at[2, o - 1], dr.at[2, o - 1], at(dz=o)) for o in zorder]
    c[2] = send_second(2, c[2])
    c[0] = gather_second(0, c[0])
    c[2] = gather_second(2, c[2])
    c[1] = gather_second(1, c[1])
    c[0] = gather_first(0, c[0])
    finish(g_z)
    spot = gk_z.at[core]
    g_c = push(spot, spot, cs.at[7], crs.at[7], at(dc=1))
    c[2] = gather_first(2, c[2])
    for copy in passed.values():
        copy.wait_send()
    g_c.wait()
    ginv[...] = gk_z[...].reshape(COMP, COMP)

    invert_blocks(ginv, 0, 3)
    c[1] = gather_first(1, c[1])
    invert_blocks(ginv, 3, 7)
    c[0] = gather_core(0, c[0])
    c[2] = gather_core(2, c[2])
    invert_blocks(ginv, 7, 13)
    c[1] = gather_core(1, c[1])
    invert_blocks(ginv, 13, 16)

    half = COMP // 2
    m = n // 2
    inverse = jnp.concatenate([ginv[i * half + j * m : i * half + j * m + m, :] for j in range(ZS) for i in range(2)], axis=0)

    def solve(tile_list):
        for j, spots in tile_list:
            pair = [jnp.concatenate([full[i, pl.ds(at0, half), :] for at0 in spots], axis=0) for i in range(2)]
            solved = jnp.dot(inverse, jnp.concatenate(pair, axis=1), precision=HIGHEST, preferred_element_type=jnp.float32)
            for i in range(2):
                dt[:, (i * halftiles + j) * 128 : (i * halftiles + j + 1) * 128] = solved[:, i * 128 : i * 128 + 128]

    finish(c[0])
    finish(c[2])
    solve([(halftiles - 1, (parts[2][0], parts[2][0] + half))])
    finish(c[1])
    solve([(j, (parts[0][0] + j * half, parts[1][0] + j * half)) for j in range(halftiles - 1)])
    sent_gram = send_gram(dt, gram2, gram2_in, 1)
    proj2[...] = lax.dot_general(dt[...].astype(jnp.bfloat16), acts[...], NT, preferred_element_type=jnp.float32)
    held = scatter_z(proj2, bufs2, 2)
    dict_out[...] = dt[...].T
    sent_gram = share_gram(sent_gram, gram2, gram2_in, gram2_tiles, 8, 9)
    relay_z(proj2, bufs2, 2, held)
    prod = gram_products(whole_gram(sent_gram, gram2_tiles, 8, 9), mid[...])
    passed = {}
    for p in range(pieces):
        out_t[chunk(z, p), :] = update(mid[chunk(z, p), :], summed_z(proj2, bufs2, held, p), prod, p)
        gather_z(out_t, 3, passed, p)
    for c in held.values():
        c.wait_send()
    forward_z(out_t, 3, passed)
    for half in range(2):
        arrive_z(passed, half)
    for c in passed.values():
        c.wait_send()


def leave(out_t, dict_in, codes_out, dict_out, held, sem):
    parts = 4
    step = dict_in.shape[0] // parts
    spots = [pl.ds(i * step, step) for i in range(parts)]
    copies = [pltpu.make_async_copy(dict_in.at[p], dict_out.at[p], sem.at[i]) for i, p in enumerate(spots)]
    for c in copies:
        c.start()
    held[...] = out_t[...].T
    copies.append(pltpu.make_async_copy(held, codes_out, sem.at[parts]))
    copies[-1].start()
    for c in copies:
        c.wait()


def per_device(acts, dictionary, codes):
    tokens, hid = acts.shape
    f32 = jnp.float32
    v = lambda *s: pltpu.VMEM(s, f32)
    n = COMP // ZS
    half = hid * COMP // 2 // 128
    count = {"x": XS, "y": YS}
    shapes = [(size, count[order[0]], count[order[1]]) for _, size, order in part_list(hid // 256)]
    sums = (v(2, n, tokens), v(2, n // 2, tokens), v(2, n, tokens), v(2, n, tokens), v(2, n, tokens))
    vmem = pl.BlockSpec(memory_space=pltpu.VMEM)
    anywhere = pl.BlockSpec(memory_space=pl.ANY)
    dma = pltpu.SemaphoreType.DMA
    out_t, dict_new = pl.pallas_call(
        kernel,
        name="semi_nmf",
        out_shape=(pltpu.VMEM((COMP, tokens), f32), pltpu.VMEM((hid, COMP), f32)),
        in_specs=[anywhere] * 3,
        out_specs=(vmem, vmem),
        scratch_shapes=[
            pltpu.VMEM((tokens, hid), jnp.bfloat16), v(hid, COMP), v(tokens, COMP), dma((3,)),
            v(COMP, hid), v(COMP, tokens), v(COMP, tokens), v(ZS, 8, 128),
            v(ZS - 1, 8, 128), v(2, XS, 8, 128), v(COMP, tokens),
            v(2, n // 2, COMP), v(n // 2, COMP), v(XS, n // 2, COMP), v(YS, n // 2, COMP), v(2, ZS, n // 2, COMP),
            v(COMP, COMP),
            v(2, half, 128), v(half, 128), v(2, half, 128),
            *[v(one - 1, size // one, 128) for size, one, two in shapes],
            *[v(size // one, 128) for size, one, two in shapes],
            *[v(two - 1, size // one // two, 128) for size, one, two in shapes],
            v(COMP, tokens), v(ZS, 8, 128), v(ZS - 1, 8, 128), v(2, XS, 8, 128),
            *sums, *sums,
            dma((4, 2, 14)), dma((4, 2, 14)), dma((3, ZS - 1)), dma((3, ZS - 1)), dma((7, YS - 1)), dma((7, YS - 1)),
            dma((9, XS - 1)), dma((9, XS - 1)), dma((10,)), dma((10,)),
        ],
        compiler_params=pltpu.CompilerParams(
            collective_id=0, has_side_effects=True, vmem_limit_bytes=56 * 1024 * 1024
        ),
    )(acts, dictionary, codes)
    return pl.pallas_call(
        leave,
        name="leave",
        out_shape=(jax.ShapeDtypeStruct((tokens, COMP), f32), jax.ShapeDtypeStruct((hid, COMP), f32)),
        in_specs=[vmem] * 2,
        out_specs=(anywhere, anywhere),
        scratch_shapes=[v(tokens, COMP), dma((5,))],
        compiler_params=pltpu.CompilerParams(vmem_limit_bytes=16 * 1024 * 1024),
    )(out_t, dict_new)


def solution(mesh):
    return jax.shard_map(
        per_device,
        mesh=mesh,
        in_specs=(P("tok", "hid"), P("hid", None), P("tok", None)),
        out_specs=(P("tok", None), P("hid", None)),
        check_vma=False,
    )
```

```python
import functools

import jax
import jax.numpy as jnp
from jax import lax
from jax.experimental import pallas as pl
from jax.experimental.pallas import tpu as pltpu
from jax.sharding import PartitionSpec as P

MESH = pl.DeviceIdType.MESH
HIGHEST = lax.Precision.HIGHEST
floor_value = 0.05
XS, YS, ZS = 4, 8, 8
COMP = 256
BLOCK = 16
TN = (((0,), (0,)), ((), ()))
NT = (((1,), (1,)), ((), ()))


def split3(v):
    hi = v.astype(jnp.bfloat16)
    rest = v - hi.astype(jnp.float32)
    mid = rest.astype(jnp.bfloat16)
    low = (rest - mid.astype(jnp.float32)).astype(jnp.bfloat16)
    return hi, mid, low


def split2(v):
    hi = v.astype(jnp.bfloat16)
    return jnp.concatenate([hi, (v - hi.astype(jnp.float32)).astype(jnp.bfloat16)], axis=0)


def outer6(c, y):
    ch, cm, cl = split3(c)
    yh, ym, yl = split3(y)
    lhs = jnp.concatenate([ch, ch, cm, cm, ch, cl], axis=0)
    rhs = jnp.concatenate([yh, ym, yh, ym, yl, yh], axis=0)
    return lax.dot_general(lhs, rhs, TN, preferred_element_type=jnp.float32)


def panel_invert(panel, k):
    size = panel.shape[1]
    tile = jnp.where(k < 128 // BLOCK, panel[:, :128], panel[:, 128:])
    tile = pltpu.roll(tile, lax.rem(128 - lax.rem(k * BLOCK, 128), 128), 1)
    cols = [jnp.broadcast_to(tile[:, j : j + 1], (BLOCK, 128)) for j in range(BLOCK)]
    row = lax.broadcasted_iota(jnp.int32, (BLOCK, 128), 0)
    lane = lax.broadcasted_iota(jnp.int32, (BLOCK, size), 1) - k * BLOCK
    wide_row = lax.broadcasted_iota(jnp.int32, (BLOCK, size), 0)
    for i in range(BLOCK):
        scaled = jnp.where(row == i, -1.0, cols[i]) * (1.0 / cols[i][i : i + 1, :])
        wide = jnp.concatenate([scaled] * (size // 128), axis=1)
        pivot = panel[i : i + 1, :]
        panel = jnp.where(lane == i, -wide, jnp.where(wide_row == i, 0.0, panel) - wide * pivot)
        for j in range(i + 1, BLOCK):
            c = cols[j][i : i + 1, :]
            cols[j] = jnp.where(row == i, 0.0, cols[j]) - scaled * c
    return panel


def invert_blocks(a, first, last):
    size = a.shape[0]

    def body(k, _):
        rows = pl.ds(pl.multiple_of(k * BLOCK, BLOCK), BLOCK)
        panel = a[rows, :]
        lane = lax.broadcasted_iota(jnp.int32, (1, size), 1)
        column = panel * jnp.where(lane < k * BLOCK, -1.0, 1.0)
        new = panel_invert(panel, k)
        inside = (lane >= k * BLOCK) & (lane < k * BLOCK + BLOCK)
        a[...] = jnp.where(inside, 0.0, a[...]) - outer6(column, new)
        a[rows, :] = new
        return 0

    lax.fori_loop(first, last, body, 0)


def gram_products(gram, codes):
    both = jnp.concatenate([jnp.maximum(-gram, 0.0), jnp.maximum(gram, 0.0)], axis=0)
    return jnp.dot(both, codes, precision=HIGHEST, preferred_element_type=jnp.float32)


def update(part, proj, prod, p):
    n = prod.shape[0] // 2
    numer = jnp.maximum(proj, 0.0) + prod[p * 8 : p * 8 + 8]
    denom = jnp.maximum(jnp.maximum(-proj, 0.0) + prod[n + p * 8 : n + p * 8 + 8], floor_value)
    return part * jnp.sqrt(numer / denom)


def part_list(halftiles):
    third = halftiles // 3
    return (
        (0, third, "xy"), (third, third, "xy"), (2 * third, third, "xy"), (3 * third, halftiles - 3 * third, "yx"),
    )


def kernel(
    acts_in, dic_in, codes_in, out_t, dict_out,
    acts, dic, codes, loaded, dt, ct, proj, gram, gram_in, gram_tiles, mid,
    gk, gk_c, gk_x, gk_y, gk_z, ginv,
    cr, cr_c, full, *rest,
):
    tok, z = lax.axis_index("tok"), lax.axis_index("hid")
    core, x, y = lax.rem(tok, 2), lax.rem(tok // 2, XS), tok // (2 * XS)

    def at(dx=0, dy=0, dz=0, dc=0):
        px, py = lax.rem(x + dx, XS), lax.rem(y + dy, YS)
        return ((py * XS + px) * 2 + lax.rem(core + dc, 2), lax.rem(z + dz, ZS))

    zorder = (4, 3, 5, 2, 6, 1, 7)
    xorder = (2, 1, 3)

    in1, sum1, in2, rest = rest[:4], rest[4:8], rest[8:12], rest[12:]
    (proj2, gram2, gram2_in, gram2_tiles), rest = rest[:4], rest[4:]
    bufs, bufs2, rest = rest[:5], rest[5:10], rest[10:]
    zs, zr, ds, dr, ys, yr, xs, xr, cs, crs = rest

    barrier = pltpu.get_barrier_semaphore()
    partners = [at(dz=o) for o in zorder] + [at(dy=o) for o in zorder] + [at(dx=o) for o in xorder] + [at(dc=1)]
    for p in partners:
        pl.semaphore_signal(barrier, inc=1, device_id=p, device_id_type=MESH)

    def push(src, dst, ss, rs, dev):
        c = pltpu.make_async_remote_copy(
            src_ref=src, dst_ref=dst, send_sem=ss, recv_sem=rs, device_id=dev, device_id_type=MESH
        )
        c.start()
        return c

    def rows(i, n):
        return pl.ds(pl.multiple_of(i * n, n), n)

    n = COMP // ZS

    pieces = n // 8
    ways = (1, -1)

    def chunk(owner, p, size=1):
        return pl.ds(pl.multiple_of(owner * n + p * 8, 8), size * 8)

    def scatter_z(part, bufs, phase):
        via1, via2, relay, fin1, fin2 = bufs
        held = {}
        for i, d in enumerate(ways):
            for p in range(pieces // 2):
                src = part.at[chunk(lax.rem(z + 4, ZS), p + i * (pieces // 2))]
                ss, rs = zs.at[phase, i, p], zr.at[phase, i, p]
                held["via2", i, p + i * (pieces // 2)] = push(src, via2.at[i, pl.ds(p * 8, 8)], ss, rs, at(dz=2 * d + ZS))
        for p in range(pieces):
            for i, d in enumerate(ways):
                src = part.at[chunk(lax.rem(z + 3 * d + ZS, ZS), p)]
                ss, rs = zs.at[phase, i, 2 + p], zr.at[phase, i, 2 + p]
                held["via1", i, p] = push(src, via1.at[i, pl.ds(p * 8, 8)], ss, rs, at(dz=d + ZS))
        for i, d in enumerate(ways):
            src = part.at[chunk(lax.rem(z + d + ZS, ZS), 0, pieces)]
            held["fin1", i] = push(src, fin1.at[i], zs.at[phase, i, 6], zr.at[phase, i, 6], at(dz=d + ZS))
        return held

    def relay_z(part, bufs, phase, held):
        via1, via2, relay, fin1, fin2 = bufs
        for p in range(pieces):
            for i, d in enumerate(ways):
                span = pl.ds(p * 8, 8)
                held["via1", i, p].wait_recv()
                total = part[chunk(lax.rem(z + 2 * d + ZS, ZS), p), :] + via1[i, span, :]
                if p // (pieces // 2) == i:
                    held["via2", i, p].wait_recv()
                    total += via2[i, pl.ds((p - i * (pieces // 2)) * 8, 8), :]
                relay[i, span, :] = total
                ss, rs = zs.at[phase, i, 7 + p], zr.at[phase, i, 7 + p]
                held["fin2", i, p] = push(relay.at[i, span], fin2.at[i, span], ss, rs, at(dz=2 * d + ZS))

    def summed_z(part, bufs, held, p):
        via1, via2, relay, fin1, fin2 = bufs
        span = pl.ds(p * 8, 8)
        total = part[chunk(z, p), :]
        for i in range(2):
            if p == 0:
                held["fin1", i].wait_recv()
            total += fin1[i, span, :]
        for i in range(2):
            held["fin2", i, p].wait_recv()
            total += fin2[i, span, :]
        return total

    def gather_z(buf, phase, held, p):
        spot = buf.at[chunk(z, p)]
        for j, hops in ((0, 2), (4, 1)):
            for i, d in enumerate(ways):
                dev = at(dz=hops * d + ZS)
                held[hops, i, p] = push(spot, spot, zs.at[phase, i, j + p], zr.at[phase, i, j + p], dev)

    def forward_z(buf, phase, held):
        for p in range(pieces):
            for i, d in enumerate(ways):
                held[2, i, p].wait_recv()
                spot = buf.at[chunk(lax.rem(z - 2 * d + ZS, ZS), p)]
                if p // (pieces // 2) == i:
                    q = 8 + p - i * (pieces // 2)
                    held[4, i, p] = push(spot, spot, zs.at[phase, i, q], zr.at[phase, i, q], at(dz=2 * d + ZS))
                held[3, i, p] = push(spot, spot, zs.at[phase, i, 10 + p], zr.at[phase, i, 10 + p], at(dz=d + ZS))
        for key, c in held.items():
            c.wait_send()
            if key[0] != 2:
                c.wait_recv()

    def send_gram(matrix, part, slots, sem):
        picked = [matrix[pl.ds(pl.multiple_of(j * n + x * 8, 8), 8), :] for j in range(ZS)]
        both = split2(jnp.concatenate(picked, axis=0))
        prod = lax.dot_general(both, split2(matrix[rows(core, 128), :]), NT, preferred_element_type=jnp.float32)
        m = 8 * ZS
        tile = prod[:m, :128] + (prod[:m, 128:] + prod[m:, :128] + prod[m:, 128:])
        part[...] = tile.reshape(part.shape)
        out = []
        for o in zorder:
            dev = at(dz=o)
            out.append(push(part.at[dev[1]], slots.at[o - 1], ds.at[sem, o - 1], dr.at[sem, o - 1], dev))
        return out

    def share_gram(sent, part, slots, tiles, step, _):
        finish(sent)
        spot = tiles.at[core, x]
        spot[...] = part[z] + sum(slots[i] for i in range(ZS - 1))
        return [push(spot, spot, xs.at[step, o - 1], xr.at[step, o - 1], at(dx=o)) for o in xorder]

    def whole_gram(sent, tiles, _, step):
        finish(sent)
        spot = tiles.at[core]
        push(spot, spot, cs.at[step], crs.at[step], at(dc=1)).wait()
        return jnp.concatenate([tiles[i].reshape(n, 128) for i in range(2)], axis=1)

    def finish(copies):
        for c in copies:
            c.wait()

    loads = [
        pltpu.make_async_copy(src, dst, loaded.at[i])
        for i, (src, dst) in enumerate(((dic_in, dic), (acts_in, acts), (codes_in, codes)))
    ]
    for c in loads:
        c.start()
    loads[0].wait()
    dt[...] = dic[...].T
    loads[1].wait()
    proj[...] = lax.dot_general(dt[...].astype(jnp.bfloat16), acts[...], NT, preferred_element_type=jnp.float32)
    pl.semaphore_wait(barrier, len(partners))
    sent_gram = send_gram(dt, gram, gram_in, 0)
    held = scatter_z(proj, bufs, 0)
    loads[2].wait()
    ct[...] = codes[...].T
    own = rows(z, n)
    sent_gram = share_gram(sent_gram, gram, gram_in, gram_tiles, 9, 10)
    relay_z(proj, bufs, 0, held)
    prod = gram_products(whole_gram(sent_gram, gram_tiles, 9, 10), ct[...])
    passed = {}
    for p in range(pieces):
        mid[chunk(z, p), :] = update(ct[chunk(z, p), :], summed_z(proj, bufs, held, p), prod, p)
        gather_z(mid, 1, passed, p)
    for c in held.values():
        c.wait_send()
    forward_z(mid, 1, passed)

    low = mid[...].astype(jnp.bfloat16)
    low_own = mid[own, :].astype(jnp.bfloat16)
    gk[...] = lax.dot_general(low_own, low, NT, preferred_element_type=jnp.float32).reshape(gk.shape)
    g_c = push(gk.at[1 - core], gk_c, cs.at[8], crs.at[8], at(dc=1))

    halftiles = acts.shape[1] // 256
    parts = part_list(halftiles)

    def cross(which, p):
        first, count, _ = parts[p]
        lanes = pl.ds(pl.multiple_of((which * halftiles + first) * 128, 128), count * 128)
        block = jnp.dot(low, acts[:, lanes], preferred_element_type=jnp.float32)
        for j in range(count):
            cr[which, pl.ds((first + j) * COMP, COMP), :] = block[:, j * 128 : j * 128 + 128]

    axes = {"x": (x, XS, xorder, xs, xr), "y": (y, YS, zorder, ys, yr)}

    def shares(p):
        first, count, order = parts[p]
        one, two = axes[order[0]], axes[order[1]]
        size = count * COMP
        return first * COMP, size, one, two, size // one[1], size // one[1] // two[1]

    def span_of(base, i, size):
        return pl.ds(pl.multiple_of(base + i * size, size), size)

    def along(name, row, src_of, dst_of):
        me, count, order, ss, rs = axes[name]
        out = []
        for o in order:
            dev = at(dx=o) if name == "x" else at(dy=o)
            out.append(push(src_of(lax.rem(me + o, count)), dst_of(o), ss.at[row, o - 1], rs.at[row, o - 1], dev))
        return out

    def send_core(p):
        base, size, _, _, _, _ = shares(p)
        span = pl.ds(base, size)
        return [push(cr.at[1 - core, span], cr_c.at[span], cs.at[p], crs.at[p], at(dc=1))]

    def send_first(p, copies):
        finish(copies)
        base, size, one, two, n1, n2 = shares(p)
        span = pl.ds(base, size)
        cr_c[span, :] += cr[core, span, :]
        return along(parts[p][2][0], 2 * p, lambda i: cr_c.at[span_of(base, i, n1)], lambda o: in1[p].at[o - 1])

    def send_second(p, copies):
        finish(copies)
        base, size, one, two, n1, n2 = shares(p)
        sum1[p][...] = cr_c[span_of(base, one[0], n1), :] + sum(in1[p][i] for i in range(one[1] - 1))
        return along(parts[p][2][1], 2 * p, lambda i: sum1[p].at[span_of(0, i, n2)], lambda o: in2[p].at[o - 1])

    def gather_second(p, copies):
        finish(copies)
        base, size, one, two, n1, n2 = shares(p)
        spot = full.at[core, span_of(base, one[0] * two[1] + two[0], n2)]
        spot[...] = sum1[p][span_of(0, two[0], n2), :] + sum(in2[p][i] for i in range(two[1] - 1))
        return along(parts[p][2][1], 2 * p + 1, lambda i: spot, lambda o: spot)

    def gather_first(p, copies):
        finish(copies)
        base, size, one, two, n1, n2 = shares(p)
        spot = full.at[core, span_of(base, one[0], n1)]
        return along(parts[p][2][0], 2 * p + 1, lambda i: spot, lambda o: spot)

    def gather_core(p, copies):
        finish(copies)
        base, size, _, _, _, _ = shares(p)
        spot = full.at[core, pl.ds(base, size)]
        return [push(spot, spot, cs.at[4 + p], crs.at[4 + p], at(dc=1))]

    c = [None] * 4
    for p in range(4):
        cross(1 - core, p)
        c[p] = send_core(p)
    g_c.wait()
    gk_x[x] = gk[core] + gk_c[...]
    g_x = along("x", 8, lambda i: gk_x.at[x], lambda o: gk_x.at[x])
    for p in range(4):
        cross(core, p)
    c[0] = send_first(0, c[0])
    c[1] = send_first(1, c[1])
    c[2] = send_first(2, c[2])
    finish(g_x)
    gk_y[y] = sum(gk_x[i] for i in range(XS))
    g_y = along("y", 8, lambda i: gk_y.at[y], lambda o: gk_y.at[y])
    c[3] = send_first(3, c[3])
    c[0] = send_second(0, c[0])
    c[1] = send_second(1, c[1])
    finish(g_y)
    spot = gk_z.at[z, core]
    spot[...] = sum(gk_y[i] for i in range(YS))
    g_z = [push(spot, spot, ds.at[2, o - 1], dr.at[2, o - 1], at(dz=o)) for o in zorder]
    c[2] = send_second(2, c[2])
    c[0] = gather_second(0, c[0])
    c[3] = send_second(3, c[3])
    c[1] = gather_second(1, c[1])
    c[2] = gather_second(2, c[2])
    c[3] = gather_second(3, c[3])
    finish(g_z)
    spot = gk_z.at[:, core]
    g_c = push(spot, spot, cs.at[9], crs.at[9], at(dc=1))
    c[0] = gather_first(0, c[0])
    g_c.wait()
    ginv[...] = gk_z[...].reshape(COMP, COMP)

    invert_blocks(ginv, 0, 2)
    c[1] = gather_first(1, c[1])
    c[3] = gather_first(3, c[3])
    invert_blocks(ginv, 2, 5)
    c[2] = gather_first(2, c[2])
    invert_blocks(ginv, 5, 7)
    c[0] = gather_core(0, c[0])
    invert_blocks(ginv, 7, 11)
    c[1] = gather_core(1, c[1])
    invert_blocks(ginv, 11, 14)
    c[3] = gather_core(3, c[3])
    c[2] = gather_core(2, c[2])
    invert_blocks(ginv, 14, 16)

    def solve(first, last):
        for j in range(first, last):
            span = pl.ds(j * COMP, COMP)
            block = jnp.concatenate([full[0, span, :], full[1, span, :]], axis=1)
            solved = jnp.dot(ginv[...], block, precision=HIGHEST, preferred_element_type=jnp.float32)
            for i in range(2):
                dt[:, (i * halftiles + j) * 128 : (i * halftiles + j + 1) * 128] = solved[:, i * 128 : i * 128 + 128]

    for p in (0, 1, 3, 2):
        finish(c[p])
        solve(parts[p][0], parts[p][0] + parts[p][1])
    sent_gram = send_gram(dt, gram2, gram2_in, 1)
    proj2[...] = lax.dot_general(dt[...].astype(jnp.bfloat16), acts[...], NT, preferred_element_type=jnp.float32)
    held = scatter_z(proj2, bufs2, 2)
    dict_out[...] = dt[...].T
    sent_gram = share_gram(sent_gram, gram2, gram2_in, gram2_tiles, 10, 11)
    relay_z(proj2, bufs2, 2, held)
    prod = gram_products(whole_gram(sent_gram, gram2_tiles, 10, 11), mid[...])
    passed = {}
    for p in range(pieces):
        out_t[chunk(z, p), :] = update(mid[chunk(z, p), :], summed_z(proj2, bufs2, held, p), prod, p)
        gather_z(out_t, 3, passed, p)
    for c in held.values():
        c.wait_send()
    forward_z(out_t, 3, passed)


def leave(out_t, dict_in, codes_out, dict_out, held, sem):
    parts = 4
    step = dict_in.shape[0] // parts
    spots = [pl.ds(i * step, step) for i in range(parts)]
    copies = [pltpu.make_async_copy(dict_in.at[p], dict_out.at[p], sem.at[i]) for i, p in enumerate(spots)]
    for c in copies:
        c.start()
    held[...] = out_t[...].T
    copies.append(pltpu.make_async_copy(held, codes_out, sem.at[parts]))
    copies[-1].start()
    for c in copies:
        c.wait()


def per_device(acts, dictionary, codes):
    tokens, hid = acts.shape
    f32 = jnp.float32
    v = lambda *s: pltpu.VMEM(s, f32)
    n = COMP // ZS
    half = hid * COMP // 2 // 128
    count = {"x": XS, "y": YS}
    shapes = [(k * COMP, count[order[0]], count[order[1]]) for _, k, order in part_list(hid // 256)]
    sums = (v(2, n, tokens), v(2, n // 2, tokens), v(2, n, tokens), v(2, n, tokens), v(2, n, tokens))
    vmem = pl.BlockSpec(memory_space=pltpu.VMEM)
    anywhere = pl.BlockSpec(memory_space=pl.ANY)
    dma = pltpu.SemaphoreType.DMA
    out_t, dict_new = pl.pallas_call(
        kernel,
        name="semi_nmf",
        out_shape=(pltpu.VMEM((COMP, tokens), f32), pltpu.VMEM((hid, COMP), f32)),
        in_specs=[anywhere] * 3,
        out_specs=(vmem, vmem),
        scratch_shapes=[
            pltpu.VMEM((tokens, hid), jnp.bfloat16), v(hid, COMP), v(tokens, COMP), dma((3,)),
            v(COMP, hid), v(COMP, tokens), v(COMP, tokens), v(ZS, 8, 128),
            v(ZS - 1, 8, 128), v(2, XS, 8, 128), v(COMP, tokens),
            v(2, n // 2, COMP), v(n // 2, COMP), v(XS, n // 2, COMP), v(YS, n // 2, COMP), v(ZS, 2, n // 2, COMP),
            v(COMP, COMP),
            v(2, half, 128), v(half, 128), v(2, half, 128),
            *[v(one - 1, size // one, 128) for size, one, two in shapes],
            *[v(size // one, 128) for size, one, two in shapes],
            *[v(two - 1, size // one // two, 128) for size, one, two in shapes],
            v(COMP, tokens), v(ZS, 8, 128), v(ZS - 1, 8, 128), v(2, XS, 8, 128),
            *sums, *sums,
            dma((4, 2, 14)), dma((4, 2, 14)), dma((3, ZS - 1)), dma((3, ZS - 1)), dma((9, YS - 1)), dma((9, YS - 1)),
            dma((11, XS - 1)), dma((11, XS - 1)), dma((12,)), dma((12,)),
        ],
        compiler_params=pltpu.CompilerParams(
            collective_id=0, has_side_effects=True, vmem_limit_bytes=56 * 1024 * 1024
        ),
    )(acts, dictionary, codes)
    return pl.pallas_call(
        leave,
        name="leave",
        out_shape=(jax.ShapeDtypeStruct((tokens, COMP), f32), jax.ShapeDtypeStruct((hid, COMP), f32)),
        in_specs=[vmem] * 2,
        out_specs=(anywhere, anywhere),
        scratch_shapes=[v(tokens, COMP), dma((5,))],
        compiler_params=pltpu.CompilerParams(vmem_limit_bytes=16 * 1024 * 1024),
    )(out_t, dict_new)


def solution(mesh):
    return jax.shard_map(
        per_device,
        mesh=mesh,
        in_specs=(P("tok", "hid"), P("hid", None), P("tok", None)),
        out_specs=(P("tok", None), P("hid", None)),
        check_vma=False,
    )
```

```python
import functools

import jax
import jax.numpy as jnp
from jax import lax
from jax.experimental import pallas as pl
from jax.experimental.pallas import tpu as pltpu
from jax.sharding import PartitionSpec as P

MESH = pl.DeviceIdType.MESH
HIGHEST = lax.Precision.HIGHEST
floor_value = 0.05
XS, YS, ZS = 4, 8, 8
COMP = 256
BLOCK = 16
TN = (((0,), (0,)), ((), ()))
NT = (((1,), (1,)), ((), ()))


def split3(v):
    hi = v.astype(jnp.bfloat16)
    rest = v - hi.astype(jnp.float32)
    mid = rest.astype(jnp.bfloat16)
    low = (rest - mid.astype(jnp.float32)).astype(jnp.bfloat16)
    return hi, mid, low


def split2(v):
    hi = v.astype(jnp.bfloat16)
    return jnp.concatenate([hi, (v - hi.astype(jnp.float32)).astype(jnp.bfloat16)], axis=0)


def outer6(c, y):
    ch, cm, cl = split3(c)
    yh, ym, yl = split3(y)
    lhs = jnp.concatenate([ch, ch, cm, cm, ch, cl], axis=0)
    rhs = jnp.concatenate([yh, ym, yh, ym, yl, yh], axis=0)
    return lax.dot_general(lhs, rhs, TN, preferred_element_type=jnp.float32)


def panel_invert(panel, k):
    size = panel.shape[1]
    tile = jnp.where(k < 128 // BLOCK, panel[:, :128], panel[:, 128:])
    tile = pltpu.roll(tile, lax.rem(128 - lax.rem(k * BLOCK, 128), 128), 1)
    cols = [jnp.broadcast_to(tile[:, j : j + 1], (BLOCK, 128)) for j in range(BLOCK)]
    row = lax.broadcasted_iota(jnp.int32, (BLOCK, 128), 0)
    lane = lax.broadcasted_iota(jnp.int32, (BLOCK, size), 1) - k * BLOCK
    wide_row = lax.broadcasted_iota(jnp.int32, (BLOCK, size), 0)
    for i in range(BLOCK):
        scaled = jnp.where(row == i, -1.0, cols[i]) * (1.0 / cols[i][i : i + 1, :])
        wide = jnp.concatenate([scaled] * (size // 128), axis=1)
        pivot = panel[i : i + 1, :]
        panel = jnp.where(lane == i, -wide, jnp.where(wide_row == i, 0.0, panel) - wide * pivot)
        for j in range(i + 1, BLOCK):
            c = cols[j][i : i + 1, :]
            cols[j] = jnp.where(row == i, 0.0, cols[j]) - scaled * c
    return panel


def invert_blocks(a, first, last):
    size = a.shape[0]

    def body(k, _):
        rows = pl.ds(pl.multiple_of(k * BLOCK, BLOCK), BLOCK)
        panel = a[rows, :]
        lane = lax.broadcasted_iota(jnp.int32, (1, size), 1)
        column = panel * jnp.where(lane < k * BLOCK, -1.0, 1.0)
        new = panel_invert(panel, k)
        inside = (lane >= k * BLOCK) & (lane < k * BLOCK + BLOCK)
        a[...] = jnp.where(inside, 0.0, a[...]) - outer6(column, new)
        a[rows, :] = new
        return 0

    lax.fori_loop(first, last, body, 0)


def gram_products(gram, codes):
    both = jnp.concatenate([jnp.maximum(-gram, 0.0), jnp.maximum(gram, 0.0)], axis=0)
    return jnp.dot(both, codes, precision=HIGHEST, preferred_element_type=jnp.float32)


def update(part, proj, prod, p):
    n = prod.shape[0] // 2
    numer = jnp.maximum(proj, 0.0) + prod[p * 8 : p * 8 + 8]
    denom = jnp.maximum(jnp.maximum(-proj, 0.0) + prod[n + p * 8 : n + p * 8 + 8], floor_value)
    return part * jnp.sqrt(numer / denom)


def part_list(halftiles):
    third = halftiles // 3
    return (
        (0, third, "xy"), (third, third, "xy"), (2 * third, third, "xy"), (3 * third, halftiles - 3 * third, "yx"),
    )


def kernel(
    acts_in, dic_in, codes_in, out_t, dict_out,
    acts, dic, codes, loaded, dt, ct, proj, gram, gram_in, gram_tiles, mid,
    gk, gk_c, gk_x, gk_y, gk_z, ginv,
    cr, cr_c, full, *rest,
):
    tok, z = lax.axis_index("tok"), lax.axis_index("hid")
    core, x, y = lax.rem(tok, 2), lax.rem(tok // 2, XS), tok // (2 * XS)

    def at(dx=0, dy=0, dz=0, dc=0):
        px, py = lax.rem(x + dx, XS), lax.rem(y + dy, YS)
        return ((py * XS + px) * 2 + lax.rem(core + dc, 2), lax.rem(z + dz, ZS))

    zorder = (4, 3, 5, 2, 6, 1, 7)
    xorder = (2, 1, 3)

    in1, sum1, in2, rest = rest[:4], rest[4:8], rest[8:12], rest[12:]
    (proj2, gram2, gram2_in, gram2_tiles), rest = rest[:4], rest[4:]
    bufs, bufs2, rest = rest[:5], rest[5:10], rest[10:]
    zs, zr, ds, dr, ys, yr, xs, xr, cs, crs = rest

    barrier = pltpu.get_barrier_semaphore()
    partners = [at(dz=o) for o in zorder] + [at(dy=o) for o in zorder] + [at(dx=o) for o in xorder] + [at(dc=1)]
    for p in partners:
        pl.semaphore_signal(barrier, inc=1, device_id=p, device_id_type=MESH)

    def push(src, dst, ss, rs, dev):
        c = pltpu.make_async_remote_copy(
            src_ref=src, dst_ref=dst, send_sem=ss, recv_sem=rs, device_id=dev, device_id_type=MESH
        )
        c.start()
        return c

    def rows(i, n):
        return pl.ds(pl.multiple_of(i * n, n), n)

    n = COMP // ZS

    pieces = n // 8
    ways = (1, -1)

    def chunk(owner, p, size=1):
        return pl.ds(pl.multiple_of(owner * n + p * 8, 8), size * 8)

    def scatter_z(part, bufs, phase):
        via1, via2, relay, fin1, fin2 = bufs
        held = {}
        for i, d in enumerate(ways):
            for p in range(pieces // 2):
                src = part.at[chunk(lax.rem(z + 4, ZS), p + i * (pieces // 2))]
                ss, rs = zs.at[phase, i, p], zr.at[phase, i, p]
                held["via2", i, p + i * (pieces // 2)] = push(src, via2.at[i, pl.ds(p * 8, 8)], ss, rs, at(dz=2 * d + ZS))
        for p in range(pieces):
            for i, d in enumerate(ways):
                src = part.at[chunk(lax.rem(z + 3 * d + ZS, ZS), p)]
                ss, rs = zs.at[phase, i, 2 + p], zr.at[phase, i, 2 + p]
                held["via1", i, p] = push(src, via1.at[i, pl.ds(p * 8, 8)], ss, rs, at(dz=d + ZS))
        for i, d in enumerate(ways):
            src = part.at[chunk(lax.rem(z + d + ZS, ZS), 0, pieces)]
            held["fin1", i] = push(src, fin1.at[i], zs.at[phase, i, 6], zr.at[phase, i, 6], at(dz=d + ZS))
        return held

    def relay_z(part, bufs, phase, held):
        via1, via2, relay, fin1, fin2 = bufs
        for p in range(pieces):
            for i, d in enumerate(ways):
                span = pl.ds(p * 8, 8)
                held["via1", i, p].wait_recv()
                total = part[chunk(lax.rem(z + 2 * d + ZS, ZS), p), :] + via1[i, span, :]
                if p // (pieces // 2) == i:
                    held["via2", i, p].wait_recv()
                    total += via2[i, pl.ds((p - i * (pieces // 2)) * 8, 8), :]
                relay[i, span, :] = total
                ss, rs = zs.at[phase, i, 7 + p], zr.at[phase, i, 7 + p]
                held["fin2", i, p] = push(relay.at[i, span], fin2.at[i, span], ss, rs, at(dz=2 * d + ZS))

    def summed_z(part, bufs, held, p):
        via1, via2, relay, fin1, fin2 = bufs
        span = pl.ds(p * 8, 8)
        total = part[chunk(z, p), :]
        for i in range(2):
            if p == 0:
                held["fin1", i].wait_recv()
            total += fin1[i, span, :]
        for i in range(2):
            held["fin2", i, p].wait_recv()
            total += fin2[i, span, :]
        return total

    def gather_z(buf, phase, held, p):
        spot = buf.at[chunk(z, p)]
        for j, hops in ((0, 2), (4, 1)):
            for i, d in enumerate(ways):
                dev = at(dz=hops * d + ZS)
                held[hops, i, p] = push(spot, spot, zs.at[phase, i, j + p], zr.at[phase, i, j + p], dev)

    def forward_z(buf, phase, held):
        for p in range(pieces):
            for i, d in enumerate(ways):
                held[2, i, p].wait_recv()
                spot = buf.at[chunk(lax.rem(z - 2 * d + ZS, ZS), p)]
                if p // (pieces // 2) == i:
                    q = 8 + p - i * (pieces // 2)
                    held[4, i, p] = push(spot, spot, zs.at[phase, i, q], zr.at[phase, i, q], at(dz=2 * d + ZS))
                held[3, i, p] = push(spot, spot, zs.at[phase, i, 10 + p], zr.at[phase, i, 10 + p], at(dz=d + ZS))
        for key, c in held.items():
            c.wait_send()
            if key[0] != 2:
                c.wait_recv()

    def make_gram(matrix, part):
        picked = [matrix[pl.ds(pl.multiple_of(j * n + x * 8, 8), 8), :] for j in range(ZS)]
        both = split2(jnp.concatenate(picked, axis=0))
        prod = lax.dot_general(both, split2(matrix[...]), NT, preferred_element_type=jnp.float32)
        m = 8 * ZS
        tile = prod[:m, :COMP] + (prod[:m, COMP:] + prod[m:, :COMP] + prod[m:, COMP:])
        part[...] = tile.reshape(part.shape)

    def send_gram(part, slots, sem):
        out = []
        for o in zorder:
            dev = at(dz=o)
            out.append(push(part.at[dev[1]], slots.at[o - 1], ds.at[sem, o - 1], dr.at[sem, o - 1], dev))
        return out

    def share_gram(sent, part, slots, tiles, step):
        finish(sent)
        spot = tiles.at[x]
        spot[...] = part[z] + sum(slots[i] for i in range(ZS - 1))
        return [push(spot, spot, xs.at[step, o - 1], xr.at[step, o - 1], at(dx=o)) for o in xorder]

    def whole_gram(sent, tiles):
        finish(sent)
        return tiles[...].reshape(n, COMP)

    def finish(copies):
        for c in copies:
            c.wait()

    loads = [
        pltpu.make_async_copy(src, dst, loaded.at[i])
        for i, (src, dst) in enumerate(((dic_in, dic), (acts_in, acts), (codes_in, codes)))
    ]
    for c in loads:
        c.start()
    loads[0].wait()
    dt[...] = dic[...].T
    make_gram(dt, gram)
    loads[1].wait()
    proj[...] = lax.dot_general(dt[...].astype(jnp.bfloat16), acts[...], NT, preferred_element_type=jnp.float32)
    pl.semaphore_wait(barrier, len(partners))
    sent_gram = send_gram(gram, gram_in, 0)
    held = scatter_z(proj, bufs, 0)
    loads[2].wait()
    ct[...] = codes[...].T
    own = rows(z, n)
    sent_gram = share_gram(sent_gram, gram, gram_in, gram_tiles, 9)
    relay_z(proj, bufs, 0, held)
    prod = gram_products(whole_gram(sent_gram, gram_tiles), ct[...])
    passed = {}
    for p in range(pieces):
        mid[chunk(z, p), :] = update(ct[chunk(z, p), :], summed_z(proj, bufs, held, p), prod, p)
        gather_z(mid, 1, passed, p)
    for c in held.values():
        c.wait_send()
    forward_z(mid, 1, passed)

    low = mid[...].astype(jnp.bfloat16)
    low_own = mid[own, :].astype(jnp.bfloat16)
    gk[...] = lax.dot_general(low_own, low, NT, preferred_element_type=jnp.float32).reshape(gk.shape)
    g_c = push(gk.at[1 - core], gk_c, cs.at[8], crs.at[8], at(dc=1))

    halftiles = acts.shape[1] // 256
    parts = part_list(halftiles)

    def cross(which, p):
        first, count, _ = parts[p]
        lanes = pl.ds(pl.multiple_of((which * halftiles + first) * 128, 128), count * 128)
        block = jnp.dot(low, acts[:, lanes], preferred_element_type=jnp.float32)
        for j in range(count):
            cr[which, pl.ds((first + j) * COMP, COMP), :] = block[:, j * 128 : j * 128 + 128]

    axes = {"x": (x, XS, xorder, xs, xr), "y": (y, YS, zorder, ys, yr)}

    def shares(p):
        first, count, order = parts[p]
        one, two = axes[order[0]], axes[order[1]]
        size = count * COMP
        return first * COMP, size, one, two, size // one[1], size // one[1] // two[1]

    def span_of(base, i, size):
        return pl.ds(pl.multiple_of(base + i * size, size), size)

    def along(name, row, src_of, dst_of):
        me, count, order, ss, rs = axes[name]
        out = []
        for o in order:
            dev = at(dx=o) if name == "x" else at(dy=o)
            out.append(push(src_of(lax.rem(me + o, count)), dst_of(o), ss.at[row, o - 1], rs.at[row, o - 1], dev))
        return out

    def send_core(p):
        base, size, _, _, _, _ = shares(p)
        span = pl.ds(base, size)
        return [push(cr.at[1 - core, span], cr_c.at[span], cs.at[p], crs.at[p], at(dc=1))]

    def send_first(p, copies):
        finish(copies)
        base, size, one, two, n1, n2 = shares(p)
        span = pl.ds(base, size)
        cr_c[span, :] += cr[core, span, :]
        return along(parts[p][2][0], 2 * p, lambda i: cr_c.at[span_of(base, i, n1)], lambda o: in1[p].at[o - 1])

    def send_second(p, copies):
        finish(copies)
        base, size, one, two, n1, n2 = shares(p)
        sum1[p][...] = cr_c[span_of(base, one[0], n1), :] + sum(in1[p][i] for i in range(one[1] - 1))
        return along(parts[p][2][1], 2 * p, lambda i: sum1[p].at[span_of(0, i, n2)], lambda o: in2[p].at[o - 1])

    def gather_second(p, copies):
        finish(copies)
        base, size, one, two, n1, n2 = shares(p)
        spot = full.at[core, span_of(base, one[0] * two[1] + two[0], n2)]
        spot[...] = sum1[p][span_of(0, two[0], n2), :] + sum(in2[p][i] for i in range(two[1] - 1))
        return along(parts[p][2][1], 2 * p + 1, lambda i: spot, lambda o: spot)

    def gather_first(p, copies):
        finish(copies)
        base, size, one, two, n1, n2 = shares(p)
        spot = full.at[core, span_of(base, one[0], n1)]
        return along(parts[p][2][0], 2 * p + 1, lambda i: spot, lambda o: spot)

    def gather_core(p, copies):
        finish(copies)
        base, size, _, _, _, _ = shares(p)
        spot = full.at[core, pl.ds(base, size)]
        return [push(spot, spot, cs.at[4 + p], crs.at[4 + p], at(dc=1))]

    c = [None] * 4
    for p in range(4):
        cross(1 - core, p)
        c[p] = send_core(p)
    g_c.wait()
    gk_x[x] = gk[core] + gk_c[...]
    g_x = along("x", 8, lambda i: gk_x.at[x], lambda o: gk_x.at[x])
    for p in range(4):
        cross(core, p)
    c[0] = send_first(0, c[0])
    c[1] = send_first(1, c[1])
    c[2] = send_first(2, c[2])
    finish(g_x)
    gk_y[y] = sum(gk_x[i] for i in range(XS))
    g_y = along("y", 8, lambda i: gk_y.at[y], lambda o: gk_y.at[y])
    c[3] = send_first(3, c[3])
    c[0] = send_second(0, c[0])
    c[1] = send_second(1, c[1])
    finish(g_y)
    spot = gk_z.at[z, core]
    spot[...] = sum(gk_y[i] for i in range(YS))
    g_z = [push(spot, spot, ds.at[2, o - 1], dr.at[2, o - 1], at(dz=o)) for o in zorder]
    c[2] = send_second(2, c[2])
    c[0] = gather_second(0, c[0])
    c[3] = send_second(3, c[3])
    c[1] = gather_second(1, c[1])
    c[2] = gather_second(2, c[2])
    c[3] = gather_second(3, c[3])
    finish(g_z)
    spot = gk_z.at[:, core]
    g_c = push(spot, spot, cs.at[9], crs.at[9], at(dc=1))
    c[0] = gather_first(0, c[0])
    g_c.wait()
    ginv[...] = gk_z[...].reshape(COMP, COMP)

    invert_blocks(ginv, 0, 2)
    c[1] = gather_first(1, c[1])
    c[3] = gather_first(3, c[3])
    invert_blocks(ginv, 2, 5)
    c[2] = gather_first(2, c[2])
    invert_blocks(ginv, 5, 7)
    c[0] = gather_core(0, c[0])
    invert_blocks(ginv, 7, 11)
    c[1] = gather_core(1, c[1])
    invert_blocks(ginv, 11, 14)
    c[3] = gather_core(3, c[3])
    c[2] = gather_core(2, c[2])
    invert_blocks(ginv, 14, 16)

    def solve(first, last):
        for j in range(first, last):
            span = pl.ds(j * COMP, COMP)
            block = jnp.concatenate([full[0, span, :], full[1, span, :]], axis=1)
            solved = jnp.dot(ginv[...], block, precision=HIGHEST, preferred_element_type=jnp.float32)
            for i in range(2):
                dt[:, (i * halftiles + j) * 128 : (i * halftiles + j + 1) * 128] = solved[:, i * 128 : i * 128 + 128]

    for p in (0, 1, 3, 2):
        finish(c[p])
        solve(parts[p][0], parts[p][0] + parts[p][1])
    make_gram(dt, gram2)
    sent_gram = send_gram(gram2, gram2_in, 1)
    proj2[...] = lax.dot_general(dt[...].astype(jnp.bfloat16), acts[...], NT, preferred_element_type=jnp.float32)
    held = scatter_z(proj2, bufs2, 2)
    dict_out[...] = dt[...].T
    sent_gram = share_gram(sent_gram, gram2, gram2_in, gram2_tiles, 10)
    relay_z(proj2, bufs2, 2, held)
    prod = gram_products(whole_gram(sent_gram, gram2_tiles), mid[...])
    passed = {}
    for p in range(pieces):
        out_t[chunk(z, p), :] = update(mid[chunk(z, p), :], summed_z(proj2, bufs2, held, p), prod, p)
        gather_z(out_t, 3, passed, p)
    for c in held.values():
        c.wait_send()
    forward_z(out_t, 3, passed)


def leave(out_t, dict_in, codes_out, dict_out, held, sem):
    parts = 4
    step = dict_in.shape[0] // parts
    spots = [pl.ds(i * step, step) for i in range(parts)]
    copies = [pltpu.make_async_copy(dict_in.at[p], dict_out.at[p], sem.at[i]) for i, p in enumerate(spots)]
    for c in copies:
        c.start()
    held[...] = out_t[...].T
    copies.append(pltpu.make_async_copy(held, codes_out, sem.at[parts]))
    copies[-1].start()
    for c in copies:
        c.wait()


def per_device(acts, dictionary, codes):
    tokens, hid = acts.shape
    f32 = jnp.float32
    v = lambda *s: pltpu.VMEM(s, f32)
    n = COMP // ZS
    half = hid * COMP // 2 // 128
    count = {"x": XS, "y": YS}
    shapes = [(k * COMP, count[order[0]], count[order[1]]) for _, k, order in part_list(hid // 256)]
    sums = (v(2, n, tokens), v(2, n // 2, tokens), v(2, n, tokens), v(2, n, tokens), v(2, n, tokens))
    vmem = pl.BlockSpec(memory_space=pltpu.VMEM)
    anywhere = pl.BlockSpec(memory_space=pl.ANY)
    dma = pltpu.SemaphoreType.DMA
    out_t, dict_new = pl.pallas_call(
        kernel,
        name="semi_nmf",
        out_shape=(pltpu.VMEM((COMP, tokens), f32), pltpu.VMEM((hid, COMP), f32)),
        in_specs=[anywhere] * 3,
        out_specs=(vmem, vmem),
        scratch_shapes=[
            pltpu.VMEM((tokens, hid), jnp.bfloat16), v(hid, COMP), v(tokens, COMP), dma((3,)),
            v(COMP, hid), v(COMP, tokens), v(COMP, tokens), v(ZS, 8, COMP),
            v(ZS - 1, 8, COMP), v(XS, 8, COMP), v(COMP, tokens),
            v(2, n // 2, COMP), v(n // 2, COMP), v(XS, n // 2, COMP), v(YS, n // 2, COMP), v(ZS, 2, n // 2, COMP),
            v(COMP, COMP),
            v(2, half, 128), v(half, 128), v(2, half, 128),
            *[v(one - 1, size // one, 128) for size, one, two in shapes],
            *[v(size // one, 128) for size, one, two in shapes],
            *[v(two - 1, size // one // two, 128) for size, one, two in shapes],
            v(COMP, tokens), v(ZS, 8, COMP), v(ZS - 1, 8, COMP), v(XS, 8, COMP),
            *sums, *sums,
            dma((4, 2, 14)), dma((4, 2, 14)), dma((3, ZS - 1)), dma((3, ZS - 1)), dma((9, YS - 1)), dma((9, YS - 1)),
            dma((11, XS - 1)), dma((11, XS - 1)), dma((12,)), dma((12,)),
        ],
        compiler_params=pltpu.CompilerParams(
            collective_id=0, has_side_effects=True, vmem_limit_bytes=56 * 1024 * 1024
        ),
    )(acts, dictionary, codes)
    return pl.pallas_call(
        leave,
        name="leave",
        out_shape=(jax.ShapeDtypeStruct((tokens, COMP), f32), jax.ShapeDtypeStruct((hid, COMP), f32)),
        in_specs=[vmem] * 2,
        out_specs=(anywhere, anywhere),
        scratch_shapes=[v(tokens, COMP), dma((5,))],
        compiler_params=pltpu.CompilerParams(vmem_limit_bytes=16 * 1024 * 1024),
    )(out_t, dict_new)


def solution(mesh):
    return jax.shard_map(
        per_device,
        mesh=mesh,
        in_specs=(P("tok", "hid"), P("hid", None), P("tok", None)),
        out_specs=(P("tok", None), P("hid", None)),
        check_vma=False,
    )
```

```python
import functools

import jax
import jax.numpy as jnp
from jax import lax
from jax.experimental import pallas as pl
from jax.experimental.pallas import tpu as pltpu
from jax.sharding import PartitionSpec as P

MESH = pl.DeviceIdType.MESH
HIGHEST = lax.Precision.HIGHEST
floor_value = 0.05
XS, YS, ZS = 4, 8, 8
COMP = 256
BLOCK = 16
TN = (((0,), (0,)), ((), ()))
NT = (((1,), (1,)), ((), ()))


def split3(v):
    hi = v.astype(jnp.bfloat16)
    rest = v - hi.astype(jnp.float32)
    mid = rest.astype(jnp.bfloat16)
    low = (rest - mid.astype(jnp.float32)).astype(jnp.bfloat16)
    return hi, mid, low


def split2(v):
    hi = v.astype(jnp.bfloat16)
    return jnp.concatenate([hi, (v - hi.astype(jnp.float32)).astype(jnp.bfloat16)], axis=0)


def outer6(c, y):
    ch, cm, cl = split3(c)
    yh, ym, yl = split3(y)
    lhs = jnp.concatenate([ch, ch, cm, cm, ch, cl], axis=0)
    rhs = jnp.concatenate([yh, ym, yh, ym, yl, yh], axis=0)
    return lax.dot_general(lhs, rhs, TN, preferred_element_type=jnp.float32)


def panel_invert(panel, k):
    size = panel.shape[1]
    tile = jnp.where(k < 128 // BLOCK, panel[:, :128], panel[:, 128:])
    tile = pltpu.roll(tile, lax.rem(128 - lax.rem(k * BLOCK, 128), 128), 1)
    cols = [jnp.broadcast_to(tile[:, j : j + 1], (BLOCK, 128)) for j in range(BLOCK)]
    row = lax.broadcasted_iota(jnp.int32, (BLOCK, 128), 0)
    lane = lax.broadcasted_iota(jnp.int32, (BLOCK, size), 1) - k * BLOCK
    wide_row = lax.broadcasted_iota(jnp.int32, (BLOCK, size), 0)
    for i in range(BLOCK):
        scaled = jnp.where(row == i, -1.0, cols[i]) * (1.0 / cols[i][i : i + 1, :])
        wide = jnp.concatenate([scaled] * (size // 128), axis=1)
        pivot = panel[i : i + 1, :]
        panel = jnp.where(lane == i, -wide, jnp.where(wide_row == i, 0.0, panel) - wide * pivot)
        for j in range(i + 1, BLOCK):
            c = cols[j][i : i + 1, :]
            cols[j] = jnp.where(row == i, 0.0, cols[j]) - scaled * c
    return panel


def invert_blocks(a, first, last):
    size = a.shape[0]

    def body(k, _):
        rows = pl.ds(pl.multiple_of(k * BLOCK, BLOCK), BLOCK)
        panel = a[rows, :]
        lane = lax.broadcasted_iota(jnp.int32, (1, size), 1)
        column = panel * jnp.where(lane < k * BLOCK, -1.0, 1.0)
        new = panel_invert(panel, k)
        inside = (lane >= k * BLOCK) & (lane < k * BLOCK + BLOCK)
        a[...] = jnp.where(inside, 0.0, a[...]) - outer6(column, new)
        a[rows, :] = new
        return 0

    lax.fori_loop(first, last, body, 0)


def gram_products(gram, codes):
    both = split2(jnp.concatenate([jnp.maximum(-gram, 0.0), jnp.maximum(gram, 0.0)], axis=0))
    hi = codes.astype(jnp.bfloat16)
    low = (codes - hi.astype(jnp.float32)).astype(jnp.bfloat16)
    prod = jnp.dot(both, low, preferred_element_type=jnp.float32) + jnp.dot(both, hi, preferred_element_type=jnp.float32)
    m = 2 * gram.shape[0]
    return prod[:m] + prod[m:]


def update(part, proj, prod, p):
    n = prod.shape[0] // 2
    numer = jnp.maximum(proj, 0.0) + prod[p * 8 : p * 8 + 8]
    denom = jnp.maximum(jnp.maximum(-proj, 0.0) + prod[n + p * 8 : n + p * 8 + 8], floor_value)
    return part * jnp.sqrt(numer / denom)


def part_list(halftiles):
    third = halftiles // 3
    return (
        (0, third, "xy"), (third, third, "xy"), (2 * third, third, "xy"), (3 * third, halftiles - 3 * third, "yx"),
    )


def kernel(
    acts_in, dic_in, codes_in, out_t, dict_out,
    acts, dic, codes, loaded, dt, ct, proj, gram, gram_in, gram_tiles, mid,
    gk, gk_c, gk_x, gk_y, gk_z, ginv,
    cr, cr_c, full, *rest,
):
    tok, z = lax.axis_index("tok"), lax.axis_index("hid")
    core, x, y = lax.rem(tok, 2), lax.rem(tok // 2, XS), tok // (2 * XS)

    def at(dx=0, dy=0, dz=0, dc=0):
        px, py = lax.rem(x + dx, XS), lax.rem(y + dy, YS)
        return ((py * XS + px) * 2 + lax.rem(core + dc, 2), lax.rem(z + dz, ZS))

    zorder = (4, 3, 5, 2, 6, 1, 7)
    xorder = (2, 1, 3)

    in1, sum1, in2, rest = rest[:4], rest[4:8], rest[8:12], rest[12:]
    (proj2, gram2, gram2_in, gram2_tiles), rest = rest[:4], rest[4:]
    bufs, bufs2, rest = rest[:5], rest[5:10], rest[10:]
    zs, zr, ds, dr, ys, yr, xs, xr, cs, crs = rest

    barrier = pltpu.get_barrier_semaphore()
    partners = [at(dz=o) for o in zorder] + [at(dy=o) for o in zorder] + [at(dx=o) for o in xorder] + [at(dc=1)]
    for p in partners:
        pl.semaphore_signal(barrier, inc=1, device_id=p, device_id_type=MESH)

    def push(src, dst, ss, rs, dev):
        c = pltpu.make_async_remote_copy(
            src_ref=src, dst_ref=dst, send_sem=ss, recv_sem=rs, device_id=dev, device_id_type=MESH
        )
        c.start()
        return c

    def rows(i, n):
        return pl.ds(pl.multiple_of(i * n, n), n)

    n = COMP // ZS

    pieces = n // 8
    ways = (1, -1)

    def chunk(owner, p, size=1):
        return pl.ds(pl.multiple_of(owner * n + p * 8, 8), size * 8)

    def scatter_z(part, bufs, phase):
        via1, via2, relay, fin1, fin2 = bufs
        held = {}
        for i, d in enumerate(ways):
            for p in range(pieces // 2):
                src = part.at[chunk(lax.rem(z + 4, ZS), p + i * (pieces // 2))]
                ss, rs = zs.at[phase, i, p], zr.at[phase, i, p]
                held["via2", i, p + i * (pieces // 2)] = push(src, via2.at[i, pl.ds(p * 8, 8)], ss, rs, at(dz=2 * d + ZS))
        for p in range(pieces):
            for i, d in enumerate(ways):
                src = part.at[chunk(lax.rem(z + 3 * d + ZS, ZS), p)]
                ss, rs = zs.at[phase, i, 2 + p], zr.at[phase, i, 2 + p]
                held["via1", i, p] = push(src, via1.at[i, pl.ds(p * 8, 8)], ss, rs, at(dz=d + ZS))
        for i, d in enumerate(ways):
            src = part.at[chunk(lax.rem(z + d + ZS, ZS), 0, pieces)]
            held["fin1", i] = push(src, fin1.at[i], zs.at[phase, i, 6], zr.at[phase, i, 6], at(dz=d + ZS))
        return held

    def relay_z(part, bufs, phase, held):
        via1, via2, relay, fin1, fin2 = bufs
        for p in range(pieces):
            for i, d in enumerate(ways):
                span = pl.ds(p * 8, 8)
                held["via1", i, p].wait_recv()
                total = part[chunk(lax.rem(z + 2 * d + ZS, ZS), p), :] + via1[i, span, :]
                if p // (pieces // 2) == i:
                    held["via2", i, p].wait_recv()
                    total += via2[i, pl.ds((p - i * (pieces // 2)) * 8, 8), :]
                relay[i, span, :] = total
                ss, rs = zs.at[phase, i, 7 + p], zr.at[phase, i, 7 + p]
                held["fin2", i, p] = push(relay.at[i, span], fin2.at[i, span], ss, rs, at(dz=2 * d + ZS))

    def summed_z(part, bufs, held, p):
        via1, via2, relay, fin1, fin2 = bufs
        span = pl.ds(p * 8, 8)
        total = part[chunk(z, p), :]
        for i in range(2):
            if p == 0:
                held["fin1", i].wait_recv()
            total += fin1[i, span, :]
        for i in range(2):
            held["fin2", i, p].wait_recv()
            total += fin2[i, span, :]
        return total

    def gather_z(buf, phase, held, p):
        spot = buf.at[chunk(z, p)]
        for j, hops in ((0, 2), (4, 1)):
            for i, d in enumerate(ways):
                dev = at(dz=hops * d + ZS)
                held[hops, i, p] = push(spot, spot, zs.at[phase, i, j + p], zr.at[phase, i, j + p], dev)

    def forward_z(buf, phase, held):
        for p in range(pieces):
            for i, d in enumerate(ways):
                held[2, i, p].wait_recv()
                spot = buf.at[chunk(lax.rem(z - 2 * d + ZS, ZS), p)]
                if p // (pieces // 2) == i:
                    q = 8 + p - i * (pieces // 2)
                    held[4, i, p] = push(spot, spot, zs.at[phase, i, q], zr.at[phase, i, q], at(dz=2 * d + ZS))
                held[3, i, p] = push(spot, spot, zs.at[phase, i, 10 + p], zr.at[phase, i, 10 + p], at(dz=d + ZS))
        for key, c in held.items():
            c.wait_send()
            if key[0] != 2:
                c.wait_recv()

    def make_gram(matrix, part):
        picked = [matrix[pl.ds(pl.multiple_of(j * n + x * 8, 8), 8), :] for j in range(ZS)]
        both = split2(jnp.concatenate(picked, axis=0))
        prod = lax.dot_general(both, split2(matrix[...]), NT, preferred_element_type=jnp.float32)
        m = 8 * ZS
        tile = prod[:m, :COMP] + (prod[:m, COMP:] + prod[m:, :COMP] + prod[m:, COMP:])
        part[...] = tile.reshape(part.shape)

    def send_gram(part, slots, sem):
        out = []
        for o in zorder:
            dev = at(dz=o)
            out.append(push(part.at[dev[1]], slots.at[o - 1], ds.at[sem, o - 1], dr.at[sem, o - 1], dev))
        return out

    def share_gram(sent, part, slots, tiles, step):
        finish(sent)
        spot = tiles.at[x]
        spot[...] = part[z] + sum(slots[i] for i in range(ZS - 1))
        return [push(spot, spot, xs.at[step, o - 1], xr.at[step, o - 1], at(dx=o)) for o in xorder]

    def whole_gram(sent, tiles):
        finish(sent)
        return tiles[...].reshape(n, COMP)

    def finish(copies):
        for c in copies:
            c.wait()

    loads = [
        pltpu.make_async_copy(src, dst, loaded.at[i])
        for i, (src, dst) in enumerate(((dic_in, dic), (acts_in, acts), (codes_in, codes)))
    ]
    for c in loads:
        c.start()
    loads[0].wait()
    dt[...] = dic[...].T
    make_gram(dt, gram)
    loads[1].wait()
    proj[...] = lax.dot_general(dt[...].astype(jnp.bfloat16), acts[...], NT, preferred_element_type=jnp.float32)
    pl.semaphore_wait(barrier, len(partners))
    sent_gram = send_gram(gram, gram_in, 0)
    held = scatter_z(proj, bufs, 0)
    loads[2].wait()
    ct[...] = codes[...].T
    own = rows(z, n)
    sent_gram = share_gram(sent_gram, gram, gram_in, gram_tiles, 9)
    relay_z(proj, bufs, 0, held)
    prod = gram_products(whole_gram(sent_gram, gram_tiles), ct[...])
    passed = {}
    for p in range(pieces):
        mid[chunk(z, p), :] = update(ct[chunk(z, p), :], summed_z(proj, bufs, held, p), prod, p)
        gather_z(mid, 1, passed, p)
    for c in held.values():
        c.wait_send()
    forward_z(mid, 1, passed)

    low = mid[...].astype(jnp.bfloat16)
    low_own = mid[own, :].astype(jnp.bfloat16)
    gk[...] = lax.dot_general(low_own, low, NT, preferred_element_type=jnp.float32).reshape(gk.shape)
    g_c = push(gk.at[1 - core], gk_c, cs.at[8], crs.at[8], at(dc=1))

    halftiles = acts.shape[1] // 256
    parts = part_list(halftiles)

    def cross(which, p):
        first, count, _ = parts[p]
        lanes = pl.ds(pl.multiple_of((which * halftiles + first) * 128, 128), count * 128)
        block = jnp.dot(low, acts[:, lanes], preferred_element_type=jnp.float32)
        for j in range(count):
            cr[which, pl.ds((first + j) * COMP, COMP), :] = block[:, j * 128 : j * 128 + 128]

    axes = {"x": (x, XS, xorder, xs, xr), "y": (y, YS, zorder, ys, yr)}

    def shares(p):
        first, count, order = parts[p]
        one, two = axes[order[0]], axes[order[1]]
        size = count * COMP
        return first * COMP, size, one, two, size // one[1], size // one[1] // two[1]

    def span_of(base, i, size):
        return pl.ds(pl.multiple_of(base + i * size, size), size)

    def along(name, row, src_of, dst_of):
        me, count, order, ss, rs = axes[name]
        out = []
        for o in order:
            dev = at(dx=o) if name == "x" else at(dy=o)
            out.append(push(src_of(lax.rem(me + o, count)), dst_of(o), ss.at[row, o - 1], rs.at[row, o - 1], dev))
        return out

    def send_core(p):
        base, size, _, _, _, _ = shares(p)
        span = pl.ds(base, size)
        return [push(cr.at[1 - core, span], cr_c.at[span], cs.at[p], crs.at[p], at(dc=1))]

    def send_first(p, copies):
        finish(copies)
        base, size, one, two, n1, n2 = shares(p)
        span = pl.ds(base, size)
        cr_c[span, :] += cr[core, span, :]
        return along(parts[p][2][0], 2 * p, lambda i: cr_c.at[span_of(base, i, n1)], lambda o: in1[p].at[o - 1])

    def send_second(p, copies):
        finish(copies)
        base, size, one, two, n1, n2 = shares(p)
        sum1[p][...] = cr_c[span_of(base, one[0], n1), :] + sum(in1[p][i] for i in range(one[1] - 1))
        return along(parts[p][2][1], 2 * p, lambda i: sum1[p].at[span_of(0, i, n2)], lambda o: in2[p].at[o - 1])

    def gather_second(p, copies):
        finish(copies)
        base, size, one, two, n1, n2 = shares(p)
        spot = full.at[core, span_of(base, one[0] * two[1] + two[0], n2)]
        spot[...] = sum1[p][span_of(0, two[0], n2), :] + sum(in2[p][i] for i in range(two[1] - 1))
        return along(parts[p][2][1], 2 * p + 1, lambda i: spot, lambda o: spot)

    def gather_first(p, copies):
        finish(copies)
        base, size, one, two, n1, n2 = shares(p)
        spot = full.at[core, span_of(base, one[0], n1)]
        return along(parts[p][2][0], 2 * p + 1, lambda i: spot, lambda o: spot)

    def gather_core(p, copies):
        finish(copies)
        base, size, _, _, _, _ = shares(p)
        spot = full.at[core, pl.ds(base, size)]
        return [push(spot, spot, cs.at[4 + p], crs.at[4 + p], at(dc=1))]

    c = [None] * 4
    for p in range(4):
        cross(1 - core, p)
        c[p] = send_core(p)
    g_c.wait()
    gk_x[x] = gk[core] + gk_c[...]
    g_x = along("x", 8, lambda i: gk_x.at[x], lambda o: gk_x.at[x])
    for p in range(4):
        cross(core, p)
    c[0] = send_first(0, c[0])
    c[1] = send_first(1, c[1])
    c[2] = send_first(2, c[2])
    finish(g_x)
    gk_y[y] = sum(gk_x[i] for i in range(XS))
    g_y = along("y", 8, lambda i: gk_y.at[y], lambda o: gk_y.at[y])
    c[3] = send_first(3, c[3])
    c[0] = send_second(0, c[0])
    c[1] = send_second(1, c[1])
    finish(g_y)
    spot = gk_z.at[z, core]
    spot[...] = sum(gk_y[i] for i in range(YS))
    g_z = [push(spot, spot, ds.at[2, o - 1], dr.at[2, o - 1], at(dz=o)) for o in zorder]
    c[2] = send_second(2, c[2])
    c[0] = gather_second(0, c[0])
    c[3] = send_second(3, c[3])
    c[1] = gather_second(1, c[1])
    c[2] = gather_second(2, c[2])
    c[3] = gather_second(3, c[3])
    finish(g_z)
    spot = gk_z.at[:, core]
    g_c = push(spot, spot, cs.at[9], crs.at[9], at(dc=1))
    c[0] = gather_first(0, c[0])
    g_c.wait()
    ginv[...] = gk_z[...].reshape(COMP, COMP)

    invert_blocks(ginv, 0, 2)
    c[1] = gather_first(1, c[1])
    c[3] = gather_first(3, c[3])
    invert_blocks(ginv, 2, 5)
    c[2] = gather_first(2, c[2])
    invert_blocks(ginv, 5, 7)
    c[0] = gather_core(0, c[0])
    invert_blocks(ginv, 7, 11)
    c[1] = gather_core(1, c[1])
    invert_blocks(ginv, 11, 14)
    c[3] = gather_core(3, c[3])
    c[2] = gather_core(2, c[2])
    invert_blocks(ginv, 14, 16)

    def solve(first, last):
        for j in range(first, last):
            span = pl.ds(j * COMP, COMP)
            block = jnp.concatenate([full[0, span, :], full[1, span, :]], axis=1)
            solved = jnp.dot(ginv[...], block, precision=HIGHEST, preferred_element_type=jnp.float32)
            for i in range(2):
                dt[:, (i * halftiles + j) * 128 : (i * halftiles + j + 1) * 128] = solved[:, i * 128 : i * 128 + 128]

    for p in (0, 1, 3, 2):
        finish(c[p])
        solve(parts[p][0], parts[p][0] + parts[p][1])
    make_gram(dt, gram2)
    sent_gram = send_gram(gram2, gram2_in, 1)
    proj2[...] = lax.dot_general(dt[...].astype(jnp.bfloat16), acts[...], NT, preferred_element_type=jnp.float32)
    held = scatter_z(proj2, bufs2, 2)
    dict_out[...] = dt[...].T
    sent_gram = share_gram(sent_gram, gram2, gram2_in, gram2_tiles, 10)
    relay_z(proj2, bufs2, 2, held)
    prod = gram_products(whole_gram(sent_gram, gram2_tiles), mid[...])
    passed = {}
    for p in range(pieces):
        out_t[chunk(z, p), :] = update(mid[chunk(z, p), :], summed_z(proj2, bufs2, held, p), prod, p)
        gather_z(out_t, 3, passed, p)
    for c in held.values():
        c.wait_send()
    forward_z(out_t, 3, passed)


def leave(out_t, dict_in, codes_out, dict_out, held, sem):
    parts = 4
    step = dict_in.shape[0] // parts
    spots = [pl.ds(i * step, step) for i in range(parts)]
    copies = [pltpu.make_async_copy(dict_in.at[p], dict_out.at[p], sem.at[i]) for i, p in enumerate(spots)]
    for c in copies:
        c.start()
    held[...] = out_t[...].T
    copies.append(pltpu.make_async_copy(held, codes_out, sem.at[parts]))
    copies[-1].start()
    for c in copies:
        c.wait()


def per_device(acts, dictionary, codes):
    tokens, hid = acts.shape
    f32 = jnp.float32
    v = lambda *s: pltpu.VMEM(s, f32)
    n = COMP // ZS
    half = hid * COMP // 2 // 128
    count = {"x": XS, "y": YS}
    shapes = [(k * COMP, count[order[0]], count[order[1]]) for _, k, order in part_list(hid // 256)]
    sums = (v(2, n, tokens), v(2, n // 2, tokens), v(2, n, tokens), v(2, n, tokens), v(2, n, tokens))
    vmem = pl.BlockSpec(memory_space=pltpu.VMEM)
    anywhere = pl.BlockSpec(memory_space=pl.ANY)
    dma = pltpu.SemaphoreType.DMA
    out_t, dict_new = pl.pallas_call(
        kernel,
        name="semi_nmf",
        out_shape=(pltpu.VMEM((COMP, tokens), f32), pltpu.VMEM((hid, COMP), f32)),
        in_specs=[anywhere] * 3,
        out_specs=(vmem, vmem),
        scratch_shapes=[
            pltpu.VMEM((tokens, hid), jnp.bfloat16), v(hid, COMP), v(tokens, COMP), dma((3,)),
            v(COMP, hid), v(COMP, tokens), v(COMP, tokens), v(ZS, 8, COMP),
            v(ZS - 1, 8, COMP), v(XS, 8, COMP), v(COMP, tokens),
            v(2, n // 2, COMP), v(n // 2, COMP), v(XS, n // 2, COMP), v(YS, n // 2, COMP), v(ZS, 2, n // 2, COMP),
            v(COMP, COMP),
            v(2, half, 128), v(half, 128), v(2, half, 128),
            *[v(one - 1, size // one, 128) for size, one, two in shapes],
            *[v(size // one, 128) for size, one, two in shapes],
            *[v(two - 1, size // one // two, 128) for size, one, two in shapes],
            v(COMP, tokens), v(ZS, 8, COMP), v(ZS - 1, 8, COMP), v(XS, 8, COMP),
            *sums, *sums,
            dma((4, 2, 14)), dma((4, 2, 14)), dma((3, ZS - 1)), dma((3, ZS - 1)), dma((9, YS - 1)), dma((9, YS - 1)),
            dma((11, XS - 1)), dma((11, XS - 1)), dma((12,)), dma((12,)),
        ],
        compiler_params=pltpu.CompilerParams(
            collective_id=0, has_side_effects=True, vmem_limit_bytes=56 * 1024 * 1024
        ),
    )(acts, dictionary, codes)
    return pl.pallas_call(
        leave,
        name="leave",
        out_shape=(jax.ShapeDtypeStruct((tokens, COMP), f32), jax.ShapeDtypeStruct((hid, COMP), f32)),
        in_specs=[vmem] * 2,
        out_specs=(anywhere, anywhere),
        scratch_shapes=[v(tokens, COMP), dma((5,))],
        compiler_params=pltpu.CompilerParams(vmem_limit_bytes=16 * 1024 * 1024),
    )(out_t, dict_new)


def solution(mesh):
    return jax.shard_map(
        per_device,
        mesh=mesh,
        in_specs=(P("tok", "hid"), P("hid", None), P("tok", None)),
        out_specs=(P("tok", None), P("hid", None)),
        check_vma=False,
    )
```
